256 devices in a mesh: pos: 32 (over y, z), strand: 2 (over x_lo), rep: 4 (over x_hi, core).
Axes of the slice: x: 4 (x_hi: 2, x_lo: 2; x = x_hi * 2 + x_lo), y: 4, z: 8, core: 2. Of those that a mesh axis runs over, the one named last changes fastest.
Arguments:
- tokens: int32 [4, 8192], P('rep', 'pos'), may hold values from 0 to 3
- embed: bfloat16 [4, 1536], replicated, may hold values from -24 to 24
- first_kernel: float32 [3, 1536], replicated, may hold values from -2.5 to 2.5
- first_gain: float32 [1536], replicated, may hold values from 0.1 to 1.9
- first_weight: bfloat16 [1536, 1536], P('pos'), may hold values from -0.15625 to 0.15625
- second_kernel: float32 [3, 1536], replicated, may hold values from -2.5 to 2.5
- second_gain: float32 [1536], replicated, may hold values from 0.1 to 1.9
- second_weight: bfloat16 [1536, 1536], P('pos'), may hold values from -0.15625 to 0.15625
- cotangent: bfloat16 [4, 2, 8192, 1536], P('rep', 'strand', 'pos'), may hold values from -6 to 6
Outputs:
- both_strands: bfloat16 [4, 2, 8192, 1536], P('rep', 'strand', 'pos')
- grad_weight_a: float32 [1536, 1536], P('pos')
- grad_weight_b: float32 [1536, 1536], P('pos')
- grad_taps_a: float32 [3, 1536], replicated
- grad_taps_b: float32 [3, 1536], replicated
- grad_gain_a: float32 [1536], replicated
- grad_gain_b: float32 [1536], replicated
The draws below stay inside these ranges and needn't reach their ends.
All inputs are finite; a program needn't handle non-finite values.
Results may differ from the reference program's by a relative error of at most 0.0067.
Values may be sent and summed in bfloat16 or wider, within the bound.
A program may use at most 128 MiB of HBM per device.

```python
import math
import jax
import jax.numpy as jnp
from jax import lax

C = 1536
FIRST_DILATE = 32
SECOND_DILATE = 64
POSITIONS = 8192
WINDOWS = 4


def draw_embed(key, part):
    key = jax.random.fold_in(key, 11)
    key_chan, key_rows, key_base = jax.random.split(key, 3)
    row_scale = jnp.exp(jax.random.uniform(key_rows, (4, 1), jnp.float32, 0.0, math.log(2.0)))
    chan_scale = jnp.exp(jax.random.uniform(key_chan, (1, C), jnp.float32, math.log(0.3), math.log(3.0)))
    base = jnp.clip(jax.random.normal(key_base, (4, C), jnp.float32), -4.0, 4.0)
    return (base * chan_scale * row_scale).astype(jnp.bfloat16)


def plant(drawn, rng, low, largest):
    longest = drawn.shape.index(max(drawn.shape))
    spots = []
    for shift in (0, 1):
        where = [jax.random.randint(jax.random.fold_in(rng, axis), (), 0, length) for axis, length in enumerate(drawn.shape)]
        where[longest] = (where[longest] + shift) % drawn.shape[longest]
        spots.append(tuple(where))
    return drawn.at[spots[0]].set(low).at[spots[1]].set(largest)


def levels(rng, dims, cuts, least, top_value):
    def one(dim, shards_of):
        heights = jax.random.uniform(jax.random.fold_in(jax.random.fold_in(rng, 6), dim), (shards_of,), jnp.float32, least / len(cuts), top_value / len(cuts))
        return jnp.repeat(jnp.exp(heights), dims[dim] // shards_of).reshape((-1,) + (1,) * (len(dims) - dim - 1))

    factor_of = one(*cuts[0])
    for cut in cuts[1:]:
        factor_of = factor_of * one(*cut)
    return factor_of


def normal_values(stream_key, extent, scale, most, cuts=(), dtype=jnp.bfloat16):
    entries = scale * jax.random.normal(stream_key, extent, jnp.float32)
    if cuts:
        entries = entries * levels(stream_key, extent, cuts, -0.22, 0.18)
    return jnp.clip(entries, -most, most).astype(dtype)


def setup_inputs(seed: int = 0) -> dict:
    keys = jax.random.split(jax.random.key(seed), 10)
    return {
        "tokens": plant(jax.random.randint(keys[0], (WINDOWS, POSITIONS), 0, 4), jax.random.fold_in(keys[0], 1), 0, 3).astype(jnp.int32),
        "embed": draw_embed(jax.random.fold_in(keys[9], 71), 0),
        "first_kernel": normal_values(keys[2], (3, C), 0.6, 2.5, (), jnp.float32),
        "first_gain": jnp.clip(1.0 + 0.18 * jax.random.normal(keys[3], (C,), jnp.float32), 0.1, 1.9),
        "first_weight": normal_values(keys[4], (C, C), C ** -0.5, 0.15625, ((0, 32),)),
        "second_kernel": normal_values(keys[5], (3, C), 0.6, 2.5, (), jnp.float32),
        "second_gain": jnp.clip(1.0 + 0.18 * jax.random.normal(keys[6], (C,), jnp.float32), 0.1, 1.9),
        "second_weight": normal_values(keys[7], (C, C), C ** -0.5, 0.15625, ((0, 32),)),
        "cotangent": normal_values(keys[8], (WINDOWS, 2, POSITIONS, C), 1.0, 6.0, ((0, 4), (1, 2), (2, 32))),
    }


epsilon = 1e-05

def gelu_slope(pre_act, incoming_gradient):
    _, pullback = jax.vjp(jax.nn.gelu, pre_act)
    return pullback(incoming_gradient)[0]

def conv_block_forward_pass(padded, inputs, kernel, scales, matrix, reach):
    sequence_length = inputs.shape[0]
    wide = padded.astype(jnp.float32)
    kernel = kernel.astype(jnp.float32)
    conv_out = kernel[0] * wide[0:sequence_length] + kernel[1] * wide[reach:reach + sequence_length] + kernel[2] * wide[2 * reach:2 * reach + sequence_length]
    inv_rms = lax.rsqrt(lax.optimization_barrier(jnp.mean(conv_out * conv_out, axis=-1, keepdims=True)) + epsilon)
    normed = (conv_out * inv_rms * scales.astype(jnp.float32)).astype(jnp.bfloat16)
    pre_act = jnp.dot(normed, matrix, preferred_element_type=jnp.float32)
    result = (inputs.astype(jnp.float32) + jax.nn.gelu(pre_act)).astype(jnp.bfloat16)
    return (result, (wide, conv_out, inv_rms, normed, pre_act))

def conv_block_reverse_pass(incoming_gradient, saved, kernel, scales, matrix, reach):
    wide, conv_out, inv_rms, normed, pre_act = saved
    sequence_length = conv_out.shape[0]
    slopes = gelu_slope(pre_act, incoming_gradient).astype(jnp.bfloat16)
    dnormed = lax.dot_general(slopes, matrix, (((1,), (1,)), ((), ())), preferred_element_type=jnp.float32)
    scaled = dnormed * scales.astype(jnp.float32)
    dconv = inv_rms * scaled - conv_out * (inv_rms * inv_rms * inv_rms) * lax.optimization_barrier(jnp.mean(scaled * conv_out, axis=-1, keepdims=True))
    gain_grad = lax.optimization_barrier(jnp.sum(dnormed * conv_out * inv_rms, axis=0))
    tap_grad = jnp.stack([lax.optimization_barrier(jnp.sum(dconv * wide[k * reach:k * reach + sequence_length], axis=0)) for k in range(3)])
    return (slopes, dconv, gain_grad, tap_grad)

def border_exchange_reverse(dconv, kernel, reach):
    kernel = kernel.astype(jnp.float32)
    first = jnp.pad(kernel[0] * dconv, ((0, 2 * reach), (0, 0)))
    center_rows = jnp.pad(kernel[1] * dconv, ((reach, reach), (0, 0)))
    last = jnp.pad(kernel[2] * dconv, ((2 * reach, 0), (0, 0)))
    return first + center_rows + last

def weight_term(normed, slopes):
    return lax.dot_general(normed, slopes, (((0,), (0,)), ((), ())), preferred_element_type=jnp.float32)

def reference(tokens, embed, first_kernel, first_gain, first_weight, second_kernel, second_gain, second_weight, cotangent):
    width = embed.shape[1]
    grad_weight_a = jnp.zeros((width, width), jnp.float32)
    grad_weight_b = jnp.zeros((width, width), jnp.float32)
    grad_taps_a = jnp.zeros((3, width), jnp.float32)
    grad_taps_b = jnp.zeros((3, width), jnp.float32)
    grad_gain_a = jnp.zeros((width,), jnp.float32)
    grad_gain_b = jnp.zeros((width,), jnp.float32)
    outputs = []
    for window in range(tokens.shape[0]):
        sequences = [tokens[window], 3 - tokens[window][::-1]]
        finals = []
        kept = []
        for bases in sequences:
            begin_index = embed[bases]
            center_rows, first_retained = conv_block_forward_pass(jnp.pad(begin_index, ((FIRST_DILATE, FIRST_DILATE), (0, 0))), begin_index, first_kernel, first_gain, first_weight, FIRST_DILATE)
            closing_output, second_retained = conv_block_forward_pass(jnp.pad(center_rows, ((SECOND_DILATE, SECOND_DILATE), (0, 0))), center_rows, second_kernel, second_gain, second_weight, SECOND_DILATE)
            finals.append(closing_output)
            kept.append((first_retained, second_retained))
        both = []
        for strand in range(2):
            mixed = 0.5 * (finals[strand].astype(jnp.float32) + finals[1 - strand][::-1, ::-1].astype(jnp.float32))
            both.append(mixed.astype(jnp.bfloat16))
        outputs.append(jnp.stack(both))
        for strand in range(2):
            incoming_gradient = 0.5 * (cotangent[window, strand].astype(jnp.float32) + cotangent[window, 1 - strand][::-1, ::-1].astype(jnp.float32))
            first_retained, second_retained = kept[strand]
            sequence_length = incoming_gradient.shape[0]
            second_activation_slopes, second_dilated_conv, second_gain_share, second_kernel_share = conv_block_reverse_pass(incoming_gradient, second_retained, second_kernel, second_gain, second_weight, SECOND_DILATE)
            grad_weight_b = grad_weight_b + weight_term(second_retained[3], second_activation_slopes)
            grad_gain_b = grad_gain_b + second_gain_share
            grad_taps_b = grad_taps_b + second_kernel_share
            first_incoming_gradient = incoming_gradient + border_exchange_reverse(second_dilated_conv, second_kernel, SECOND_DILATE)[SECOND_DILATE:SECOND_DILATE + sequence_length]
            first_activation_slopes, first_dilated_conv, first_gain_share, first_kernel_share = conv_block_reverse_pass(first_incoming_gradient, first_retained, first_kernel, first_gain, first_weight, FIRST_DILATE)
            grad_weight_a = grad_weight_a + weight_term(first_retained[3], first_activation_slopes)
            grad_gain_a = grad_gain_a + first_gain_share
            grad_taps_a = grad_taps_a + first_kernel_share
    return (jnp.stack(outputs), grad_weight_a, grad_weight_b, grad_taps_a, grad_taps_b, grad_gain_a, grad_gain_b)
```

```python
import functools

import jax
import jax.numpy as jnp
from jax import lax
from jax.experimental import pallas as pl
from jax.experimental.pallas import tpu as pltpu
from jax.sharding import PartitionSpec as P

MESH = pl.DeviceIdType.MESH
HIGH = lax.Precision.HIGHEST
F32 = jnp.float32
BF16 = jnp.bfloat16
C = 1536
L = 256
FIRST_DILATE = 32
SECOND_DILATE = 64
EPS = 1e-05
CODES = 96
PAD = 128
ROWS = 256
WIDE = 2560
OWN = 48
GELU_A = 0.7978845608028654
GELU_B = 0.044715


def coords():
    pos = lax.axis_index("pos")
    strand = lax.axis_index("strand")
    rep = lax.axis_index("rep")
    return pos // 8, pos % 8, (rep // 2) * 2 + strand, rep % 2


def device(y, z, x, c):
    return {"pos": y * 8 + z, "strand": x % 2, "rep": (x // 2) * 2 + c}


def along_y(d):
    y, z, x, c = coords()
    return device((y + d) % 4, z, x, c)


def along_z(d):
    y, z, x, c = coords()
    return device(y, (z + d) % 8, x, c)


def along_half_z(d):
    y, z, x, c = coords()
    return device(y, (z // 4) * 4 + (z + d) % 4, x, c)


def along_x(d):
    y, z, x, c = coords()
    return device(y, z, (x + d) % 4, c)


def other_core():
    y, z, x, c = coords()
    return device(y, z, x, 1 - c)


def axis_peers():
    return (
        [along_z(d) for d in range(1, 8)]
        + [along_y(d) for d in range(1, 4)]
        + [along_x(d) for d in range(1, 4)]
        + [other_core()]
    )


class Sender:
    def __init__(self, send, recv):
        self.send, self.recv, self.used = send, recv, 0

    def start(self, src, dst, to):
        copy = pltpu.make_async_remote_copy(
            src_ref=src,
            dst_ref=dst,
            send_sem=self.send.at[self.used],
            recv_sem=self.recv.at[self.used],
            device_id=to,
            device_id_type=MESH,
        )
        self.used += 1
        copy.start()
        return copy


def finish(copies):
    for copy in copies:
        copy.wait()


def lanes(index, width):
    return pl.ds(pl.multiple_of(index * width, 128), width)


def rows(index, height):
    return pl.ds(pl.multiple_of(index * height, 8), height)


def dot(a, b, precision=None):
    return lax.dot_general(
        a, b, (((1,), (0,)), ((), ())), preferred_element_type=F32, precision=precision
    )


def dot_nt(a, b):
    return lax.dot_general(a, b, (((1,), (1,)), ((), ())), preferred_element_type=F32)


def split(value):
    high = value.astype(BF16)
    return high, (value - high.astype(F32)).astype(BF16)


def gelu_parts(pre):
    square = pre * pre
    th = jnp.tanh(GELU_A * pre * (1.0 + GELU_B * square))
    half = 0.5 * (1.0 + th)
    slope = half + 0.5 * pre * (1.0 - th * th) * (GELU_A * (1.0 + 3.0 * GELU_B * square))
    return pre * half, slope


def code_bases(code):
    inner, left = code < 64, code < 80
    one = jnp.where(inner, code // 16, jnp.where(left, -1, (code - 80) // 4))
    two = jnp.where(inner, (code // 4) % 4, jnp.where(left, (code - 64) // 4, code % 4))
    three = jnp.where(inner | left, code % 4, -1)
    return one, two, three


def code_onehot(code, column):
    one, two, three = code_bases(code)
    hit = (column == one) & (one >= 0)
    hit = hit | (column == 4 + two) | ((column == 8 + three) & (three >= 0))
    return jnp.where(hit & (code < CODES), 1.0, 0.0)


def iota(shape, axis):
    return lax.broadcasted_iota(jnp.int32, shape, axis)


def tap_rows(taps, table):
    return jnp.concatenate(
        [taps[0] * table[0:80], taps[1] * table[0:96], taps[2] * table[0:64], taps[2] * table[80:96]],
        axis=0,
    )


def tables_kernel(
    tok_ref,
    emb_ref,
    k1_ref,
    g1_ref,
    w1_ref,
    k2_ref,
    g2_ref,
    w2_ref,
    ext_ref,
    m_ref,
    p_ref,
    own_ref,
    tsend,
    trecv,
    qpart,
    qy,
    qz,
    qfull,
    wpad1,
    wpad2,
    aown,
    ppart,
    py,
    psum,
    pz,
    pmid,
    pbuf,
    tsem,
    send,
    recv,
):
    y, z, x, c = coords()
    pos = lax.axis_index("pos")
    strand = lax.axis_index("strand")
    rep = lax.axis_index("rep")
    frame = jnp.where(strand == 1, 31 - pos, pos)
    targets = [(frame + d + 32) % 32 for d in (-1, 0, 1)]

    barrier = pltpu.get_barrier_semaphore()
    peers = axis_peers()
    for peer in peers:
        pl.semaphore_signal(barrier, inc=1, device_id=peer, device_id_type=MESH)
    count = len(peers)
    for t in targets:
        @pl.when(t != pos)
        def _():
            pl.semaphore_signal(
                barrier,
                inc=1,
                device_id={"pos": t, "strand": strand, "rep": rep},
                device_id_type=MESH,
            )
        count = count + jnp.where(t != pos, 1, 0)

    tokens = jnp.broadcast_to(tok_ref[...], (8, L)).astype(F32)
    flip = jnp.where(iota((L, L), 0) + iota((L, L), 1) == L - 1, 1.0, 0.0)
    turned = 3.0 - dot(tokens, flip)
    tsend[...] = jnp.where(strand == 1, turned, tokens).astype(jnp.int32)
    wpad1[...] = jnp.zeros_like(wpad1)
    wpad2[...] = jnp.zeros_like(wpad2)
    wpad1[0:OWN] = w1_ref[...]
    wpad2[0:OWN] = w2_ref[...]
    emb = emb_ref[...].astype(F32)
    k1, k2 = k1_ref[...], k2_ref[...]
    g1, g2 = g1_ref[...], g2_ref[...]
    pick = jnp.where(
        (iota((C, PAD), 0) == pos * OWN + iota((C, PAD), 1)) & (iota((C, PAD), 1) < OWN), 1.0, 0.0
    )
    packed = jnp.concatenate([emb, k1, g1, k2, g2, jnp.zeros((4, C), F32)], axis=0)
    vec = dot(packed, pick, HIGH)
    e_own = vec[0:4]
    te_own = jnp.concatenate([vec[4 + k : 5 + k] * e_own for k in range(3)], axis=0)
    high, low = split(
        jnp.concatenate([vec[7:8] * te_own, jnp.zeros((4, PAD), F32)], axis=0)
    )
    part = dot(jnp.concatenate([high, low], axis=0), wpad1[...])
    part = part[0:16] + part[16:32]
    qpart[0] = part[0:8]
    qpart[1] = part[8:16]

    pl.semaphore_wait(barrier, count)

    net = Sender(send, recv)
    for j, t in enumerate(targets):
        slot = trecv.at[2 - j]

        @pl.when(t != pos)
        def _():
            pltpu.make_async_remote_copy(
                src_ref=tsend,
                dst_ref=slot,
                send_sem=tsem.at[0, j],
                recv_sem=tsem.at[1, j],
                device_id={"pos": t, "strand": strand, "rep": rep},
                device_id_type=MESH,
            ).start()

        @pl.when(t == pos)
        def _():
            trecv[2 - j] = tsend[...]

    mine = lanes(x, 384)
    piece = qpart.at[c, :, mine]
    copies = [net.start(piece, qy.at[y], along_y(d)) for d in range(1, 4)]
    qy[y] = qpart[c, :, mine]

    te = jnp.concatenate([k1[k : k + 1] * emb for k in range(3)] + [jnp.zeros((4, C), F32)], axis=0)
    hot = code_onehot(iota((PAD, 16), 0), iota((PAD, 16), 1))
    conv = dot(hot, te, HIGH)
    inv = lax.rsqrt(jnp.mean(conv * conv, axis=-1, keepdims=True) + EPS)
    pads = jnp.zeros((4, C), F32)
    center = dot(hot, jnp.concatenate([pads, emb, pads, pads], axis=0))
    finish(copies)

    qz[z] = qy[0] + qy[1] + qy[2] + qy[3]
    copies = [net.start(qz.at[z], qz.at[z], along_z(d)) for d in range(1, 8)]
    finish(copies)
    total = qz[0]
    for i in range(1, 8):
        total = total + qz[i]
    qfull[c, :, mine] = total
    copies = [
        net.start(qfull.at[c, :, mine], qfull.at[c, :, mine], along_x(d)) for d in range(1, 4)
    ]
    finish(copies)
    copies = [net.start(qfull.at[c], qfull.at[c], other_core())]
    finish(copies)

    q = jnp.concatenate([qfull[0], qfull[1]], axis=0)
    pre = inv * dot(hot, q, HIGH)
    act, _ = gelu_parts(pre)
    table = jnp.where(iota((PAD, C), 0) < CODES, center + act, 0.0).astype(BF16)
    m_ref[...] = table
    m_own = dot(table, pick.astype(BF16))
    own_ref[0] = dot(pre, pick, HIGH)
    own_ref[1] = jnp.broadcast_to(inv, (PAD, PAD))
    own_ref[2] = m_own
    own_ref[3] = jnp.concatenate([vec, jnp.zeros((PAD - 16, PAD), F32)], axis=0)

    taps = [vec[8 + k : 9 + k] for k in range(3)]
    aown[...] = vec[11:12] * tap_rows(taps, m_own)
    high, low = split(aown[rows(c, 128)])
    w2 = wpad2[:, mine]
    ppart[...] = dot(high, w2) + dot(low, w2)
    copies = [
        net.start(ppart.at[rows((y + d) % 4, 32)], py.at[y], along_y(d)) for d in range(1, 4)
    ]
    py[y] = ppart[rows(y, 32)]
    finish(copies)
    psum[...] = py[0] + py[1] + py[2] + py[3]
    copies = [
        net.start(psum.at[rows((z + d) % 4, 8)], pz.at[z], along_z(d)) for d in range(1, 8)
    ]
    pz[z] = psum[rows(z % 4, 8)]
    finish(copies)
    total = pz[0]
    for i in range(1, 8):
        total = total + pz[i]
    pmid[z % 4] = total
    copies = [
        net.start(pmid.at[z % 4], pmid.at[z % 4], along_half_z(d)) for d in range(1, 4)
    ]
    finish(copies)
    half = rows(c, 128)
    quarter = pl.ds(pl.multiple_of(c * 128 + y * 32, 32), 32)
    pbuf[quarter, mine] = jnp.concatenate([pmid[i] for i in range(4)], axis=0).astype(BF16)
    block = pbuf.at[quarter, mine]
    finish([net.start(block, block, along_y(d)) for d in range(1, 4)])
    block = pbuf.at[half, mine]
    finish([net.start(block, block, along_x(d)) for d in range(1, 4)])
    block = pbuf.at[half]
    finish([net.start(block, block, other_core())])
    p_ref[...] = pbuf[...]

    for j, t in enumerate(targets):
        @pl.when(t != pos)
        def _():
            pltpu.make_async_remote_copy(
                src_ref=tsend,
                dst_ref=trecv.at[2 - j],
                send_sem=tsem.at[0, j],
                recv_sem=tsem.at[1, j],
                device_id={"pos": t, "strand": strand, "rep": rep},
                device_id_type=MESH,
            ).wait()
    joined = jnp.concatenate([trecv[0], trecv[1], trecv[2]], axis=1)
    place = (pos - 1) * L + iota((8, 3 * L), 1)
    ext_ref[...] = jnp.where((place >= 0) & (place < 32 * L), joined, 4)


def tables(tokens, embed, k1, g1, w1, k2, g2, w2):
    vmem = pl.BlockSpec(memory_space=pltpu.VMEM)
    return pl.pallas_call(
        tables_kernel,
        out_shape=(
            jax.ShapeDtypeStruct((8, 3 * L), jnp.int32),
            jax.ShapeDtypeStruct((PAD, C), BF16),
            jax.ShapeDtypeStruct((ROWS, C), BF16),
            jax.ShapeDtypeStruct((4, PAD, PAD), F32),
        ),
        in_specs=[vmem] * 8,
        out_specs=(vmem,) * 4,
        scratch_shapes=[
            pltpu.VMEM((8, L), jnp.int32),
            pltpu.VMEM((3, 8, L), jnp.int32),
            pltpu.VMEM((2, 8, C), F32),
            pltpu.VMEM((4, 8, 384), F32),
            pltpu.VMEM((8, 8, 384), F32),
            pltpu.VMEM((2, 8, C), F32),
            pltpu.VMEM((PAD, C), BF16),
            pltpu.VMEM((PAD, C), BF16),
            pltpu.VMEM((ROWS, PAD), F32),
            pltpu.VMEM((128, 384), F32),
            pltpu.VMEM((4, 32, 384), F32),
            pltpu.VMEM((32, 384), F32),
            pltpu.VMEM((8, 8, 384), F32),
            pltpu.VMEM((4, 8, 384), F32),
            pltpu.VMEM((ROWS, C), BF16),
            pltpu.SemaphoreType.DMA((2, 3)),
            pltpu.SemaphoreType.DMA((40,)),
            pltpu.SemaphoreType.DMA((40,)),
        ],
        compiler_params=pltpu.CompilerParams(
            collective_id=0, has_side_effects=True, vmem_limit_bytes=40 * 2**20
        ),
        name="tables",
    )(tokens, embed, k1, g1, w1, k2, g2, w2)


BLOCK = 256
BLOCKS = C // BLOCK


def code_of(left, middle, right):
    code = jnp.where(
        left == 4,
        64 + 4 * middle + right,
        jnp.where(right == 4, 80 + 4 * left + middle, 16 * left + 4 * middle + right),
    )
    return jnp.where(middle == 4, -1, code)


def tap_index(codes):
    first, second, third = codes
    second = jnp.where(second < 0, -1, 80 + second)
    third = jnp.where(third < 0, -1, jnp.where(third < 64, 176 + third, 160 + third))
    return first, second, third


def rows_kernel(
    ext_ref,
    m_ref,
    p_ref,
    k2_ref,
    cot_ref,
    out_ref,
    x_ref,
    hot,
    hot_t,
    wide_a,
    wide_b,
    mid_t,
    cots,
    mids,
    fins,
    preu,
    slope,
    acc,
    acc2,
):
    ext = ext_ref[...]
    left = pltpu.roll(ext, FIRST_DILATE, 1)
    right = pltpu.roll(ext, 3 * L - FIRST_DILATE, 1)

    def other(base):
        return jnp.where(base == 4, 4, 3 - base)

    start = L - SECOND_DILATE
    code_a = pltpu.roll(code_of(left, ext, right), 3 * L - start, 1)[:, 0:384]
    code_b = pltpu.roll(code_of(other(right), other(ext), other(left)), 3 * L - start, 1)[:, 0:384]

    def shifts(code):
        return [code[:, 0:L]] + [
            pltpu.roll(code, 384 - s, 1)[:, 0:L] for s in (SECOND_DILATE, 2 * SECOND_DILATE)
        ]

    three_a = shifts(code_a)
    three_b = shifts(code_b)[::-1]
    index = [jnp.concatenate([a, b], axis=1) for a, b in zip(tap_index(three_a), tap_index(three_b))]
    line = iota((ROWS, 2 * L), 0)
    hit = (line == index[0][0:1]) | (line == index[1][0:1]) | (line == index[2][0:1])
    hot_t[...] = jnp.where(hit, 1.0, 0.0).astype(BF16)
    mid_t[...] = jnp.where(
        iota((PAD, 2 * L), 0) == jnp.concatenate([three_a[1], three_b[1]], axis=1)[0:1], 1.0, 0.0
    ).astype(BF16)

    def column(row):
        return jnp.transpose(row.astype(F32))[:, 0:1].astype(jnp.int32)

    columns = [column(row) for row in index]
    line = iota((2 * L, ROWS), 1)
    hit = (line == columns[0]) | (line == columns[1]) | (line == columns[2])
    hot[...] = jnp.where(hit, 1.0, 0.0).astype(BF16)
    line = iota((384, PAD), 1)
    wide_a[...] = jnp.where(line == column(code_a), 1.0, 0.0).astype(BF16)
    wide_b[...] = jnp.where(line == column(code_b), 1.0, 0.0).astype(BF16)

    mirror = jnp.where(
        iota((BLOCK, BLOCK), 0) + iota((BLOCK, BLOCK), 1) == BLOCK - 1, 1.0, 0.0
    ).astype(BF16)

    acc[...] = jnp.zeros_like(acc)
    acc2[...] = jnp.zeros_like(acc2)

    def first_pass(b, carry):
        here = lanes(b, BLOCK)
        there = lanes(BLOCKS - 1 - b, BLOCK)
        cots[0:L, here] = cot_ref[:, here]
        cots[L : 2 * L, here] = dot(cot_ref[:, there], mirror).astype(BF16)
        m = m_ref[:, here]
        taps = k2_ref[:, here]
        for n, (wide, order) in enumerate(((wide_a, (0, 1, 2)), (wide_b, (2, 1, 0)))):
            mid = dot(wide[...], m)
            conv = (
                taps[order[0] : order[0] + 1] * mid[0:L]
                + taps[order[1] : order[1] + 1] * mid[64 : 64 + L]
                + taps[order[2] : order[2] + 1] * mid[128 : 128 + L]
            )
            square = conv * conv
            acc[n * L : n * L + L] += square[:, 0:128] + square[:, 128:256]
            mids[n * L : n * L + L, here] = mid[64 : 64 + L].astype(BF16)
        return carry

    lax.fori_loop(0, BLOCKS, first_pass, 0)
    acc[...] = jnp.broadcast_to(
        lax.rsqrt(jnp.sum(acc[...], axis=1, keepdims=True) * (1.0 / C) + EPS), (2 * L, 128)
    )

    def second_pass(b, carry):
        here = lanes(b, BLOCK)
        preu[...] = dot(hot[...], p_ref[:, here])

        def chunk(r, carry):
            some = rows(r, 64)
            inv = acc[some][:, 0:1]
            pre = inv * preu[some]
            act, grad = gelu_parts(pre)
            fins[some, here] = (mids[some, here].astype(F32) + act).astype(BF16)
            sl = cots[some, here].astype(F32) * grad
            prod = sl * pre
            acc2[some] += prod[:, 0:128] + prod[:, 128:256]
            slope[some] = (inv * sl).astype(BF16)
            return carry

        lax.fori_loop(0, 8, chunk, 0)
        x_ref[:, here] = 0.5 * dot(hot_t[...], slope[...])
        return carry

    lax.fori_loop(0, BLOCKS, second_pass, 0)

    def third_pass(b, carry):
        here = lanes(b, BLOCK)
        there = lanes(BLOCKS - 1 - b, BLOCK)
        far = dot(fins[L : 2 * L, there], mirror)
        out_ref[:, here] = (0.5 * (fins[0:L, here].astype(F32) + far)).astype(BF16)
        return carry

    lax.fori_loop(0, BLOCKS, third_pass, 0)

    inv = acc[:, 0:1]
    weight = (0.5 / C) * inv * inv * jnp.sum(acc2[...], axis=1, keepdims=True)
    high, low = split(weight * hot[...].astype(F32))
    x_ref[:, C : C + ROWS] = dot(hot_t[...], high) + dot(hot_t[...], low)
    x_ref[192:256, C + ROWS : WIDE] = jnp.zeros((64, WIDE - C - ROWS), F32)
    for n in range(2):
        v = 0.5 * dot(mid_t[...], cots[:, 768 * n : 768 * n + 768])
        x_ref[CODES * n : CODES * n + CODES, C + ROWS : WIDE] = v[0:CODES]


def row_work(ext, m, p, k2, cot):
    vmem = pl.BlockSpec(memory_space=pltpu.VMEM)
    return pl.pallas_call(
        rows_kernel,
        out_shape=(
            jax.ShapeDtypeStruct((L, C), BF16),
            jax.ShapeDtypeStruct((ROWS, WIDE), F32),
        ),
        in_specs=[vmem] * 5,
        out_specs=(vmem,) * 2,
        scratch_shapes=[
            pltpu.VMEM((2 * L, ROWS), BF16),
            pltpu.VMEM((ROWS, 2 * L), BF16),
            pltpu.VMEM((384, PAD), BF16),
            pltpu.VMEM((384, PAD), BF16),
            pltpu.VMEM((PAD, 2 * L), BF16),
            pltpu.VMEM((2 * L, C), BF16),
            pltpu.VMEM((2 * L, C), BF16),
            pltpu.VMEM((2 * L, C), BF16),
            pltpu.VMEM((2 * L, BLOCK), F32),
            pltpu.VMEM((2 * L, BLOCK), BF16),
            pltpu.VMEM((2 * L, 128), F32),
            pltpu.VMEM((2 * L, 128), F32),
        ],
        compiler_params=pltpu.CompilerParams(vmem_limit_bytes=40 * 2**20),
        name="rows",
    )(ext, m, p, k2, cot)


QUART = WIDE // 4


def tail_kernel(
    x_ref,
    own_ref,
    w1_ref,
    w2_ref,
    gwa_ref,
    gwb_ref,
    vec_ref,
    from_core,
    half_sum,
    half_low,
    xin,
    xsum,
    yin,
    ysum,
    zin,
    zmid,
    full,
    wpad1,
    wpad2,
    pack,
    packs,
    fbuf,
    pack2,
    packs2,
    send,
    recv,
):
    y, z, x, c = coords()
    pos = lax.axis_index("pos")
    barrier = pltpu.get_barrier_semaphore()
    peers = axis_peers()
    for peer in peers:
        pl.semaphore_signal(barrier, inc=1, device_id=peer, device_id_type=MESH)
    wpad1[...] = jnp.zeros_like(wpad1)
    wpad2[...] = jnp.zeros_like(wpad2)
    wpad1[0:OWN] = w1_ref[...]
    wpad2[0:OWN] = w2_ref[...]
    pl.semaphore_wait(barrier, len(peers))

    net = Sender(send, recv)
    half = rows(c, 128)
    finish([net.start(x_ref.at[rows(1 - c, 128)], from_core, other_core())])
    half_sum[...] = x_ref[half] + from_core[...]
    half_low[...] = half_sum[...].astype(BF16)
    copies = [
        net.start(half_low.at[rows((x + d) % 4, 32)], xin.at[d - 1], along_x(d))
        for d in range(1, 4)
    ]
    finish(copies)
    xsum[...] = (
        half_sum[rows(x, 32)] + xin[0].astype(F32) + xin[1].astype(F32) + xin[2].astype(F32)
    )
    copies = [
        net.start(xsum.at[:, lanes((y + d) % 4, QUART)], yin.at[d - 1], along_y(d))
        for d in range(1, 4)
    ]
    finish(copies)
    quart = lanes(y, QUART)
    ysum[...] = xsum[:, quart] + yin[0] + yin[1] + yin[2]
    copies = [
        net.start(ysum.at[rows((z + d) % 4, 8)], zin.at[z], along_z(d)) for d in range(1, 8)
    ]
    zin[z] = ysum[rows(z % 4, 8)]
    finish(copies)
    total = zin[0]
    for i in range(1, 8):
        total = total + zin[i]
    zmid[z % 4] = total
    finish([net.start(zmid.at[z % 4], zmid.at[z % 4], along_half_z(d)) for d in range(1, 4)])
    third = pl.ds(pl.multiple_of(c * 128 + x * 32, 32), 32)
    full[third, quart] = jnp.concatenate([zmid[i] for i in range(4)], axis=0).astype(BF16)
    block = full.at[third, quart]
    finish([net.start(block, block, along_y(d)) for d in range(1, 4)])
    block = full.at[third]
    finish([net.start(block, block, along_x(d)) for d in range(1, 4)])
    block = full.at[half]
    finish([net.start(block, block, other_core())])

    pre, inv, m_own = own_ref[0], own_ref[1], own_ref[2]
    vec = own_ref[3, 0:16]
    e_own, g1, g2 = vec[0:4], vec[7:8], vec[11:12]
    taps = [vec[8 + k : 9 + k] for k in range(3)]
    b_own = tap_rows(taps, m_own)
    energy = full[:, 0:C]
    ew = dot_nt(energy, wpad2[...])
    high, low = split(b_own)
    gram = full[:, C : C + ROWS]
    d = g2 * ew - (dot(gram, high) + dot(gram, low))
    m0, m1 = m_own[0:64], m_own[64:80]
    m2 = m_own[80:96]

    def total_rows(value):
        return jnp.sum(value, axis=0, keepdims=True)

    taps_b = [
        total_rows(m_own[0:80] * d[0:80]),
        total_rows(m_own[0:96] * d[80:176]),
        total_rows(m0 * d[176:240]) + total_rows(m2 * d[240:256]),
    ]
    gain_b = total_rows(b_own * ew)
    pick = jnp.where(
        (iota((C, PAD), 0) == pos * OWN + iota((C, PAD), 1)) & (iota((C, PAD), 1) < OWN), 1.0, 0.0
    ).astype(BF16)
    v = dot(full[0:CODES, C + ROWS : WIDE], pick[0:768]) + dot(
        full[CODES : 2 * CODES, C + ROWS : WIDE], pick[768:C]
    )
    up = v + taps[1] * d[80:176]
    up = up + jnp.concatenate(
        [taps[0] * d[0:64] + taps[2] * d[176:240], taps[0] * d[64:80], taps[2] * d[240:256]],
        axis=0,
    )
    _, slope = gelu_parts(pre[0:CODES])
    s = slope * up
    a = jnp.sum(s * pre[0:CODES], axis=1, keepdims=True) * (1.0 / C)
    inv = inv[0:CODES]
    hot_t = code_onehot(iota((16, CODES), 1), iota((16, CODES), 0))
    hot_far = code_onehot(iota((CODES, PAD), 0), iota((CODES, PAD), 1) - 64)
    f = dot(hot_t, inv * s, HIGH)
    gram_a = dot(hot_t, (inv * inv * a) * hot_far, HIGH)
    pack_rows = jnp.concatenate([jnp.zeros((12, PAD), F32)] + taps_b + [gain_b], axis=0)
    packet = f + gram_a + pack_rows
    pack[0] = packet[0:8]
    pack[1] = packet[8:16]
    packs[c, z, y] = pack[c]
    copies = [net.start(pack.at[c], packs.at[c, z, y], along_y(d)) for d in range(1, 4)]

    a_own = g2 * b_own
    high, low = split(jnp.transpose(a_own))
    finish(copies)
    block = packs.at[c, z]
    copies = [net.start(block, block, along_z(d)) for d in range(1, 8)]
    both = jnp.concatenate([high[0:OWN], low[0:OWN]], axis=0)
    for b in range(0, C, 512):
        grad = dot(both, full[:, b : b + 512])
        gwb_ref[:, b : b + 512] = grad[0:OWN] + grad[OWN : 2 * OWN]
    finish(copies)
    block = packs.at[c]
    finish([net.start(block, block, other_core())])

    gram_a = jnp.zeros((16, PAD), F32)
    fbuf[...] = jnp.zeros_like(fbuf)
    for i in range(32):
        for h in range(2):
            fbuf[8 * h : 8 * h + 8, OWN * i : OWN * i + OWN] = packs[h, i % 8, i // 8][:, 0:OWN]
        gram_a = gram_a + jnp.concatenate(
            [packs[0, i % 8, i // 8], packs[1, i % 8, i // 8]], axis=0
        )
    f = fbuf[0:16]
    te_own = jnp.concatenate(
        [vec[4 + k : 5 + k] * e_own for k in range(3)] + [jnp.zeros((4, PAD), F32)], axis=0
    )
    high, low = split(f)
    fw = dot_nt(jnp.concatenate([high, low], axis=0), wpad1[...])
    fw = fw[0:16] + fw[16:32]
    spread = jnp.concatenate(
        [jnp.zeros((64, PAD), F32), te_own, jnp.zeros((48, PAD), F32)], axis=0
    )
    far = jnp.where(iota((16, PAD), 1) >= 64, gram_a, 0.0)
    da = g1 * fw - dot(far, spread, HIGH)
    rows_a = [total_rows(e_own * da[4 * k : 4 * k + 4]) for k in range(3)]
    rows_a = rows_a + [total_rows(te_own * fw), jnp.zeros((4, PAD), F32)]
    pack2[...] = jnp.concatenate(rows_a, axis=0)
    packs2[z, y] = pack2[...]
    copies = [net.start(pack2, packs2.at[z, y], along_y(d)) for d in range(1, 4)]

    wide = jnp.concatenate([g1 * te_own, jnp.zeros((PAD - 16, PAD), F32)], axis=0)
    wide = jnp.transpose(wide)
    finish(copies)
    block = packs2.at[z]
    copies = [net.start(block, block, along_z(d)) for d in range(1, 8)]
    for b in range(0, C, 512):
        gwa_ref[:, b : b + 512] = dot(wide, fbuf[:, b : b + 512], HIGH)[0:OWN]
    finish(copies)
    for i in range(32):
        vec_ref[0:4, OWN * i : OWN * i + OWN] = packs2[i % 8, i // 8][0:4, 0:OWN]
    vec_ref[4:8, :] = fbuf[12:16, :]


def tail(x, own, w1, w2):
    vmem = pl.BlockSpec(memory_space=pltpu.VMEM)
    return pl.pallas_call(
        tail_kernel,
        out_shape=(
            jax.ShapeDtypeStruct((OWN, C), F32),
            jax.ShapeDtypeStruct((OWN, C), F32),
            jax.ShapeDtypeStruct((8, C), F32),
        ),
        in_specs=[vmem] * 4,
        out_specs=(vmem,) * 3,
        scratch_shapes=[
            pltpu.VMEM((128, WIDE), F32),
            pltpu.VMEM((128, WIDE), F32),
            pltpu.VMEM((128, WIDE), BF16),
            pltpu.VMEM((3, 32, WIDE), BF16),
            pltpu.VMEM((32, WIDE), F32),
            pltpu.VMEM((3, 32, QUART), F32),
            pltpu.VMEM((32, QUART), F32),
            pltpu.VMEM((8, 8, QUART), F32),
            pltpu.VMEM((4, 8, QUART), F32),
            pltpu.VMEM((ROWS, WIDE), BF16),
            pltpu.VMEM((PAD, C), BF16),
            pltpu.VMEM((PAD, C), BF16),
            pltpu.VMEM((2, 8, PAD), F32),
            pltpu.VMEM((2, 8, 4, 8, PAD), F32),
            pltpu.VMEM((PAD, C), F32),
            pltpu.VMEM((8, PAD), F32),
            pltpu.VMEM((8, 4, 8, PAD), F32),
            pltpu.SemaphoreType.DMA((52,)),
            pltpu.SemaphoreType.DMA((52,)),
        ],
        compiler_params=pltpu.CompilerParams(
            collective_id=1, has_side_effects=True, vmem_limit_bytes=40 * 2**20
        ),
        name="tail",
    )(x, own, w1, w2)


def shards(tokens, embed, k1, g1, w1, k2, g2, w2, cotangent):
    ext, m, p, own = tables(
        tokens, embed, k1, g1.reshape(1, C), w1, k2, g2.reshape(1, C), w2
    )
    out, x = row_work(ext, m, p, k2, cotangent[0, 0])
    gwa, gwb, vec = tail(x, own, w1, w2)
    return (out[None, None], gwa, gwb, vec[0:3], vec[4:7], vec[3], vec[7])


def solution(mesh):
    placed = (
        P("rep", "pos"),
        P(),
        P(),
        P(),
        P("pos", None),
        P(),
        P(),
        P("pos", None),
        P("rep", "strand", "pos", None),
    )
    return jax.shard_map(
        shards,
        mesh=mesh,
        in_specs=placed,
        out_specs=(
            P("rep", "strand", "pos", None),
            P("pos", None),
            P("pos", None),
            P(),
            P(),
            P(),
            P(),
        ),
        check_vma=False,
    )
```

```python
import functools

import jax
import jax.numpy as jnp
from jax import lax
from jax.experimental import pallas as pl
from jax.experimental.pallas import tpu as pltpu
from jax.sharding import PartitionSpec as P

MESH = pl.DeviceIdType.MESH
HIGH = lax.Precision.HIGHEST
F32 = jnp.float32
BF16 = jnp.bfloat16
C = 1536
L = 256
FIRST_DILATE = 32
SECOND_DILATE = 64
EPS = 1e-05
CODES = 96
PAD = 128
ROWS = 256
WIDE = 2048
QUART = WIDE // 4
BLOCK = 256
BLOCKS = C // BLOCK
OWN = 48
GELU_A = 0.7978845608028654
GELU_B = 0.044715


def coords():
    pos = lax.axis_index("pos")
    strand = lax.axis_index("strand")
    rep = lax.axis_index("rep")
    return pos // 8, pos % 8, (rep // 2) * 2 + strand, rep % 2


def device(y, z, x, c):
    return {"pos": y * 8 + z, "strand": x % 2, "rep": (x // 2) * 2 + c}


def along_y(d):
    y, z, x, c = coords()
    return device((y + d) % 4, z, x, c)


def along_z(d):
    y, z, x, c = coords()
    return device(y, (z + d) % 8, x, c)


def along_half_z(d):
    y, z, x, c = coords()
    return device(y, (z // 4) * 4 + (z + d) % 4, x, c)


def other_core():
    y, z, x, c = coords()
    return device(y, z, x, 1 - c)


PLANE = [(a, b) for a in range(4) for b in range(8) if a or b]
SQUARE = [(a, b) for a in range(4) for b in range(4) if a or b]


def in_plane(a, b):
    y, z, x, c = coords()
    return device((y + a) % 4, (z + b) % 8, x, c)


def in_square(a, b):
    y, z, x, c = coords()
    return device((y + b) % 4, z, (x + a) % 4, c)


class Net:
    def __init__(self, send, recv):
        self.send, self.recv, self.used = send, recv, 0

    def take(self, count):
        first = self.used
        self.used += count
        return first

    def copy(self, src, dst, to, sem):
        return pltpu.make_async_remote_copy(
            src_ref=src,
            dst_ref=dst,
            send_sem=self.send.at[sem],
            recv_sem=self.recv.at[sem],
            device_id=to,
            device_id_type=MESH,
        )

    def start(self, src, dst, to):
        copy = self.copy(src, dst, to, self.take(1))
        copy.start()
        return copy


def finish(copies):
    for copy in copies:
        copy.wait()


def lanes(index, width):
    return pl.ds(pl.multiple_of(index * width, 128), width)


def rows(index, height):
    return pl.ds(pl.multiple_of(index * height, 8), height)


def dot(a, b, precision=None):
    return lax.dot_general(
        a, b, (((1,), (0,)), ((), ())), preferred_element_type=F32, precision=precision
    )


def dot_nt(a, b):
    return lax.dot_general(a, b, (((1,), (1,)), ((), ())), preferred_element_type=F32)


def split(value):
    high = value.astype(BF16)
    return high, (value - high.astype(F32)).astype(BF16)


def gelu_parts(pre):
    square = pre * pre
    th = jnp.tanh(GELU_A * pre * (1.0 + GELU_B * square))
    half = 0.5 * (1.0 + th)
    slope = half + 0.5 * pre * (1.0 - th * th) * (GELU_A * (1.0 + 3.0 * GELU_B * square))
    return pre * half, slope


def code_bases(code):
    inner, left = code < 64, code < 80
    one = jnp.where(inner, code // 16, jnp.where(left, -1, (code - 80) // 4))
    two = jnp.where(inner, (code // 4) % 4, jnp.where(left, (code - 64) // 4, code % 4))
    three = jnp.where(inner | left, code % 4, -1)
    return one, two, three


def code_onehot(code, column):
    one, two, three = code_bases(code)
    hit = (column == one) & (one >= 0)
    hit = hit | (column == 4 + two) | ((column == 8 + three) & (three >= 0))
    return jnp.where(hit & (code < CODES), 1.0, 0.0)


def iota(shape, axis):
    return lax.broadcasted_iota(jnp.int32, shape, axis)


def tap_rows(taps, table):
    return jnp.concatenate(
        [taps[0] * table[0:80], taps[1] * table[0:96], taps[2] * table[0:64], taps[2] * table[80:96]],
        axis=0,
    )


def code_of(left, middle, right):
    code = jnp.where(
        left == 4,
        64 + 4 * middle + right,
        jnp.where(right == 4, 80 + 4 * left + middle, 16 * left + 4 * middle + right),
    )
    return jnp.where(middle == 4, -1, code)


def tap_index(codes):
    first, second, third = codes
    second = jnp.where(second < 0, -1, 80 + second)
    third = jnp.where(third < 0, -1, jnp.where(third < 64, 176 + third, 160 + third))
    return first, second, third


def whole_kernel(
    tok_in,
    emb_in,
    k1_in,
    g1_in,
    w1_in,
    k2_in,
    g2_in,
    w2_in,
    cot_in,
    out_out,
    gw_ref,
    vec_ref,
    tok,
    emb16,
    k1_ref,
    g1_ref,
    k2_ref,
    g2_ref,
    wpad1,
    wpad2,
    cot,
    tsend,
    trecv,
    qsend,
    qrecv,
    qown,
    qparts,
    qfull,
    aown,
    ppart,
    py,
    psum,
    pz,
    pmid,
    pbuf,
    table,
    table_slope,
    table_v,
    hot,
    hot_t,
    wide_a,
    wide_b,
    mid_t,
    cots,
    mids,
    fins,
    preu,
    slope,
    acc,
    acc2,
    out_buf,
    xbuf,
    core_send,
    from_core,
    chip_low,
    xin,
    xsum,
    zin,
    zout,
    full,
    pack,
    packs,
    fbuf,
    pack2,
    packs2,
    lsem,
    tsem,
    send,
    recv,
):
    y, z, x, c = coords()
    pos = lax.axis_index("pos")
    strand = lax.axis_index("strand")
    rep = lax.axis_index("rep")
    frame = jnp.where(strand == 1, 31 - pos, pos)
    targets = [(frame + d + 32) % 32 for d in (-1, 0, 1)]
    net = Net(send, recv)

    wpad1[OWN:PAD] = jnp.zeros((PAD - OWN, C), BF16)
    wpad2[OWN:PAD] = jnp.zeros((PAD - OWN, C), BF16)
    loads = [
        pltpu.make_async_copy(src, dst, lsem.at[i])
        for i, (src, dst) in enumerate(
            (
                (emb_in, emb16),
                (k1_in, k1_ref),
                (g1_in, g1_ref),
                (w1_in, wpad1.at[0:OWN]),
                (k2_in, k2_ref),
                (g2_in, g2_ref),
                (tok_in, tok),
                (w2_in, wpad2.at[0:OWN]),
                (cot_in, cot),
            )
        )
    ]
    for load in loads:
        load.start()

    barrier = pltpu.get_barrier_semaphore()
    peers = (
        [in_plane(a, b) for a, b in PLANE]
        + [in_square(a, b) for a, b in SQUARE if a]
        + [other_core()]
    )
    for peer in peers:
        pl.semaphore_signal(barrier, inc=1, device_id=peer, device_id_type=MESH)

    for load in loads[:7]:
        load.wait()
    tokens = jnp.broadcast_to(tok[...], (8, L)).astype(F32)
    flip = jnp.where(iota((L, L), 0) + iota((L, L), 1) == L - 1, 1.0, 0.0)
    turned = 3.0 - dot(tokens, flip)
    tsend[...] = jnp.where(strand == 1, turned, tokens).astype(jnp.int32)
    emb = emb16[...].astype(F32)
    k1, k2 = k1_ref[...], k2_ref[...]
    g1, g2 = g1_ref[...], g2_ref[...]
    packed = jnp.concatenate([emb, k1, g1, k2, g2, jnp.zeros((4, C), F32)], axis=0)
    vec = pltpu.roll(packed, lax.rem(C - pos * OWN, C), 1)[:, 0:PAD]
    vec = jnp.where(iota((16, PAD), 1) < OWN, vec, 0.0)
    e_own, g1_own, g2_own = vec[0:4], vec[7:8], vec[11:12]
    taps = [vec[8 + k : 9 + k] for k in range(3)]
    te_own = jnp.concatenate(
        [vec[4 + k : 5 + k] * e_own for k in range(3)] + [jnp.zeros((4, PAD), F32)], axis=0
    )
    high, low = split(g1_own * te_own)
    part = dot(jnp.concatenate([high, low], axis=0), wpad1[...])
    part = part[0:16] + part[16:32]
    qsend[...] = jnp.zeros_like(qsend)
    for i in range(32):
        qsend[i, :, 0:OWN] = part[0:8, OWN * i : OWN * i + OWN]
        qsend[i, :, 64 : 64 + OWN] = part[8:16, OWN * i : OWN * i + OWN]
    qrecv[pos] = qsend[pos]

    pl.semaphore_wait(barrier, len(peers))

    def token_copy(j):
        return pltpu.make_async_remote_copy(
            src_ref=tsend,
            dst_ref=trecv.at[2 - j],
            send_sem=tsem.at[0, j],
            recv_sem=tsem.at[1, j],
            device_id={"pos": targets[j], "strand": strand, "rep": rep},
            device_id_type=MESH,
        )

    for j in range(3):
        @pl.when(targets[j] != pos)
        def _():
            token_copy(j).start()

        @pl.when(targets[j] == pos)
        def _():
            trecv[2 - j] = tsend[...]

    q_copies = []
    for a, b in PLANE:
        there = ((y + a) % 4) * 8 + (z + b) % 8
        q_copies.append(net.start(qsend.at[there], qrecv.at[pos], in_plane(a, b)))

    te = jnp.concatenate([k1[k : k + 1] * emb for k in range(3)] + [jnp.zeros((4, C), F32)], axis=0)
    hot_code = code_onehot(iota((PAD, 16), 0), iota((PAD, 16), 1))
    conv = dot(hot_code, te, HIGH)
    inv_a = lax.rsqrt(jnp.mean(conv * conv, axis=-1, keepdims=True) + EPS)

    mirror = jnp.where(
        iota((BLOCK, BLOCK), 0) + iota((BLOCK, BLOCK), 1) == BLOCK - 1, 1.0, 0.0
    ).astype(BF16)
    loads[7].wait()
    loads[8].wait()

    def turn_cot(b, carry):
        here = lanes(b, BLOCK)
        there = lanes(BLOCKS - 1 - b, BLOCK)
        cots[0:L, here] = cot[:, here]
        cots[L : 2 * L, here] = dot(cot[:, there], mirror).astype(BF16)
        return carry

    lax.fori_loop(0, BLOCKS, turn_cot, 0)

    finish(q_copies)
    total = qrecv[0]
    for i in range(1, 32):
        total = total + qrecv[i]
    qown[...] = total
    qparts[pos] = total
    q_copies = [net.start(qown, qparts.at[pos], in_plane(a, b)) for a, b in PLANE]

    q_two = jnp.concatenate([total, pltpu.roll(total, 64, 1)], axis=0)
    q_two = jnp.where(iota((16, PAD), 1) < OWN, q_two, 0.0)
    pre_own = inv_a * dot(hot_code, q_two, HIGH)
    act, slope_own = gelu_parts(pre_own)
    pads = jnp.zeros((4, PAD), F32)
    center = dot(hot_code, jnp.concatenate([pads, e_own, pads, pads], axis=0), HIGH)
    m_own = jnp.where(iota((PAD, PAD), 0) < CODES, center + act, 0.0)
    m_own = m_own.astype(BF16).astype(F32)
    b_own = tap_rows(taps, m_own)
    a_own = g2_own * b_own
    aown[...] = a_own
    high, low = split(aown[rows(c, 128)])
    mine = lanes(x, 384)
    w2 = wpad2[:, mine]
    ppart[...] = dot(high, w2) + dot(low, w2)
    p_copies = [
        net.start(ppart.at[rows((y + d) % 4, 32)], py.at[d - 1], along_y(d)) for d in range(1, 4)
    ]

    for j in range(3):
        @pl.when(targets[j] != pos)
        def _():
            token_copy(j).wait()
    joined = jnp.concatenate([trecv[0], trecv[1], trecv[2]], axis=1)
    place = (pos - 1) * L + iota((8, 3 * L), 1)
    ext = jnp.where((place >= 0) & (place < 32 * L), joined, 4)
    left = pltpu.roll(ext, FIRST_DILATE, 1)
    right = pltpu.roll(ext, 3 * L - FIRST_DILATE, 1)

    def other(base):
        return jnp.where(base == 4, 4, 3 - base)

    start = L - SECOND_DILATE
    code_a = pltpu.roll(code_of(left, ext, right), 3 * L - start, 1)[:, 0:384]
    code_b = pltpu.roll(code_of(other(right), other(ext), other(left)), 3 * L - start, 1)[:, 0:384]

    def shifts(code):
        return [code[:, 0:L]] + [
            pltpu.roll(code, 384 - s, 1)[:, 0:L] for s in (SECOND_DILATE, 2 * SECOND_DILATE)
        ]

    three_a = shifts(code_a)
    three_b = shifts(code_b)[::-1]
    index = [jnp.concatenate([a, b], axis=1) for a, b in zip(tap_index(three_a), tap_index(three_b))]
    line = iota((ROWS, 2 * L), 0)
    hit = (line == index[0][0:1]) | (line == index[1][0:1]) | (line == index[2][0:1])
    hot_t[...] = jnp.where(hit, 1.0, 0.0).astype(BF16)
    mid_t[...] = jnp.where(
        iota((PAD, 2 * L), 0) == jnp.concatenate([three_a[1], three_b[1]], axis=1)[0:1], 1.0, 0.0
    ).astype(BF16)

    def column(row):
        return jnp.transpose(row.astype(F32))[:, 0:1].astype(jnp.int32)

    finish(p_copies)
    psum[...] = ppart[rows(y, 32)] + py[0] + py[1] + py[2]
    p_copies = [
        net.start(psum.at[rows((z + d) % 4, 8)], pz.at[z], along_z(d)) for d in range(1, 8)
    ]
    pz[z] = psum[rows(z % 4, 8)]

    columns = [column(row) for row in index]
    line = iota((2 * L, ROWS), 1)
    hit = (line == columns[0]) | (line == columns[1]) | (line == columns[2])
    hot[...] = jnp.where(hit, 1.0, 0.0).astype(BF16)
    line = iota((384, PAD), 1)
    wide_a[...] = jnp.where(line == column(code_a), 1.0, 0.0).astype(BF16)
    wide_b[...] = jnp.where(line == column(code_b), 1.0, 0.0).astype(BF16)

    finish(q_copies)
    for i in range(32):
        tile = qparts[i]
        qfull[0:8, OWN * i : OWN * i + OWN] = tile[:, 0:OWN]
        qfull[8:16, OWN * i : OWN * i + OWN] = tile[:, 64 : 64 + OWN]

    finish(p_copies)
    total = pz[0]
    for i in range(1, 8):
        total = total + pz[i]
    pmid[z % 4] = total
    p_copies = [
        net.start(pmid.at[z % 4], pmid.at[z % 4], along_half_z(d)) for d in range(1, 4)
    ]

    table_v[...] = jnp.zeros_like(table_v)
    pads = jnp.zeros((4, BLOCK), F32)
    sums = jnp.zeros((PAD, 128), F32)
    for b in range(BLOCKS):
        here = slice(BLOCK * b, BLOCK * b + BLOCK)
        pre = inv_a * dot(hot_code, qfull[:, here], HIGH)
        act, grad = gelu_parts(pre)
        center = dot(hot_code, jnp.concatenate([pads, emb[:, here], pads, pads], axis=0))
        live = iota((PAD, BLOCK), 0) < CODES
        table[:, here] = jnp.where(live, center + act, 0.0).astype(BF16)
        sv = jnp.where(live, grad * (0.5 * dot(mid_t[...], cots[:, here])), 0.0)
        table_v[:, here] = inv_a * sv
        prod = sv * pre
        sums = sums + prod[:, 0:128] + prod[:, 128:256]

    finish(p_copies)
    quarter = pl.ds(pl.multiple_of(c * 128 + y * 32, 32), 32)
    pbuf[quarter, mine] = jnp.concatenate([pmid[i] for i in range(4)], axis=0).astype(BF16)
    block = pbuf.at[quarter, mine]
    p_copies = [net.start(block, block, in_square(a, b)) for a, b in SQUARE]
    p_shares = [net.start(block, block, other_core())]

    hot_ct = code_onehot(iota((16, PAD), 1), iota((16, PAD), 0))
    fv = dot(hot_ct, table_v[...], HIGH)
    mean_v = jnp.sum(sums, axis=1, keepdims=True) * (1.0 / C)
    hot_gram = code_onehot(iota((PAD, PAD), 0), iota((PAD, PAD), 1) - 96)
    gram_v = dot(hot_ct, (inv_a * inv_a * mean_v) * hot_gram, HIGH)
    xbuf[:, C + ROWS : WIDE] = jnp.zeros((ROWS, WIDE - C - ROWS), F32)
    xbuf[0:16, C + ROWS : C + ROWS + PAD] = gram_v
    for i in range(16):
        xbuf[16 * i : 16 * i + 16, C + ROWS : C + ROWS + 96] = fv[:, 96 * i : 96 * i + 96]

    acc[...] = jnp.zeros_like(acc)
    acc2[...] = jnp.zeros_like(acc2)

    def first_pass(b, carry):
        here = lanes(b, BLOCK)
        m = table[:, here]
        taps2 = k2_ref[:, here]
        for n, (wide, order) in enumerate(((wide_a, (0, 1, 2)), (wide_b, (2, 1, 0)))):
            mid = dot(wide[...], m)
            conv = (
                taps2[order[0] : order[0] + 1] * mid[0:L]
                + taps2[order[1] : order[1] + 1] * mid[64 : 64 + L]
                + taps2[order[2] : order[2] + 1] * mid[128 : 128 + L]
            )
            square = conv * conv
            acc[n * L : n * L + L] += square[:, 0:128] + square[:, 128:256]
            mids[n * L : n * L + L, here] = mid[64 : 64 + L].astype(BF16)
        return carry

    lax.fori_loop(0, BLOCKS, first_pass, 0)
    acc[...] = jnp.broadcast_to(
        lax.rsqrt(jnp.sum(acc[...], axis=1, keepdims=True) * (1.0 / C) + EPS), (2 * L, 128)
    )

    for copy, (a, b) in zip(p_copies, SQUARE):
        copy.wait()
        here = pl.ds(pl.multiple_of(c * 128 + ((y - b + 4) % 4) * 32, 32), 32)
        block = pbuf.at[here, lanes((x - a + 4) % 4, 384)]
        p_shares.append(net.start(block, block, other_core()))
    finish(p_shares)

    base = net.take(BLOCKS)
    away = rows(1 - c, 128)

    def core_copy(b):
        here = lanes(b, BLOCK)
        return net.copy(core_send.at[:, here], from_core.at[:, here], other_core(), base + b)

    def second_pass(b, carry):
        here = lanes(b, BLOCK)
        preu[...] = dot(hot[...], pbuf[:, here])

        def chunk(r, carry):
            some = rows(r, 64)
            inv = acc[some][:, 0:1]
            pre = inv * preu[some]
            act, grad = gelu_parts(pre)
            fins[some, here] = (mids[some, here].astype(F32) + act).astype(BF16)
            sl = cots[some, here].astype(F32) * grad
            prod = sl * pre
            acc2[some] += prod[:, 0:128] + prod[:, 128:256]
            slope[some] = (inv * sl).astype(BF16)
            return carry

        lax.fori_loop(0, 8, chunk, 0)
        xbuf[:, here] = 0.5 * dot(hot_t[...], slope[...])
        core_send[:, here] = xbuf[away, here].astype(BF16)
        core_copy(b).start()
        return carry

    lax.fori_loop(0, BLOCKS, second_pass, 0)

    inv = acc[:, 0:1]
    weight = (0.5 / C) * inv * inv * jnp.sum(acc2[...], axis=1, keepdims=True)
    high, low = split(weight * hot[...].astype(F32))
    xbuf[:, C : C + ROWS] = dot(hot_t[...], high) + dot(hot_t[...], low)
    core_send[:, C:WIDE] = xbuf[away, C:WIDE].astype(BF16)
    last = net.start(core_send.at[:, C:WIDE], from_core.at[:, C:WIDE], other_core())
    for b in range(BLOCKS):
        core_copy(b).wait()
    half = rows(c, 128)
    xbuf[half, 0:C] = xbuf[half, 0:C] + from_core[:, 0:C].astype(F32)
    chip_low[:, 0:C] = xbuf[half, 0:C].astype(BF16)
    last.wait()
    xbuf[half, C:WIDE] = xbuf[half, C:WIDE] + from_core[:, C:WIDE].astype(F32)
    chip_low[:, C:WIDE] = xbuf[half, C:WIDE].astype(BF16)
    copies = []
    for j, (a, b) in enumerate(SQUARE):
        block = chip_low.at[rows((x + a) % 4, 32), lanes((y + b) % 4, QUART)]
        copies.append(net.start(block, xin.at[j], in_square(a, b)))

    def third_pass(b, carry):
        here = lanes(b, BLOCK)
        there = lanes(BLOCKS - 1 - b, BLOCK)
        far = dot(fins[L : 2 * L, there], mirror)
        out_buf[:, here] = (0.5 * (fins[0:L, here].astype(F32) + far)).astype(BF16)
        return carry

    lax.fori_loop(0, BLOCKS, third_pass, 0)
    store = pltpu.make_async_copy(out_buf, out_out, lsem.at[9])
    store.start()

    finish(copies)
    third = pl.ds(pl.multiple_of(c * 128 + x * 32, 32), 32)
    quart = lanes(y, QUART)
    total = xbuf[third, quart]
    for j in range(15):
        total = total + xin[j].astype(F32)
    xsum[0] = total[:, 0:256]
    xsum[1] = total[:, 256:512]
    copies = []
    for d in range(1, 8):
        to = (z + d) % 8
        copies.append(net.start(xsum.at[to // 4, rows(to % 4, 8)], zin.at[d - 1], along_z(d)))
    finish(copies)
    total = xsum[z // 4, rows(z % 4, 8)]
    for d in range(7):
        total = total + zin[d]
    zout[z] = total
    finish([net.start(zout.at[z], zout.at[z], along_z(d)) for d in range(1, 8)])
    for h in range(2):
        here = pl.ds(pl.multiple_of(y * QUART + h * 256, 128), 256)
        full[third, here] = jnp.concatenate([zout[4 * h + i] for i in range(4)], axis=0).astype(BF16)
    block = full.at[third, quart]
    copies = [net.start(block, block, in_square(a, b)) for a, b in SQUARE]
    shares = [net.start(block, block, other_core())]
    for copy, (a, b) in zip(copies, SQUARE):
        copy.wait()
        here = pl.ds(pl.multiple_of(c * 128 + ((x - a + 4) % 4) * 32, 32), 32)
        block = full.at[here, lanes((y - b + 4) % 4, QUART)]
        shares.append(net.start(block, block, other_core()))
    finish(shares)

    energy = full[:, 0:C]
    ew = dot_nt(energy, wpad2[...])
    high, low = split(b_own)
    gram = full[:, C : C + ROWS]
    d = g2_own * ew - (dot(gram, high) + dot(gram, low))

    def total_rows(value):
        return jnp.sum(value, axis=0, keepdims=True)

    taps_b = [
        total_rows(m_own[0:80] * d[0:80]),
        total_rows(m_own[0:96] * d[80:176]),
        total_rows(m_own[0:64] * d[176:240]) + total_rows(m_own[80:96] * d[240:256]),
    ]
    gain_b = total_rows(b_own * ew)
    up = taps[1] * d[80:176] + jnp.concatenate(
        [taps[0] * d[0:64] + taps[2] * d[176:240], taps[0] * d[64:80], taps[2] * d[240:256]],
        axis=0,
    )
    s = slope_own[0:CODES] * up
    inv = inv_a[0:CODES]
    mean_s = jnp.sum(s * pre_own[0:CODES], axis=1, keepdims=True) * (1.0 / C)
    narrow = hot_ct[:, 0:CODES]
    hot_far = code_onehot(iota((CODES, PAD), 0), iota((CODES, PAD), 1) - OWN)
    extra = C + ROWS
    fv = full[pl.ds(pl.multiple_of((pos // 2) * 16, 16), 16), extra : extra + PAD].astype(F32)
    fv = jnp.where(pos % 2 == 1, pltpu.roll(fv, PAD - OWN, 1), fv)
    fv = jnp.where(iota((16, PAD), 1) < OWN, fv, 0.0)
    own_rows = fv + dot(narrow, inv * s, HIGH)
    f_rows = jnp.where(iota((16, PAD), 0) < 12, own_rows, 0.0)
    vec_rows = jnp.concatenate([jnp.zeros((12, PAD), F32)] + taps_b + [gain_b], axis=0)
    packet = f_rows + vec_rows + dot(narrow, (inv * inv * mean_s) * hot_far, HIGH)
    pack[...] = packet[0:8] + pltpu.roll(packet[8:16], 64, 1)
    packs[pos] = pack[...]
    copies = [net.start(pack, packs.at[pos], in_plane(a, b)) for a, b in PLANE]

    high, low = split(jnp.transpose(a_own))
    both = jnp.concatenate([high[0:OWN], low[0:OWN]], axis=0)
    for b in range(0, C, 512):
        grad = dot(both, full[:, b : b + 512])
        gw_ref[OWN : 2 * OWN, b : b + 512] = grad[0:OWN] + grad[OWN : 2 * OWN]
    fbuf[...] = jnp.zeros_like(fbuf)
    finish(copies)
    total = jnp.zeros((8, PAD), F32)
    for i in range(32):
        tile = packs[i]
        fbuf[0:8, OWN * i : OWN * i + OWN] = tile[:, 0:OWN]
        fbuf[8:16, OWN * i : OWN * i + OWN] = tile[:, 64 : 64 + OWN]
        total = total + tile
    far = jnp.concatenate([total, pltpu.roll(total, 64, 1)], axis=0)
    far = far + pltpu.roll(full[0:16, extra : extra + PAD].astype(F32), PAD - OWN, 1)
    far = jnp.where((iota((16, PAD), 1) >= OWN) & (iota((16, PAD), 1) < OWN + 12), far, 0.0)
    high, low = split(fbuf[0:16])
    fw = dot_nt(jnp.concatenate([high, low], axis=0), wpad1[...])
    fw = fw[0:16] + fw[16:32]
    spread = jnp.concatenate(
        [jnp.zeros((OWN, PAD), F32), te_own, jnp.zeros((64, PAD), F32)], axis=0
    )
    da = g1_own * fw - dot(far, spread, HIGH)
    rows_a = [total_rows(e_own * da[4 * k : 4 * k + 4]) for k in range(3)]
    rows_a = rows_a + [total_rows(te_own * fw)]
    pack2[...] = jnp.concatenate(
        [
            rows_a[0] + pltpu.roll(rows_a[1], 64, 1),
            rows_a[2] + pltpu.roll(rows_a[3], 64, 1),
        ],
        axis=0,
    )
    packs2[pos] = pack2[...]
    copies = [net.start(pack2, packs2.at[pos], in_plane(a, b)) for a, b in PLANE]

    wide = jnp.concatenate([g1_own * te_own, jnp.zeros((PAD - 16, PAD), F32)], axis=0)
    wide = jnp.transpose(wide)
    for b in range(0, C, 512):
        gw_ref[0:OWN, b : b + 512] = dot(wide, fbuf[:, b : b + 512], HIGH)[0:OWN]
    vec_ref[4:8, :] = fbuf[12:16, :]
    finish(copies)
    for i in range(32):
        tile = packs2[i]
        here = slice(OWN * i, OWN * i + OWN)
        vec_ref[0:1, here] = tile[0:1, 0:OWN]
        vec_ref[1:2, here] = tile[0:1, 64 : 64 + OWN]
        vec_ref[2:3, here] = tile[1:2, 0:OWN]
        vec_ref[3:4, here] = tile[1:2, 64 : 64 + OWN]
    store.wait()


def whole(*args):
    vmem = pl.BlockSpec(memory_space=pltpu.VMEM)
    hbm = pl.BlockSpec(memory_space=pl.ANY)
    return pl.pallas_call(
        whole_kernel,
        out_shape=(
            jax.ShapeDtypeStruct((L, C), BF16),
            jax.ShapeDtypeStruct((2 * OWN, C), F32),
            jax.ShapeDtypeStruct((8, C), F32),
        ),
        in_specs=[hbm] * 9,
        out_specs=(hbm, vmem, vmem),
        scratch_shapes=[
            pltpu.VMEM((1, L), jnp.int32),
            pltpu.VMEM((4, C), BF16),
            pltpu.VMEM((3, C), F32),
            pltpu.VMEM((1, C), F32),
            pltpu.VMEM((3, C), F32),
            pltpu.VMEM((1, C), F32),
            pltpu.VMEM((PAD, C), BF16),
            pltpu.VMEM((PAD, C), BF16),
            pltpu.VMEM((L, C), BF16),
            pltpu.VMEM((8, L), jnp.int32),
            pltpu.VMEM((3, 8, L), jnp.int32),
            pltpu.VMEM((32, 8, PAD), F32),
            pltpu.VMEM((32, 8, PAD), F32),
            pltpu.VMEM((8, PAD), F32),
            pltpu.VMEM((32, 8, PAD), F32),
            pltpu.VMEM((16, C), F32),
            pltpu.VMEM((ROWS, PAD), F32),
            pltpu.VMEM((128, 384), F32),
            pltpu.VMEM((3, 32, 384), F32),
            pltpu.VMEM((32, 384), F32),
            pltpu.VMEM((8, 8, 384), F32),
            pltpu.VMEM((4, 8, 384), F32),
            pltpu.VMEM((ROWS, C), BF16),
            pltpu.VMEM((PAD, C), BF16),
            pltpu.VMEM((8, PAD), F32),
            pltpu.VMEM((PAD, C), F32),
            pltpu.VMEM((2 * L, ROWS), BF16),
            pltpu.VMEM((ROWS, 2 * L), BF16),
            pltpu.VMEM((384, PAD), BF16),
            pltpu.VMEM((384, PAD), BF16),
            pltpu.VMEM((PAD, 2 * L), BF16),
            pltpu.VMEM((2 * L, C), BF16),
            pltpu.VMEM((2 * L, C), BF16),
            pltpu.VMEM((2 * L, C), BF16),
            pltpu.VMEM((2 * L, BLOCK), F32),
            pltpu.VMEM((2 * L, BLOCK), BF16),
            pltpu.VMEM((2 * L, 128), F32),
            pltpu.VMEM((2 * L, 128), F32),
            pltpu.VMEM((L, C), BF16),
            pltpu.VMEM((ROWS, WIDE), F32),
            pltpu.VMEM((128, WIDE), BF16),
            pltpu.VMEM((128, WIDE), BF16),
            pltpu.VMEM((128, WIDE), BF16),
            pltpu.VMEM((15, 32, QUART), BF16),
            pltpu.VMEM((2, 32, 256), F32),
            pltpu.VMEM((7, 8, 256), F32),
            pltpu.VMEM((8, 8, 256), F32),
            pltpu.VMEM((ROWS, WIDE), BF16),
            pltpu.VMEM((8, PAD), F32),
            pltpu.VMEM((32, 8, PAD), F32),
            pltpu.VMEM((PAD, C), F32),
            pltpu.VMEM((2, PAD), F32),
            pltpu.VMEM((32, 2, PAD), F32),
            pltpu.SemaphoreType.DMA((10,)),
            pltpu.SemaphoreType.DMA((2, 3)),
            pltpu.SemaphoreType.DMA((256,)),
            pltpu.SemaphoreType.DMA((256,)),
        ],
        compiler_params=pltpu.CompilerParams(
            collective_id=0, has_side_effects=True, vmem_limit_bytes=62 * 2**20
        ),
        name="whole",
    )(*args)


def shards(tokens, embed, k1, g1, w1, k2, g2, w2, cotangent):
    out, gw, vec = whole(
        tokens,
        embed,
        k1,
        g1.reshape(1, C),
        w1,
        k2,
        g2.reshape(1, C),
        w2,
        cotangent.reshape(L, C),
    )
    return (
        out[None, None],
        gw[0:OWN],
        gw[OWN:],
        vec[0:3],
        vec[4:7],
        vec[3],
        vec[7],
    )


def solution(mesh):
    placed = (
        P("rep", "pos"),
        P(),
        P(),
        P(),
        P("pos", None),
        P(),
        P(),
        P("pos", None),
        P("rep", "strand", "pos", None),
    )
    return jax.shard_map(
        shards,
        mesh=mesh,
        in_specs=placed,
        out_specs=(
            P("rep", "strand", "pos", None),
            P("pos", None),
            P("pos", None),
            P(),
            P(),
            P(),
            P(),
        ),
        check_vma=False,
    )
```

```python
import functools

import jax
import jax.numpy as jnp
from jax import lax
from jax.experimental import pallas as pl
from jax.experimental.pallas import tpu as pltpu
from jax.sharding import PartitionSpec as P

MESH = pl.DeviceIdType.MESH
HIGH = lax.Precision.HIGHEST
F32 = jnp.float32
BF16 = jnp.bfloat16
C = 1536
L = 256
FIRST_DILATE = 32
SECOND_DILATE = 64
EPS = 1e-05
CODES = 96
PAD = 128
ROWS = 256
WIDE = 2048
BLOCK = 256
BLOCKS = C // BLOCK
OWN = 48
GELU_A = 0.7978845608028654
GELU_B = 0.044715


def coords():
    pos = lax.axis_index("pos")
    strand = lax.axis_index("strand")
    rep = lax.axis_index("rep")
    return pos // 8, pos % 8, (rep // 2) * 2 + strand, rep % 2


def device(y, z, x, c):
    return {"pos": y * 8 + z, "strand": x % 2, "rep": (x // 2) * 2 + c}


def along_y(d):
    y, z, x, c = coords()
    return device((y + d) % 4, z, x, c)


def along_z(d):
    y, z, x, c = coords()
    return device(y, (z + d) % 8, x, c)


def along_half_z(d):
    y, z, x, c = coords()
    return device(y, (z // 4) * 4 + (z + d) % 4, x, c)


def other_core():
    y, z, x, c = coords()
    return device(y, z, x, 1 - c)


PLANE = [(a, b) for a in range(4) for b in range(8) if a or b]
SQUARE = [(a, b) for a in range(4) for b in range(4) if a or b]


def in_plane(a, b):
    y, z, x, c = coords()
    return device((y + a) % 4, (z + b) % 8, x, c)


def in_square(a, b):
    y, z, x, c = coords()
    return device((y + b) % 4, z, (x + a) % 4, c)


class Net:
    def __init__(self, send, recv):
        self.send, self.recv, self.used = send, recv, 0

    def take(self, count):
        first = self.used
        self.used += count
        return first

    def copy(self, src, dst, to, sem):
        return pltpu.make_async_remote_copy(
            src_ref=src,
            dst_ref=dst,
            send_sem=self.send.at[sem],
            recv_sem=self.recv.at[sem],
            device_id=to,
            device_id_type=MESH,
        )

    def start(self, src, dst, to):
        copy = self.copy(src, dst, to, self.take(1))
        copy.start()
        return copy


def finish(copies):
    for copy in copies:
        copy.wait()


def lanes(index, width):
    return pl.ds(pl.multiple_of(index * width, 128), width)


def rows(index, height):
    return pl.ds(pl.multiple_of(index * height, 8), height)


def dot(a, b, precision=None):
    return lax.dot_general(
        a, b, (((1,), (0,)), ((), ())), preferred_element_type=F32, precision=precision
    )


def dot_nt(a, b):
    return lax.dot_general(a, b, (((1,), (1,)), ((), ())), preferred_element_type=F32)


def split(value):
    high = value.astype(BF16)
    return high, (value - high.astype(F32)).astype(BF16)


def gelu_parts(pre):
    square = pre * pre
    th = jnp.tanh(pre * (GELU_A + (GELU_A * GELU_B) * square))
    half = 0.5 + 0.5 * th
    bend = pre * (GELU_A + (3.0 * GELU_A * GELU_B) * square)
    return pre * half, half * (1.0 + (1.0 - th) * bend)


def code_bases(code):
    inner, left = code < 64, code < 80
    one = jnp.where(inner, code // 16, jnp.where(left, -1, (code - 80) // 4))
    two = jnp.where(inner, (code // 4) % 4, jnp.where(left, (code - 64) // 4, code % 4))
    three = jnp.where(inner | left, code % 4, -1)
    return one, two, three


def code_onehot(code, column):
    one, two, three = code_bases(code)
    hit = (column == one) & (one >= 0)
    hit = hit | (column == 4 + two) | ((column == 8 + three) & (three >= 0))
    return jnp.where(hit & (code < CODES), 1.0, 0.0)


def iota(shape, axis):
    return lax.broadcasted_iota(jnp.int32, shape, axis)


def tap_rows(taps, table):
    return jnp.concatenate(
        [taps[0] * table[0:80], taps[1] * table[0:96], taps[2] * table[0:64], taps[2] * table[80:96]],
        axis=0,
    )


def code_of(left, middle, right):
    code = jnp.where(
        left == 4,
        64 + 4 * middle + right,
        jnp.where(right == 4, 80 + 4 * left + middle, 16 * left + 4 * middle + right),
    )
    return jnp.where(middle == 4, -1, code)


def tap_index(codes):
    first, second, third = codes
    second = jnp.where(second < 0, -1, 80 + second)
    third = jnp.where(third < 0, -1, jnp.where(third < 64, 176 + third, 160 + third))
    return first, second, third


def whole_kernel(
    tok_in,
    emb_in,
    k1_in,
    g1_in,
    w1_in,
    k2_in,
    g2_in,
    w2_in,
    cot_in,
    out_out,
    gw_ref,
    vec_ref,
    tok,
    emb16,
    k1_ref,
    g1_ref,
    k2_ref,
    g2_ref,
    wpad1,
    wpad2,
    cot,
    tsend,
    trecv,
    qsend,
    qrecv,
    qown,
    qparts,
    qfull,
    aown,
    ppart,
    py,
    psum,
    pz,
    pmid,
    pbuf,
    table,
    table_slope,
    table_v,
    hot,
    hot_t,
    wide_a,
    wide_b,
    mid_t,
    cots,
    mids,
    fins,
    preu,
    slope,
    acc,
    acc2,
    out_buf,
    xbuf,
    core_send,
    from_core,
    chip_low,
    xin,
    xsum,
    zin,
    zout,
    full,
    pack,
    packs,
    fbuf,
    pack2,
    packs2,
    lsem,
    tsem,
    send,
    recv,
):
    y, z, x, c = coords()
    pos = lax.axis_index("pos")
    strand = lax.axis_index("strand")
    rep = lax.axis_index("rep")
    frame = jnp.where(strand == 1, 31 - pos, pos)
    targets = [(frame + d + 32) % 32 for d in (-1, 0, 1)]
    net = Net(send, recv)

    wpad1[OWN:PAD] = jnp.zeros((PAD - OWN, C), BF16)
    wpad2[OWN:PAD] = jnp.zeros((PAD - OWN, C), BF16)
    loads = [
        pltpu.make_async_copy(src, dst, lsem.at[i])
        for i, (src, dst) in enumerate(
            (
                (emb_in, emb16),
                (k1_in, k1_ref),
                (g1_in, g1_ref),
                (w1_in, wpad1.at[0:OWN]),
                (k2_in, k2_ref),
                (g2_in, g2_ref),
                (tok_in, tok),
                (w2_in, wpad2.at[0:OWN]),
                (cot_in, cot),
            )
        )
    ]
    for load in loads:
        load.start()

    barrier = pltpu.get_barrier_semaphore()
    peers = (
        [in_plane(a, b) for a, b in PLANE]
        + [in_square(a, b) for a, b in SQUARE if a]
        + [other_core()]
    )
    for peer in peers:
        pl.semaphore_signal(barrier, inc=1, device_id=peer, device_id_type=MESH)

    for load in loads[:6]:
        load.wait()
    emb = emb16[...].astype(F32)
    k1, k2 = k1_ref[...], k2_ref[...]
    g1, g2 = g1_ref[...].reshape(1, C), g2_ref[...].reshape(1, C)
    packed = jnp.concatenate([emb, k1, g1, k2, g2, jnp.zeros((4, C), F32)], axis=0)
    vec = pltpu.roll(packed, lax.rem(C - pos * OWN, C), 1)[:, 0:PAD]
    vec = jnp.where(iota((16, PAD), 1) < OWN, vec, 0.0)
    e_own, g1_own, g2_own = vec[0:4], vec[7:8], vec[11:12]
    taps = [vec[8 + k : 9 + k] for k in range(3)]
    te_own = jnp.concatenate(
        [vec[4 + k : 5 + k] * e_own for k in range(3)] + [jnp.zeros((4, PAD), F32)], axis=0
    )
    high, low = split(g1_own * te_own)
    part = dot(jnp.concatenate([high, low], axis=0), wpad1[...])
    part = part[0:16] + part[16:32]
    qsend[...] = jnp.zeros_like(qsend)
    for i in range(32):
        qsend[i, :, 0:OWN] = part[0:8, OWN * i : OWN * i + OWN]
        qsend[i, :, 64 : 64 + OWN] = part[8:16, OWN * i : OWN * i + OWN]
    qrecv[pos] = qsend[pos]

    pl.semaphore_wait(barrier, len(peers))

    q_copies = []
    for a, b in PLANE:
        there = ((y + a) % 4) * 8 + (z + b) % 8
        q_copies.append(net.start(qsend.at[there], qrecv.at[pos], in_plane(a, b)))

    loads[6].wait()
    tokens = jnp.broadcast_to(tok[...], (8, L)).astype(F32)
    flip = jnp.where(iota((L, L), 0) + iota((L, L), 1) == L - 1, 1.0, 0.0)
    turned = 3.0 - dot(tokens, flip)
    tsend[...] = jnp.where(strand == 1, turned, tokens).astype(jnp.int32)

    def token_copy(j):
        return pltpu.make_async_remote_copy(
            src_ref=tsend,
            dst_ref=trecv.at[2 - j],
            send_sem=tsem.at[0, j],
            recv_sem=tsem.at[1, j],
            device_id={"pos": targets[j], "strand": strand, "rep": rep},
            device_id_type=MESH,
        )

    for j in range(3):
        @pl.when(targets[j] != pos)
        def _():
            token_copy(j).start()

        @pl.when(targets[j] == pos)
        def _():
            trecv[2 - j] = tsend[...]

    te = jnp.concatenate([k1[k : k + 1] * emb for k in range(3)] + [jnp.zeros((4, C), F32)], axis=0)
    hot_code = code_onehot(iota((PAD, 16), 0), iota((PAD, 16), 1))
    conv = dot(hot_code, te, HIGH)
    inv_a = lax.rsqrt(jnp.mean(conv * conv, axis=-1, keepdims=True) + EPS)

    mirror = jnp.where(
        iota((BLOCK, BLOCK), 0) + iota((BLOCK, BLOCK), 1) == BLOCK - 1, 1.0, 0.0
    ).astype(BF16)
    loads[7].wait()
    loads[8].wait()

    def turn_cot(b, carry):
        here = lanes(b, BLOCK)
        there = lanes(BLOCKS - 1 - b, BLOCK)
        cots[0:L, here] = cot[:, here]
        cots[L : 2 * L, here] = dot(cot[:, there], mirror).astype(BF16)
        return carry

    lax.fori_loop(0, BLOCKS, turn_cot, 0)

    finish(q_copies)
    total = qrecv[0]
    for i in range(1, 32):
        total = total + qrecv[i]
    qown[...] = total
    qparts[pos] = total

    q_two = jnp.concatenate([total, pltpu.roll(total, 64, 1)], axis=0)
    q_two = jnp.where(iota((16, PAD), 1) < OWN, q_two, 0.0)
    pre_own = inv_a * dot(hot_code, q_two, HIGH)
    act, slope_own = gelu_parts(pre_own)
    pads = jnp.zeros((4, PAD), F32)
    center = dot(hot_code, jnp.concatenate([pads, e_own, pads, pads], axis=0), HIGH)
    m_own = jnp.where(iota((PAD, PAD), 0) < CODES, center + act, 0.0)
    m_own = m_own.astype(BF16).astype(F32)
    b_own = tap_rows(taps, m_own)
    a_own = g2_own * b_own
    aown[...] = a_own
    high, low = split(aown[rows(c, 128)])
    mine = lanes(x, 384)
    w2 = wpad2[:, mine]
    ppart[...] = dot(high, w2) + dot(low, w2)
    p_copies = [
        net.start(ppart.at[rows((y + d) % 4, 32)], py.at[d - 1], along_y(d)) for d in range(1, 4)
    ]
    q_copies = [net.start(qown, qparts.at[pos], in_plane(a, b)) for a, b in PLANE]

    for j in range(3):
        @pl.when(targets[j] != pos)
        def _():
            token_copy(j).wait()
    joined = jnp.concatenate([trecv[0], trecv[1], trecv[2]], axis=1)
    place = (pos - 1) * L + iota((8, 3 * L), 1)
    ext = jnp.where((place >= 0) & (place < 32 * L), joined, 4)
    left = pltpu.roll(ext, FIRST_DILATE, 1)
    right = pltpu.roll(ext, 3 * L - FIRST_DILATE, 1)

    def other(base):
        return jnp.where(base == 4, 4, 3 - base)

    start = L - SECOND_DILATE
    code_a = pltpu.roll(code_of(left, ext, right), 3 * L - start, 1)[:, 0:384]
    code_b = pltpu.roll(code_of(other(right), other(ext), other(left)), 3 * L - start, 1)[:, 0:384]

    def shifts(code):
        return [code[:, 0:L]] + [
            pltpu.roll(code, 384 - s, 1)[:, 0:L] for s in (SECOND_DILATE, 2 * SECOND_DILATE)
        ]

    three_a = shifts(code_a)
    three_b = shifts(code_b)[::-1]
    index = [jnp.concatenate([a, b], axis=1) for a, b in zip(tap_index(three_a), tap_index(three_b))]
    line = iota((ROWS, 2 * L), 0)
    hit = (line == index[0][0:1]) | (line == index[1][0:1]) | (line == index[2][0:1])
    hot_t[...] = jnp.where(hit, 1.0, 0.0).astype(BF16)
    mid_t[...] = jnp.where(
        iota((PAD, 2 * L), 0) == jnp.concatenate([three_a[1], three_b[1]], axis=1)[0:1], 1.0, 0.0
    ).astype(BF16)

    def column(row):
        return jnp.transpose(row.astype(F32))[:, 0:1].astype(jnp.int32)

    finish(p_copies)
    psum[...] = ppart[rows(y, 32)] + py[0] + py[1] + py[2]
    p_copies = [
        net.start(psum.at[rows((z + d) % 4, 8)], pz.at[z], along_z(d)) for d in range(1, 8)
    ]
    pz[z] = psum[rows(z % 4, 8)]

    columns = [column(row) for row in index]
    line = iota((2 * L, ROWS), 1)
    hit = (line == columns[0]) | (line == columns[1]) | (line == columns[2])
    hot[...] = jnp.where(hit, 1.0, 0.0).astype(BF16)
    line = iota((384, PAD), 1)
    wide_a[...] = jnp.where(line == column(code_a), 1.0, 0.0).astype(BF16)
    wide_b[...] = jnp.where(line == column(code_b), 1.0, 0.0).astype(BF16)

    finish(q_copies)
    for i in range(32):
        tile = qparts[i]
        qfull[0:8, OWN * i : OWN * i + OWN] = tile[:, 0:OWN]
        qfull[8:16, OWN * i : OWN * i + OWN] = tile[:, 64 : 64 + OWN]

    table_v[...] = jnp.zeros_like(table_v)
    pads = jnp.zeros((4, BLOCK), F32)
    sums = jnp.zeros((PAD, 128), F32)
    for b in range(BLOCKS):
        if b == BLOCKS // 2:
            finish(p_copies)
            total = pz[0]
            for i in range(1, 8):
                total = total + pz[i]
            pmid[z % 4] = total
            p_copies = [
                net.start(pmid.at[z % 4], pmid.at[z % 4], along_half_z(d)) for d in range(1, 4)
            ]
        here = slice(BLOCK * b, BLOCK * b + BLOCK)
        pre = inv_a * dot(hot_code, qfull[:, here], HIGH)
        act, grad = gelu_parts(pre)
        center = dot(hot_code, jnp.concatenate([pads, emb[:, here], pads, pads], axis=0))
        live = iota((PAD, BLOCK), 0) < CODES
        table[:, here] = jnp.where(live, center + act, 0.0).astype(BF16)
        sv = jnp.where(live, grad * (0.5 * dot(mid_t[...], cots[:, here])), 0.0)
        table_v[:, here] = inv_a * sv
        prod = sv * pre
        sums = sums + prod[:, 0:128] + prod[:, 128:256]

    finish(p_copies)
    quarter = pl.ds(pl.multiple_of(c * 128 + y * 32, 32), 32)
    pbuf[quarter, mine] = jnp.concatenate([pmid[i] for i in range(4)], axis=0).astype(BF16)
    block = pbuf.at[quarter, mine]
    p_copies = [net.start(block, block, in_square(a, b)) for a, b in SQUARE]
    p_shares = [net.start(block, block, other_core())]

    hot_ct = code_onehot(iota((16, PAD), 1), iota((16, PAD), 0))
    fv = dot(hot_ct, table_v[...], HIGH)
    mean_v = jnp.sum(sums, axis=1, keepdims=True) * (1.0 / C)
    hot_gram = code_onehot(iota((PAD, PAD), 0), iota((PAD, PAD), 1) - 96)
    gram_v = dot(hot_ct, (inv_a * inv_a * mean_v) * hot_gram, HIGH)
    xbuf[:, C + ROWS : WIDE] = jnp.zeros((ROWS, WIDE - C - ROWS), F32)
    xbuf[0:16, C + ROWS : C + ROWS + PAD] = gram_v
    for i in range(16):
        xbuf[16 * i : 16 * i + 16, C + ROWS : C + ROWS + 96] = fv[:, 96 * i : 96 * i + 96]

    acc[...] = jnp.zeros_like(acc)
    acc2[...] = jnp.zeros_like(acc2)

    def first_pass(b, carry):
        here = lanes(b, BLOCK)
        m = table[:, here]
        taps2 = k2_ref[:, here]
        for n, (wide, order) in enumerate(((wide_a, (0, 1, 2)), (wide_b, (2, 1, 0)))):
            mid = dot(wide[...], m)
            conv = (
                taps2[order[0] : order[0] + 1] * mid[0:L]
                + taps2[order[1] : order[1] + 1] * mid[64 : 64 + L]
                + taps2[order[2] : order[2] + 1] * mid[128 : 128 + L]
            )
            square = conv * conv
            acc[n * L : n * L + L] += square[:, 0:128] + square[:, 128:256]
            mids[n * L : n * L + L, here] = mid[64 : 64 + L].astype(BF16)
        return carry

    lax.fori_loop(0, BLOCKS, first_pass, 0)
    acc[...] = jnp.broadcast_to(
        lax.rsqrt(jnp.sum(acc[...], axis=1, keepdims=True) * (1.0 / C) + EPS), (2 * L, 128)
    )

    for copy, (a, b) in zip(p_copies, SQUARE):
        copy.wait()
        here = pl.ds(pl.multiple_of(c * 128 + ((y - b + 4) % 4) * 32, 32), 32)
        block = pbuf.at[here, lanes((x - a + 4) % 4, 384)]
        p_shares.append(net.start(block, block, other_core()))
    finish(p_shares)

    base = net.take(BLOCKS)
    away = rows(1 - c, 128)

    def core_copy(b):
        here = lanes(b, BLOCK)
        return net.copy(core_send.at[:, here], from_core.at[:, here], other_core(), base + b)

    def second_pass(b, carry):
        here = lanes(b, BLOCK)
        preu[...] = dot(hot[...], pbuf[:, here])

        def chunk(r, carry):
            some = rows(r, 64)
            inv = acc[some]
            kept = acc2[some]
            for part in (0, 128):
                cut = pl.ds(pl.multiple_of(b * BLOCK + part, 128), 128)
                pre = inv * preu[some, part : part + 128]
                act, grad = gelu_parts(pre)
                fins[some, cut] = (mids[some, cut].astype(F32) + act).astype(BF16)
                sl = cots[some, cut].astype(F32) * grad
                kept = kept + sl * pre
                slope[some, part : part + 128] = (inv * sl).astype(BF16)
            acc2[some] = kept
            return carry

        lax.fori_loop(0, 8, chunk, 0)
        xbuf[:, here] = 0.5 * dot(hot_t[...], slope[...])
        core_send[:, here] = xbuf[away, here].astype(BF16)
        core_copy(b).start()
        return carry

    half = rows(c, 128)
    third = pl.ds(pl.multiple_of(c * 128 + x * 32, 32), 32)

    def chip_sum(first, last):
        xbuf[half, first:last] = xbuf[half, first:last] + from_core[:, first:last].astype(F32)
        chip_low[:, first:last] = xbuf[half, first:last].astype(BF16)

    def strip(h, at):
        return pl.ds(pl.multiple_of(1024 * h + at * 256, 128), 256)

    def square_scatter(h):
        return [
            net.start(
                chip_low.at[rows((x + a) % 4, 32), strip(h, (y + b) % 4)], xin.at[h, j], in_square(a, b)
            )
            for j, (a, b) in enumerate(SQUARE)
        ]

    def line_scatter(h, copies):
        finish(copies)
        total = xbuf[third, strip(h, y)]
        for j in range(15):
            total = total + xin[h, j].astype(F32)
        xsum[h, 0] = total[:, 0:128]
        xsum[h, 1] = total[:, 128:256]
        started = []
        for d in range(1, 8):
            to = (z + d) % 8
            block = xsum.at[h, to // 4, rows(to % 4, 8)]
            started.append(net.start(block, zin.at[h, d - 1], along_z(d)))
        return started

    def line_gather(h, copies):
        finish(copies)
        total = xsum[h, z // 4, rows(z % 4, 8)]
        for d in range(7):
            total = total + zin[h, d]
        zout[h, z] = total
        return [net.start(zout.at[h, z], zout.at[h, z], along_z(d)) for d in range(1, 8)]

    def square_gather(h, copies):
        finish(copies)
        for i in range(2):
            here = pl.ds(pl.multiple_of(1024 * h + y * 256 + 128 * i, 128), 128)
            tiles = [zout[h, 4 * i + q] for q in range(4)]
            full[third, here] = jnp.concatenate(tiles, axis=0).astype(BF16)
        block = full.at[third, strip(h, y)]
        shares = [net.start(block, block, other_core())]
        return [net.start(block, block, in_square(a, b)) for a, b in SQUARE], shares

    def share(h, copies, shares):
        for copy, (a, b) in zip(copies, SQUARE):
            copy.wait()
            here = pl.ds(pl.multiple_of(c * 128 + ((x - a + 4) % 4) * 32, 32), 32)
            block = full.at[here, strip(h, (y - b + 4) % 4)]
            shares.append(net.start(block, block, other_core()))

    lax.fori_loop(0, 4, second_pass, 0)
    for b in range(4):
        core_copy(b).wait()
    chip_sum(0, 1024)
    scatter_0 = square_scatter(0)
    lax.fori_loop(4, BLOCKS, second_pass, 0)

    inv = acc[:, 0:1]
    weight = (0.5 / C) * inv * inv * jnp.sum(acc2[...], axis=1, keepdims=True)
    high, low = split(weight * hot[...].astype(F32))
    xbuf[:, C : C + ROWS] = dot(hot_t[...], high) + dot(hot_t[...], low)
    core_send[:, C:WIDE] = xbuf[away, C:WIDE].astype(BF16)
    last = net.start(core_send.at[:, C:WIDE], from_core.at[:, C:WIDE], other_core())
    for b in range(4, BLOCKS):
        core_copy(b).wait()
    chip_sum(1024, C)
    last.wait()
    chip_sum(C, WIDE)
    scatter_1 = square_scatter(1)
    line_0 = line_scatter(0, scatter_0)

    def third_pass(b, carry):
        here = lanes(b, BLOCK)
        there = lanes(BLOCKS - 1 - b, BLOCK)
        far = dot(fins[L : 2 * L, there], mirror)
        out_buf[:, here] = (0.5 * (fins[0:L, here].astype(F32) + far)).astype(BF16)
        return carry

    lax.fori_loop(0, BLOCKS, third_pass, 0)
    store = pltpu.make_async_copy(out_buf, out_out, lsem.at[9])
    store.start()

    gather_0 = line_gather(0, line_0)
    line_1 = line_scatter(1, scatter_1)
    back_0, shares_0 = square_gather(0, gather_0)
    gather_1 = line_gather(1, line_1)
    back_1, shares_1 = square_gather(1, gather_1)
    share(0, back_0, shares_0)
    finish(shares_0)
    turned_high, turned_low = split(jnp.transpose(a_own))
    both = jnp.concatenate([turned_high[0:OWN], turned_low[0:OWN]], axis=0)

    def grad_b(b):
        grad = dot(both, full[:, b : b + 512])
        gw_ref[OWN : 2 * OWN, b : b + 512] = grad[0:OWN] + grad[OWN : 2 * OWN]

    ew = dot_nt(full[:, 0:1024], wpad2[:, 0:1024])
    grad_b(0)
    grad_b(512)
    fbuf[...] = jnp.zeros_like(fbuf)
    share(1, back_1, shares_1)
    finish(shares_1)

    ew = ew + dot_nt(full[:, 1024:C], wpad2[:, 1024:C])
    high, low = split(b_own)
    gram = full[:, C : C + ROWS]
    d = g2_own * ew - (dot(gram, high) + dot(gram, low))

    def total_rows(value):
        return jnp.sum(value, axis=0, keepdims=True)

    taps_b = [
        total_rows(m_own[0:80] * d[0:80]),
        total_rows(m_own[0:96] * d[80:176]),
        total_rows(m_own[0:64] * d[176:240]) + total_rows(m_own[80:96] * d[240:256]),
    ]
    gain_b = total_rows(b_own * ew)
    up = taps[1] * d[80:176] + jnp.concatenate(
        [taps[0] * d[0:64] + taps[2] * d[176:240], taps[0] * d[64:80], taps[2] * d[240:256]],
        axis=0,
    )
    s = slope_own[0:CODES] * up
    inv = inv_a[0:CODES]
    mean_s = jnp.sum(s * pre_own[0:CODES], axis=1, keepdims=True) * (1.0 / C)
    narrow = hot_ct[:, 0:CODES]
    hot_far = code_onehot(iota((CODES, PAD), 0), iota((CODES, PAD), 1) - OWN)
    extra = C + ROWS
    fv = full[pl.ds(pl.multiple_of((pos // 2) * 16, 16), 16), extra : extra + PAD].astype(F32)
    fv = jnp.where(pos % 2 == 1, pltpu.roll(fv, PAD - OWN, 1), fv)
    fv = jnp.where(iota((16, PAD), 1) < OWN, fv, 0.0)
    own_rows = fv + dot(narrow, inv * s, HIGH)
    f_rows = jnp.where(iota((16, PAD), 0) < 12, own_rows, 0.0)
    vec_rows = jnp.concatenate([jnp.zeros((12, PAD), F32)] + taps_b + [gain_b], axis=0)
    packet = f_rows + vec_rows + dot(narrow, (inv * inv * mean_s) * hot_far, HIGH)
    pack[...] = packet[0:8] + pltpu.roll(packet[8:16], 64, 1)
    packs[pos] = pack[...]
    copies = [net.start(pack, packs.at[pos], in_plane(a, b)) for a, b in PLANE]

    grad_b(1024)
    finish(copies)
    total = jnp.zeros((8, PAD), F32)
    for i in range(32):
        tile = packs[i]
        fbuf[0:8, OWN * i : OWN * i + OWN] = tile[:, 0:OWN]
        fbuf[8:16, OWN * i : OWN * i + OWN] = tile[:, 64 : 64 + OWN]
        total = total + tile
    far = jnp.concatenate([total, pltpu.roll(total, 64, 1)], axis=0)
    far = far + pltpu.roll(full[0:16, extra : extra + PAD].astype(F32), PAD - OWN, 1)
    far = jnp.where((iota((16, PAD), 1) >= OWN) & (iota((16, PAD), 1) < OWN + 12), far, 0.0)
    high, low = split(fbuf[0:16])
    fw = dot_nt(jnp.concatenate([high, low], axis=0), wpad1[...])
    fw = fw[0:16] + fw[16:32]
    spread = jnp.concatenate(
        [jnp.zeros((OWN, PAD), F32), te_own, jnp.zeros((64, PAD), F32)], axis=0
    )
    da = g1_own * fw - dot(far, spread, HIGH)
    rows_a = [total_rows(e_own * da[4 * k : 4 * k + 4]) for k in range(3)]
    rows_a = rows_a + [total_rows(te_own * fw)]
    pack2[...] = jnp.concatenate(
        [
            rows_a[0] + pltpu.roll(rows_a[1], 64, 1),
            rows_a[2] + pltpu.roll(rows_a[3], 64, 1),
        ],
        axis=0,
    )
    packs2[pos] = pack2[...]
    copies = [net.start(pack2, packs2.at[pos], in_plane(a, b)) for a, b in PLANE]

    wide = jnp.concatenate([g1_own * te_own, jnp.zeros((PAD - 16, PAD), F32)], axis=0)
    wide = jnp.transpose(wide)
    for b in range(0, C, 512):
        gw_ref[0:OWN, b : b + 512] = dot(wide, fbuf[:, b : b + 512], HIGH)[0:OWN]
    vec_ref[4:8, :] = fbuf[12:16, :]
    finish(copies)
    for i in range(32):
        tile = packs2[i]
        here = slice(OWN * i, OWN * i + OWN)
        vec_ref[0:1, here] = tile[0:1, 0:OWN]
        vec_ref[1:2, here] = tile[0:1, 64 : 64 + OWN]
        vec_ref[2:3, here] = tile[1:2, 0:OWN]
        vec_ref[3:4, here] = tile[1:2, 64 : 64 + OWN]
    store.wait()


def whole(*args):
    vmem = pl.BlockSpec(memory_space=pltpu.VMEM)
    hbm = pl.BlockSpec(memory_space=pltpu.HBM)
    anywhere = pl.BlockSpec(memory_space=pl.ANY)
    return pl.pallas_call(
        whole_kernel,
        out_shape=(
            jax.ShapeDtypeStruct((L, C), BF16),
            jax.ShapeDtypeStruct((2 * OWN, C), F32),
            jax.ShapeDtypeStruct((8, C), F32),
        ),
        in_specs=[hbm] * 9,
        out_specs=(anywhere, vmem, vmem),
        scratch_shapes=[
            pltpu.VMEM((1, L), jnp.int32),
            pltpu.VMEM((4, C), BF16),
            pltpu.VMEM((3, C), F32),
            pltpu.VMEM((C,), F32),
            pltpu.VMEM((3, C), F32),
            pltpu.VMEM((C,), F32),
            pltpu.VMEM((PAD, C), BF16),
            pltpu.VMEM((PAD, C), BF16),
            pltpu.VMEM((L, C), BF16),
            pltpu.VMEM((8, L), jnp.int32),
            pltpu.VMEM((3, 8, L), jnp.int32),
            pltpu.VMEM((32, 8, PAD), F32),
            pltpu.VMEM((32, 8, PAD), F32),
            pltpu.VMEM((8, PAD), F32),
            pltpu.VMEM((32, 8, PAD), F32),
            pltpu.VMEM((16, C), F32),
            pltpu.VMEM((ROWS, PAD), F32),
            pltpu.VMEM((128, 384), F32),
            pltpu.VMEM((3, 32, 384), F32),
            pltpu.VMEM((32, 384), F32),
            pltpu.VMEM((8, 8, 384), F32),
            pltpu.VMEM((4, 8, 384), F32),
            pltpu.VMEM((ROWS, C), BF16),
            pltpu.VMEM((PAD, C), BF16),
            pltpu.VMEM((8, PAD), F32),
            pltpu.VMEM((PAD, C), F32),
            pltpu.VMEM((2 * L, ROWS), BF16),
            pltpu.VMEM((ROWS, 2 * L), BF16),
            pltpu.VMEM((384, PAD), BF16),
            pltpu.VMEM((384, PAD), BF16),
            pltpu.VMEM((PAD, 2 * L), BF16),
            pltpu.VMEM((2 * L, C), BF16),
            pltpu.VMEM((2 * L, C), BF16),
            pltpu.VMEM((2 * L, C), BF16),
            pltpu.VMEM((2 * L, BLOCK), F32),
            pltpu.VMEM((2 * L, BLOCK), BF16),
            pltpu.VMEM((2 * L, 128), F32),
            pltpu.VMEM((2 * L, 128), F32),
            pltpu.VMEM((L, C), BF16),
            pltpu.VMEM((ROWS, WIDE), F32),
            pltpu.VMEM((128, WIDE), BF16),
            pltpu.VMEM((128, WIDE), BF16),
            pltpu.VMEM((128, WIDE), BF16),
            pltpu.VMEM((2, 15, 32, 256), BF16),
            pltpu.VMEM((2, 2, 32, 128), F32),
            pltpu.VMEM((2, 7, 8, 128), F32),
            pltpu.VMEM((2, 8, 8, 128), F32),
            pltpu.VMEM((ROWS, WIDE), BF16),
            pltpu.VMEM((8, PAD), F32),
            pltpu.VMEM((32, 8, PAD), F32),
            pltpu.VMEM((PAD, C), F32),
            pltpu.VMEM((2, PAD), F32),
            pltpu.VMEM((32, 2, PAD), F32),
            pltpu.SemaphoreType.DMA((10,)),
            pltpu.SemaphoreType.DMA((2, 3)),
            pltpu.SemaphoreType.DMA((320,)),
            pltpu.SemaphoreType.DMA((320,)),
        ],
        compiler_params=pltpu.CompilerParams(
            collective_id=0, has_side_effects=True, vmem_limit_bytes=62 * 2**20
        ),
        name="whole",
    )(*args)


def place_kernel(out_in, gw_in, vec_ref, out_ref, gwa_ref, gwb_ref, ta_ref, tb_ref, ga_ref, gb_ref):
    out_ref[...] = out_in[...]
    gwa_ref[...] = gw_in[0:OWN]
    gwb_ref[...] = gw_in[OWN : 2 * OWN]
    ta_ref[...] = vec_ref[0:3]
    tb_ref[...] = vec_ref[4:7]
    ga_ref[...] = vec_ref[3]
    gb_ref[...] = vec_ref[7]


def placed_outputs(out, gw, vec):
    vmem = pl.BlockSpec(memory_space=pltpu.VMEM)
    return pl.pallas_call(
        place_kernel,
        out_shape=(
            jax.ShapeDtypeStruct((L, C), BF16),
            jax.ShapeDtypeStruct((OWN, C), F32),
            jax.ShapeDtypeStruct((OWN, C), F32),
            jax.ShapeDtypeStruct((3, C), F32),
            jax.ShapeDtypeStruct((3, C), F32),
            jax.ShapeDtypeStruct((C,), F32),
            jax.ShapeDtypeStruct((C,), F32),
        ),
        in_specs=[vmem] * 3,
        out_specs=(vmem,) * 7,
        compiler_params=pltpu.CompilerParams(vmem_limit_bytes=62 * 2**20),
        name="place",
    )(out, gw, vec)


def shards(tokens, embed, k1, g1, w1, k2, g2, w2, cotangent):
    out, gw, vec = whole(tokens, embed, k1, g1, w1, k2, g2, w2, cotangent.reshape(L, C))
    out, gwa, gwb, ta, tb, ga, gb = placed_outputs(out, gw, vec)
    return (out[None, None], gwa, gwb, ta, tb, ga, gb)


def solution(mesh):
    placed = (
        P("rep", "pos"),
        P(),
        P(),
        P(),
        P("pos", None),
        P(),
        P(),
        P("pos", None),
        P("rep", "strand", "pos", None),
    )
    return jax.shard_map(
        shards,
        mesh=mesh,
        in_specs=placed,
        out_specs=(
            P("rep", "strand", "pos", None),
            P("pos", None),
            P("pos", None),
            P(),
            P(),
            P(),
            P(),
        ),
        check_vma=False,
    )
```

```python
import functools

import jax
import jax.numpy as jnp
from jax import lax
from jax.experimental import pallas as pl
from jax.experimental.pallas import tpu as pltpu
from jax.sharding import PartitionSpec as P

MESH = pl.DeviceIdType.MESH
HIGH = lax.Precision.HIGHEST
F32 = jnp.float32
BF16 = jnp.bfloat16
C = 1536
L = 256
FIRST_DILATE = 32
SECOND_DILATE = 64
EPS = 1e-05
CODES = 96
PAD = 128
ROWS = 256
WIDE = 2048
BLOCK = 256
BLOCKS = C // BLOCK
OWN = 48
GELU_A = 0.7978845608028654
GELU_B = 0.044715


def coords():
    pos = lax.axis_index("pos")
    strand = lax.axis_index("strand")
    rep = lax.axis_index("rep")
    return pos // 8, pos % 8, (rep // 2) * 2 + strand, rep % 2


def device(y, z, x, c):
    return {"pos": y * 8 + z, "strand": x % 2, "rep": (x // 2) * 2 + c}


def along_y(d):
    y, z, x, c = coords()
    return device((y + d) % 4, z, x, c)


def along_z(d):
    y, z, x, c = coords()
    return device(y, (z + d) % 8, x, c)


def along_half_z(d):
    y, z, x, c = coords()
    return device(y, (z // 4) * 4 + (z + d) % 4, x, c)


def other_core():
    y, z, x, c = coords()
    return device(y, z, x, 1 - c)


PLANE = [(a, b) for a in range(4) for b in range(8) if a or b]
SQUARE = [(a, b) for a in range(4) for b in range(4) if a or b]


def in_plane(a, b):
    y, z, x, c = coords()
    return device((y + a) % 4, (z + b) % 8, x, c)


def in_square(a, b):
    y, z, x, c = coords()
    return device((y + b) % 4, z, (x + a) % 4, c)


class Net:
    def __init__(self, send, recv):
        self.send, self.recv, self.used = send, recv, 0

    def take(self, count):
        first = self.used
        self.used += count
        return first

    def copy(self, src, dst, to, sem):
        return pltpu.make_async_remote_copy(
            src_ref=src,
            dst_ref=dst,
            send_sem=self.send.at[sem],
            recv_sem=self.recv.at[sem],
            device_id=to,
            device_id_type=MESH,
        )

    def start(self, items, total):
        sem = self.take(1)
        for src, dst, to in items:
            self.copy(src, dst, to, sem).start()
        return self.copy(total, total, other_core(), sem)


def share_out(onehot, value, parts):
    total = None
    for _ in range(parts):
        part = value.astype(BF16)
        value = value - part.astype(F32)
        term = dot(onehot.astype(BF16), part)
        total = term if total is None else total + term
    return total


def lanes(index, width):
    return pl.ds(pl.multiple_of(index * width, 128), width)


def rows(index, height):
    return pl.ds(pl.multiple_of(index * height, 8), height)


def dot(a, b, precision=None):
    return lax.dot_general(
        a, b, (((1,), (0,)), ((), ())), preferred_element_type=F32, precision=precision
    )


def dot_nt(a, b):
    return lax.dot_general(a, b, (((1,), (1,)), ((), ())), preferred_element_type=F32)


def split(value):
    high = value.astype(BF16)
    return high, (value - high.astype(F32)).astype(BF16)


def gelu_parts(pre):
    square = pre * pre
    th = jnp.tanh(pre * (GELU_A + (GELU_A * GELU_B) * square))
    half = 0.5 + 0.5 * th
    bend = pre * (GELU_A + (3.0 * GELU_A * GELU_B) * square)
    return pre * half, half * (1.0 + (1.0 - th) * bend)


def code_bases(code):
    inner, left = code < 64, code < 80
    one = jnp.where(inner, code // 16, jnp.where(left, -1, (code - 80) // 4))
    two = jnp.where(inner, (code // 4) % 4, jnp.where(left, (code - 64) // 4, code % 4))
    three = jnp.where(inner | left, code % 4, -1)
    return one, two, three


def code_onehot(code, column):
    one, two, three = code_bases(code)
    hit = (column == one) & (one >= 0)
    hit = hit | (column == 4 + two) | ((column == 8 + three) & (three >= 0))
    return jnp.where(hit & (code < CODES), 1.0, 0.0)


def iota(shape, axis):
    return lax.broadcasted_iota(jnp.int32, shape, axis)


def tap_rows(taps, table):
    return jnp.concatenate(
        [taps[0] * table[0:80], taps[1] * table[0:96], taps[2] * table[0:64], taps[2] * table[80:96]],
        axis=0,
    )


def code_of(left, middle, right):
    code = jnp.where(
        left == 4,
        64 + 4 * middle + right,
        jnp.where(right == 4, 80 + 4 * left + middle, 16 * left + 4 * middle + right),
    )
    return jnp.where(middle == 4, -1, code)


def tap_index(codes):
    first, second, third = codes
    second = jnp.where(second < 0, -1, 80 + second)
    third = jnp.where(third < 0, -1, jnp.where(third < 64, 176 + third, 160 + third))
    return first, second, third


def whole_kernel(
    tok_in,
    emb_in,
    k1_in,
    g1_in,
    w1_in,
    k2_in,
    g2_in,
    w2_in,
    cot_in,
    out_out,
    gw_ref,
    vec_ref,
    tok,
    emb16,
    k1_ref,
    g1_ref,
    k2_ref,
    g2_ref,
    wpad1,
    wpad2,
    cot,
    tsend,
    trecv,
    qsend,
    qrecv,
    qown,
    qparts,
    qfull,
    aown,
    ppart,
    py,
    psum,
    pz,
    pmid,
    pbuf,
    table,
    table_slope,
    table_v,
    hot,
    hot_t,
    wide_a,
    wide_b,
    mid_t,
    cots,
    mids,
    fins,
    preu,
    slope,
    acc,
    acc2,
    out_buf,
    xbuf,
    core_send,
    from_core,
    chip_low,
    xin,
    xsum,
    zin,
    zout,
    full,
    pack,
    packs,
    fbuf,
    pack2,
    packs2,
    lsem,
    tsem,
    send,
    recv,
):
    y, z, x, c = coords()
    pos = lax.axis_index("pos")
    strand = lax.axis_index("strand")
    rep = lax.axis_index("rep")
    frame = jnp.where(strand == 1, 31 - pos, pos)
    targets = [(frame + d + 32) % 32 for d in (-1, 0, 1)]
    net = Net(send, recv)

    wpad1[OWN:PAD] = jnp.zeros((PAD - OWN, C), BF16)
    wpad2[OWN:PAD] = jnp.zeros((PAD - OWN, C), BF16)
    loads = [
        pltpu.make_async_copy(src, dst, lsem.at[i])
        for i, (src, dst) in enumerate(
            (
                (emb_in, emb16),
                (k1_in, k1_ref),
                (g1_in, g1_ref),
                (w1_in, wpad1.at[0:OWN]),
                (k2_in, k2_ref),
                (g2_in, g2_ref),
                (tok_in, tok),
                (w2_in, wpad2.at[0:OWN]),
                (cot_in, cot),
            )
        )
    ]
    for load in loads:
        load.start()

    barrier = pltpu.get_barrier_semaphore()
    peers = (
        [in_plane(a, b) for a, b in PLANE]
        + [in_square(a, b) for a, b in SQUARE if a]
        + [other_core()]
    )
    for peer in peers:
        pl.semaphore_signal(barrier, inc=1, device_id=peer, device_id_type=MESH)

    for load in loads[:6]:
        load.wait()
    emb = emb16[...].astype(F32)
    k1, k2 = k1_ref[...], k2_ref[...]
    g1, g2 = g1_ref[...].reshape(1, C), g2_ref[...].reshape(1, C)
    packed = jnp.concatenate([emb, k1, g1, k2, g2, jnp.zeros((4, C), F32)], axis=0)
    vec = pltpu.roll(packed, lax.rem(C - pos * OWN, C), 1)[:, 0:PAD]
    vec = jnp.where(iota((16, PAD), 1) < OWN, vec, 0.0)
    e_own, g1_own, g2_own = vec[0:4], vec[7:8], vec[11:12]
    taps = [vec[8 + k : 9 + k] for k in range(3)]
    te_own = jnp.concatenate(
        [vec[4 + k : 5 + k] * e_own for k in range(3)] + [jnp.zeros((4, PAD), F32)], axis=0
    )
    high, low = split(g1_own * te_own)
    part = dot(jnp.concatenate([high, low], axis=0), wpad1[...])
    part = part[0:16] + part[16:32]
    qsend[...] = jnp.zeros_like(qsend)
    for i in range(32):
        qsend[i, :, 0:OWN] = part[0:8, OWN * i : OWN * i + OWN]
        qsend[i, :, 64 : 64 + OWN] = part[8:16, OWN * i : OWN * i + OWN]
    qrecv[pos] = qsend[pos]

    pl.semaphore_wait(barrier, len(peers))

    q_copies = net.start(
        [
            (qsend.at[((y + a) % 4) * 8 + (z + b) % 8], qrecv.at[pos], in_plane(a, b))
            for a, b in PLANE
        ],
        qrecv.at[0:31],
    )

    loads[6].wait()
    tokens = jnp.broadcast_to(tok[...], (8, L)).astype(F32)
    flip = jnp.where(iota((L, L), 0) + iota((L, L), 1) == L - 1, 1.0, 0.0)
    turned = 3.0 - dot(tokens, flip)
    tsend[...] = jnp.where(strand == 1, turned, tokens).astype(jnp.int32)

    def token_copy(j):
        return pltpu.make_async_remote_copy(
            src_ref=tsend,
            dst_ref=trecv.at[2 - j],
            send_sem=tsem.at[0, j],
            recv_sem=tsem.at[1, j],
            device_id={"pos": targets[j], "strand": strand, "rep": rep},
            device_id_type=MESH,
        )

    for j in range(3):
        @pl.when(targets[j] != pos)
        def _():
            token_copy(j).start()

        @pl.when(targets[j] == pos)
        def _():
            trecv[2 - j] = tsend[...]

    te = jnp.concatenate([k1[k : k + 1] * emb for k in range(3)] + [jnp.zeros((4, C), F32)], axis=0)
    hot_code = code_onehot(iota((PAD, 16), 0), iota((PAD, 16), 1))
    conv = share_out(hot_code, te, 3)
    inv_a = lax.rsqrt(jnp.mean(conv * conv, axis=-1, keepdims=True) + EPS)

    mirror = jnp.where(
        iota((BLOCK, BLOCK), 0) + iota((BLOCK, BLOCK), 1) == BLOCK - 1, 1.0, 0.0
    ).astype(BF16)
    loads[7].wait()
    loads[8].wait()

    def turn_cot(b, carry):
        here = lanes(b, BLOCK)
        there = lanes(BLOCKS - 1 - b, BLOCK)
        cots[0:L, here] = cot[:, here]
        cots[L : 2 * L, here] = dot(cot[:, there], mirror).astype(BF16)
        return carry

    lax.fori_loop(0, BLOCKS, turn_cot, 0)

    q_copies.wait()
    total = qrecv[0]
    for i in range(1, 32):
        total = total + qrecv[i]
    qown[...] = total
    qparts[pos] = total

    q_two = jnp.concatenate([total, pltpu.roll(total, 64, 1)], axis=0)
    q_two = jnp.where(iota((16, PAD), 1) < OWN, q_two, 0.0)
    pre_own = inv_a * share_out(hot_code, q_two, 3)
    act, slope_own = gelu_parts(pre_own)
    pads = jnp.zeros((4, PAD), F32)
    center = share_out(hot_code, jnp.concatenate([pads, e_own, pads, pads], axis=0), 1)
    m_own = jnp.where(iota((PAD, PAD), 0) < CODES, center + act, 0.0)
    m_own = m_own.astype(BF16).astype(F32)
    b_own = tap_rows(taps, m_own)
    a_own = g2_own * b_own
    aown[...] = a_own
    high, low = split(aown[rows(c, 128)])
    mine = lanes(x, 384)
    w2 = wpad2[:, mine]
    ppart[...] = dot(high, w2) + dot(low, w2)
    p_copies = net.start(
        [(ppart.at[rows((y + d) % 4, 32)], py.at[d - 1], along_y(d)) for d in range(1, 4)], py
    )
    q_copies = net.start(
        [(qown, qparts.at[pos], in_plane(a, b)) for a, b in PLANE], qparts.at[0:31]
    )

    for j in range(3):
        @pl.when(targets[j] != pos)
        def _():
            token_copy(j).wait()
    joined = jnp.concatenate([trecv[0], trecv[1], trecv[2]], axis=1)
    place = (pos - 1) * L + iota((8, 3 * L), 1)
    ext = jnp.where((place >= 0) & (place < 32 * L), joined, 4)
    left = pltpu.roll(ext, FIRST_DILATE, 1)
    right = pltpu.roll(ext, 3 * L - FIRST_DILATE, 1)

    def other(base):
        return jnp.where(base == 4, 4, 3 - base)

    start = L - SECOND_DILATE
    code_a = pltpu.roll(code_of(left, ext, right), 3 * L - start, 1)[:, 0:384]
    code_b = pltpu.roll(code_of(other(right), other(ext), other(left)), 3 * L - start, 1)[:, 0:384]

    def shifts(code):
        return [code[:, 0:L]] + [
            pltpu.roll(code, 384 - s, 1)[:, 0:L] for s in (SECOND_DILATE, 2 * SECOND_DILATE)
        ]

    three_a = shifts(code_a)
    three_b = shifts(code_b)[::-1]
    index = [jnp.concatenate([a, b], axis=1) for a, b in zip(tap_index(three_a), tap_index(three_b))]
    line = iota((ROWS, 2 * L), 0)
    hit = (line == index[0][0:1]) | (line == index[1][0:1]) | (line == index[2][0:1])
    hot_t[...] = jnp.where(hit, 1.0, 0.0).astype(BF16)
    mid_t[...] = jnp.where(
        iota((PAD, 2 * L), 0) == jnp.concatenate([three_a[1], three_b[1]], axis=1)[0:1], 1.0, 0.0
    ).astype(BF16)

    def column(row):
        return jnp.transpose(row.astype(F32))[:, 0:1].astype(jnp.int32)

    p_copies.wait()
    psum[...] = ppart[rows(y, 32)] + py[0] + py[1] + py[2]
    p_copies = net.start(
        [(psum.at[rows((z + d) % 4, 8)], pz.at[z], along_z(d)) for d in range(1, 8)], pz.at[0:7]
    )
    pz[z] = psum[rows(z % 4, 8)]

    columns = [column(row) for row in index]
    line = iota((2 * L, ROWS), 1)
    hit = (line == columns[0]) | (line == columns[1]) | (line == columns[2])
    hot[...] = jnp.where(hit, 1.0, 0.0).astype(BF16)
    line = iota((384, PAD), 1)
    wide_a[...] = jnp.where(line == column(code_a), 1.0, 0.0).astype(BF16)
    wide_b[...] = jnp.where(line == column(code_b), 1.0, 0.0).astype(BF16)

    q_copies.wait()
    for i in range(32):
        tile = qparts[i]
        qfull[0:8, OWN * i : OWN * i + OWN] = tile[:, 0:OWN]
        qfull[8:16, OWN * i : OWN * i + OWN] = tile[:, 64 : 64 + OWN]

    table_v[...] = jnp.zeros_like(table_v)
    pads = jnp.zeros((4, BLOCK), F32)
    sums = jnp.zeros((PAD, 128), F32)
    for b in range(BLOCKS):
        if b == BLOCKS // 2:
            p_copies.wait()
            total = pz[0]
            for i in range(1, 8):
                total = total + pz[i]
            pmid[z % 4] = total
            p_copies = net.start(
                [(pmid.at[z % 4], pmid.at[z % 4], along_half_z(d)) for d in range(1, 4)],
                pmid.at[0:3],
            )
        here = slice(BLOCK * b, BLOCK * b + BLOCK)
        pre = inv_a * share_out(hot_code, qfull[:, here], 3)
        act, grad = gelu_parts(pre)
        center = share_out(
            hot_code, jnp.concatenate([pads, emb[:, here], pads, pads], axis=0), 1
        )
        live = iota((PAD, BLOCK), 0) < CODES
        table[:, here] = jnp.where(live, center + act, 0.0).astype(BF16)
        sv = jnp.where(live, grad * (0.5 * dot(mid_t[...], cots[:, here])), 0.0)
        table_v[:, here] = inv_a * sv
        prod = sv * pre
        sums = sums + prod[:, 0:128] + prod[:, 128:256]

    p_copies.wait()
    quarter = pl.ds(pl.multiple_of(c * 128 + y * 32, 32), 32)
    pbuf[quarter, mine] = jnp.concatenate([pmid[i] for i in range(4)], axis=0).astype(BF16)
    block = pbuf.at[quarter, mine]
    p_copies = net.start(
        [(block, block, in_square(a, b)) for a, b in SQUARE], pbuf.at[0:240, 0:768]
    )

    hot_ct = code_onehot(iota((16, PAD), 1), iota((16, PAD), 0))
    fv = share_out(hot_ct, table_v[...], 2)
    mean_v = jnp.sum(sums, axis=1, keepdims=True) * (1.0 / C)
    hot_gram = code_onehot(iota((PAD, PAD), 0), iota((PAD, PAD), 1) - 96)
    gram_v = share_out(hot_ct, (inv_a * inv_a * mean_v) * hot_gram, 2)
    xbuf[:, C + ROWS : WIDE] = jnp.zeros((ROWS, WIDE - C - ROWS), F32)
    xbuf[0:16, C + ROWS : C + ROWS + PAD] = gram_v
    for i in range(16):
        xbuf[16 * i : 16 * i + 16, C + ROWS : C + ROWS + 96] = fv[:, 96 * i : 96 * i + 96]

    acc[...] = jnp.zeros_like(acc)
    acc2[...] = jnp.zeros_like(acc2)

    def first_pass(b, carry):
        here = lanes(b, BLOCK)
        m = table[:, here]
        taps2 = k2_ref[:, here]
        for n, (wide, order) in enumerate(((wide_a, (0, 1, 2)), (wide_b, (2, 1, 0)))):
            mid = dot(wide[...], m)
            conv = (
                taps2[order[0] : order[0] + 1] * mid[0:L]
                + taps2[order[1] : order[1] + 1] * mid[64 : 64 + L]
                + taps2[order[2] : order[2] + 1] * mid[128 : 128 + L]
            )
            square = conv * conv
            acc[n * L : n * L + L] += square[:, 0:128] + square[:, 128:256]
            mids[n * L : n * L + L, here] = mid[64 : 64 + L].astype(BF16)
        return carry

    lax.fori_loop(0, BLOCKS, first_pass, 0)
    acc[...] = jnp.broadcast_to(
        lax.rsqrt(jnp.sum(acc[...], axis=1, keepdims=True) * (1.0 / C) + EPS), (2 * L, 128)
    )

    half = rows(c, 128)
    p_copies.wait()
    net.start([(pbuf.at[half], pbuf.at[half], other_core())], pbuf.at[half]).wait()

    base = net.take(2)
    away = rows(1 - c, 128)

    def core_copy(b):
        here = lanes(b, BLOCK)
        return net.copy(core_send.at[:, here], from_core.at[:, here], other_core(), base + b // 4)

    def second_pass(b, carry):
        here = lanes(b, BLOCK)
        preu[...] = dot(hot[...], pbuf[:, here])

        def chunk(r, carry):
            some = rows(r, 64)
            inv = acc[some]
            kept = acc2[some]
            for part in (0, 128):
                cut = pl.ds(pl.multiple_of(b * BLOCK + part, 128), 128)
                pre = inv * preu[some, part : part + 128]
                act, grad = gelu_parts(pre)
                fins[some, cut] = (mids[some, cut].astype(F32) + act).astype(BF16)
                sl = cots[some, cut].astype(F32) * grad
                kept = kept + sl * pre
                slope[some, part : part + 128] = (inv * sl).astype(BF16)
            acc2[some] = kept
            return carry

        lax.fori_loop(0, 8, chunk, 0)
        xbuf[:, here] = 0.5 * dot(hot_t[...], slope[...])
        core_send[:, here] = xbuf[away, here].astype(BF16)
        core_copy(b).start()
        return carry

    third = pl.ds(pl.multiple_of(c * 128 + x * 32, 32), 32)

    def chip_sum(first, last):
        xbuf[half, first:last] = xbuf[half, first:last] + from_core[:, first:last].astype(F32)
        chip_low[:, first:last] = xbuf[half, first:last].astype(BF16)

    def strip(h, at):
        return pl.ds(pl.multiple_of(1024 * h + at * 256, 128), 256)

    def square_scatter(h):
        items = []
        for j, (a, b) in enumerate(SQUARE):
            block = chip_low.at[rows((x + a) % 4, 32), strip(h, (y + b) % 4)]
            items.append((block, xin.at[h, j], in_square(a, b)))
        return net.start(items, xin.at[h])

    def line_scatter(h, copies):
        copies.wait()
        total = xbuf[third, strip(h, y)]
        for j in range(15):
            total = total + xin[h, j].astype(F32)
        xsum[h, 0] = total[:, 0:128]
        xsum[h, 1] = total[:, 128:256]
        items = []
        for d in range(1, 8):
            to = (z + d) % 8
            block = xsum.at[h, to // 4, rows(to % 4, 8)]
            items.append((block, zin.at[h, d - 1], along_z(d)))
        return net.start(items, zin.at[h])

    def line_gather(h, copies):
        copies.wait()
        total = xsum[h, z // 4, rows(z % 4, 8)]
        for d in range(7):
            total = total + zin[h, d]
        zout[h, z] = total
        items = [(zout.at[h, z], zout.at[h, z], along_z(d)) for d in range(1, 8)]
        return net.start(items, zout.at[h, 0:7])

    def square_gather(h, copies):
        copies.wait()
        for i in range(2):
            here = pl.ds(pl.multiple_of(1024 * h + y * 256 + 128 * i, 128), 128)
            tiles = [zout[h, 4 * i + q] for q in range(4)]
            full[third, here] = jnp.concatenate(tiles, axis=0).astype(BF16)
        block = full.at[third, strip(h, y)]
        items = [(block, block, in_square(a, b)) for a, b in SQUARE]
        return net.start(items, full.at[0:240, 0:512])

    def share(h, copies):
        copies.wait()
        block = full.at[half, 1024 * h : 1024 * h + 1024]
        return net.start([(block, block, other_core())], block)

    lax.fori_loop(0, 4, second_pass, 0)
    net.copy(core_send.at[:, 0:1024], from_core.at[:, 0:1024], other_core(), base).wait()
    chip_sum(0, 1024)
    scatter_0 = square_scatter(0)
    lax.fori_loop(4, BLOCKS, second_pass, 0)

    inv = acc[:, 0:1]
    weight = (0.5 / C) * inv * inv * jnp.sum(acc2[...], axis=1, keepdims=True)
    high, low = split(weight * hot[...].astype(F32))
    xbuf[:, C : C + ROWS] = dot(hot_t[...], high) + dot(hot_t[...], low)
    core_send[:, C:WIDE] = xbuf[away, C:WIDE].astype(BF16)
    net.copy(core_send.at[:, C:WIDE], from_core.at[:, C:WIDE], other_core(), base + 1).start()
    net.copy(core_send.at[:, 1024:WIDE], from_core.at[:, 1024:WIDE], other_core(), base + 1).wait()
    chip_sum(1024, WIDE)
    scatter_1 = square_scatter(1)
    line_0 = line_scatter(0, scatter_0)

    gather_0 = line_gather(0, line_0)
    line_1 = line_scatter(1, scatter_1)

    def third_pass(b, carry):
        here = lanes(b, BLOCK)
        there = lanes(BLOCKS - 1 - b, BLOCK)
        far = dot(fins[L : 2 * L, there], mirror)
        out_buf[:, here] = (0.5 * (fins[0:L, here].astype(F32) + far)).astype(BF16)
        return carry

    lax.fori_loop(0, BLOCKS, third_pass, 0)
    store = pltpu.make_async_copy(out_buf, out_out, lsem.at[9])
    store.start()

    back_0 = square_gather(0, gather_0)
    gather_1 = line_gather(1, line_1)
    back_1 = square_gather(1, gather_1)
    shares = share(0, back_0)
    turned_high, turned_low = split(jnp.transpose(a_own))
    both = jnp.concatenate([turned_high[0:OWN], turned_low[0:OWN]], axis=0)

    def grad_b(b):
        grad = dot(both, full[:, b : b + 512])
        gw_ref[OWN : 2 * OWN, b : b + 512] = grad[0:OWN] + grad[OWN : 2 * OWN]

    shares.wait()
    ew = dot_nt(full[:, 0:1024], wpad2[:, 0:1024])
    shares = share(1, back_1)
    grad_b(0)
    grad_b(512)
    fbuf[...] = jnp.zeros_like(fbuf)
    shares.wait()

    ew = ew + dot_nt(full[:, 1024:C], wpad2[:, 1024:C])
    high, low = split(b_own)
    gram = full[:, C : C + ROWS]
    d = g2_own * ew - (dot(gram, high) + dot(gram, low))

    def total_rows(value):
        return jnp.sum(value, axis=0, keepdims=True)

    taps_b = [
        total_rows(m_own[0:80] * d[0:80]),
        total_rows(m_own[0:96] * d[80:176]),
        total_rows(m_own[0:64] * d[176:240]) + total_rows(m_own[80:96] * d[240:256]),
    ]
    gain_b = total_rows(b_own * ew)
    up = taps[1] * d[80:176] + jnp.concatenate(
        [taps[0] * d[0:64] + taps[2] * d[176:240], taps[0] * d[64:80], taps[2] * d[240:256]],
        axis=0,
    )
    s = slope_own[0:CODES] * up
    inv = inv_a[0:CODES]
    mean_s = jnp.sum(s * pre_own[0:CODES], axis=1, keepdims=True) * (1.0 / C)
    narrow = hot_ct[:, 0:CODES]
    hot_far = code_onehot(iota((CODES, PAD), 0), iota((CODES, PAD), 1) - OWN)
    extra = C + ROWS
    fv = full[pl.ds(pl.multiple_of((pos // 2) * 16, 16), 16), extra : extra + PAD].astype(F32)
    fv = jnp.where(pos % 2 == 1, pltpu.roll(fv, PAD - OWN, 1), fv)
    fv = jnp.where(iota((16, PAD), 1) < OWN, fv, 0.0)
    own_rows = fv + share_out(narrow, inv * s, 2)
    f_rows = jnp.where(iota((16, PAD), 0) < 12, own_rows, 0.0)
    vec_rows = jnp.concatenate([jnp.zeros((12, PAD), F32)] + taps_b + [gain_b], axis=0)
    packet = f_rows + vec_rows + share_out(narrow, (inv * inv * mean_s) * hot_far, 2)
    pack[...] = packet[0:8] + pltpu.roll(packet[8:16], 64, 1)
    packs[pos] = pack[...]
    copies = net.start([(pack, packs.at[pos], in_plane(a, b)) for a, b in PLANE], packs.at[0:31])

    grad_b(1024)
    copies.wait()
    total = jnp.zeros((8, PAD), F32)
    for i in range(32):
        tile = packs[i]
        fbuf[0:8, OWN * i : OWN * i + OWN] = tile[:, 0:OWN]
        fbuf[8:16, OWN * i : OWN * i + OWN] = tile[:, 64 : 64 + OWN]
        total = total + tile
    far = jnp.concatenate([total, pltpu.roll(total, 64, 1)], axis=0)
    far = far + pltpu.roll(full[0:16, extra : extra + PAD].astype(F32), PAD - OWN, 1)
    far = jnp.where((iota((16, PAD), 1) >= OWN) & (iota((16, PAD), 1) < OWN + 12), far, 0.0)
    high, low = split(fbuf[0:16])
    fw = dot_nt(jnp.concatenate([high, low], axis=0), wpad1[...])
    fw = fw[0:16] + fw[16:32]
    spread = jnp.concatenate(
        [jnp.zeros((OWN, PAD), F32), te_own, jnp.zeros((64, PAD), F32)], axis=0
    )
    da = g1_own * fw - dot(far, spread, HIGH)
    rows_a = [total_rows(e_own * da[4 * k : 4 * k + 4]) for k in range(3)]
    rows_a = rows_a + [total_rows(te_own * fw)]
    pack2[...] = jnp.concatenate(
        [
            rows_a[0] + pltpu.roll(rows_a[1], 64, 1),
            rows_a[2] + pltpu.roll(rows_a[3], 64, 1),
        ],
        axis=0,
    )
    packs2[pos] = pack2[...]
    copies = net.start(
        [(pack2, packs2.at[pos], in_plane(a, b)) for a, b in PLANE], packs2.at[0:31]
    )

    wide = jnp.concatenate([g1_own * te_own, jnp.zeros((PAD - 16, PAD), F32)], axis=0)
    wide_high, wide_low = split(jnp.transpose(wide)[0:OWN])
    wide = jnp.concatenate([wide_high, wide_low], axis=0)
    for b in range(0, C, 512):
        f_high, f_low = split(fbuf[:, b : b + 512])
        grad = dot(wide, f_high)
        gw_ref[0:OWN, b : b + 512] = grad[0:OWN] + grad[OWN : 2 * OWN] + dot(wide_high, f_low)
    vec_ref[4:8, :] = fbuf[12:16, :]
    copies.wait()
    for i in range(32):
        tile = packs2[i]
        here = slice(OWN * i, OWN * i + OWN)
        vec_ref[0:1, here] = tile[0:1, 0:OWN]
        vec_ref[1:2, here] = tile[0:1, 64 : 64 + OWN]
        vec_ref[2:3, here] = tile[1:2, 0:OWN]
        vec_ref[3:4, here] = tile[1:2, 64 : 64 + OWN]
    store.wait()


def whole(*args):
    vmem = pl.BlockSpec(memory_space=pltpu.VMEM)
    hbm = pl.BlockSpec(memory_space=pltpu.HBM)
    anywhere = pl.BlockSpec(memory_space=pl.ANY)
    return pl.pallas_call(
        whole_kernel,
        out_shape=(
            jax.ShapeDtypeStruct((L, C), BF16),
            jax.ShapeDtypeStruct((2 * OWN, C), F32),
            jax.ShapeDtypeStruct((8, C), F32),
        ),
        in_specs=[hbm] * 9,
        out_specs=(anywhere, vmem, vmem),
        scratch_shapes=[
            pltpu.VMEM((1, L), jnp.int32),
            pltpu.VMEM((4, C), BF16),
            pltpu.VMEM((3, C), F32),
            pltpu.VMEM((C,), F32),
            pltpu.VMEM((3, C), F32),
            pltpu.VMEM((C,), F32),
            pltpu.VMEM((PAD, C), BF16),
            pltpu.VMEM((PAD, C), BF16),
            pltpu.VMEM((L, C), BF16),
            pltpu.VMEM((8, L), jnp.int32),
            pltpu.VMEM((3, 8, L), jnp.int32),
            pltpu.VMEM((32, 8, PAD), F32),
            pltpu.VMEM((32, 8, PAD), F32),
            pltpu.VMEM((8, PAD), F32),
            pltpu.VMEM((32, 8, PAD), F32),
            pltpu.VMEM((16, C), F32),
            pltpu.VMEM((ROWS, PAD), F32),
            pltpu.VMEM((128, 384), F32),
            pltpu.VMEM((3, 32, 384), F32),
            pltpu.VMEM((32, 384), F32),
            pltpu.VMEM((8, 8, 384), F32),
            pltpu.VMEM((4, 8, 384), F32),
            pltpu.VMEM((ROWS, C), BF16),
            pltpu.VMEM((PAD, C), BF16),
            pltpu.VMEM((8, PAD), F32),
            pltpu.VMEM((PAD, C), F32),
            pltpu.VMEM((2 * L, ROWS), BF16),
            pltpu.VMEM((ROWS, 2 * L), BF16),
            pltpu.VMEM((384, PAD), BF16),
            pltpu.VMEM((384, PAD), BF16),
            pltpu.VMEM((PAD, 2 * L), BF16),
            pltpu.VMEM((2 * L, C), BF16),
            pltpu.VMEM((2 * L, C), BF16),
            pltpu.VMEM((2 * L, C), BF16),
            pltpu.VMEM((2 * L, BLOCK), F32),
            pltpu.VMEM((2 * L, BLOCK), BF16),
            pltpu.VMEM((2 * L, 128), F32),
            pltpu.VMEM((2 * L, 128), F32),
            pltpu.VMEM((L, C), BF16),
            pltpu.VMEM((ROWS, WIDE), F32),
            pltpu.VMEM((128, WIDE), BF16),
            pltpu.VMEM((128, WIDE), BF16),
            pltpu.VMEM((128, WIDE), BF16),
            pltpu.VMEM((2, 15, 32, 256), BF16),
            pltpu.VMEM((2, 2, 32, 128), F32),
            pltpu.VMEM((2, 7, 8, 128), F32),
            pltpu.VMEM((2, 8, 8, 128), F32),
            pltpu.VMEM((ROWS, WIDE), BF16),
            pltpu.VMEM((8, PAD), F32),
            pltpu.VMEM((32, 8, PAD), F32),
            pltpu.VMEM((PAD, C), F32),
            pltpu.VMEM((2, PAD), F32),
            pltpu.VMEM((32, 2, PAD), F32),
            pltpu.SemaphoreType.DMA((10,)),
            pltpu.SemaphoreType.DMA((2, 3)),
            pltpu.SemaphoreType.DMA((24,)),
            pltpu.SemaphoreType.DMA((24,)),
        ],
        compiler_params=pltpu.CompilerParams(
            collective_id=0, has_side_effects=True, vmem_limit_bytes=62 * 2**20
        ),
        name="whole",
    )(*args)


def place_kernel(out_in, gw_in, vec_ref, out_ref, gwa_ref, gwb_ref, ta_ref, tb_ref, ga_ref, gb_ref):
    out_ref[...] = out_in[...]
    gwa_ref[...] = gw_in[0:OWN]
    gwb_ref[...] = gw_in[OWN : 2 * OWN]
    ta_ref[...] = vec_ref[0:3]
    tb_ref[...] = vec_ref[4:7]
    ga_ref[...] = vec_ref[3]
    gb_ref[...] = vec_ref[7]


def placed_outputs(out, gw, vec):
    vmem = pl.BlockSpec(memory_space=pltpu.VMEM)
    return pl.pallas_call(
        place_kernel,
        out_shape=(
            jax.ShapeDtypeStruct((L, C), BF16),
            jax.ShapeDtypeStruct((OWN, C), F32),
            jax.ShapeDtypeStruct((OWN, C), F32),
            jax.ShapeDtypeStruct((3, C), F32),
            jax.ShapeDtypeStruct((3, C), F32),
            jax.ShapeDtypeStruct((C,), F32),
            jax.ShapeDtypeStruct((C,), F32),
        ),
        in_specs=[vmem] * 3,
        out_specs=(vmem,) * 7,
        compiler_params=pltpu.CompilerParams(vmem_limit_bytes=62 * 2**20),
        name="place",
    )(out, gw, vec)


def shards(tokens, embed, k1, g1, w1, k2, g2, w2, cotangent):
    out, gw, vec = whole(tokens, embed, k1, g1, w1, k2, g2, w2, cotangent.reshape(L, C))
    out, gwa, gwb, ta, tb, ga, gb = placed_outputs(out, gw, vec)
    return (out[None, None], gwa, gwb, ta, tb, ga, gb)


def solution(mesh):
    placed = (
        P("rep", "pos"),
        P(),
        P(),
        P(),
        P("pos", None),
        P(),
        P(),
        P("pos", None),
        P("rep", "strand", "pos", None),
    )
    return jax.shard_map(
        shards,
        mesh=mesh,
        in_specs=placed,
        out_specs=(
            P("rep", "strand", "pos", None),
            P("pos", None),
            P("pos", None),
            P(),
            P(),
            P(),
            P(),
        ),
        check_vma=False,
    )
```

```python
import functools

import jax
import jax.numpy as jnp
from jax import lax
from jax.experimental import pallas as pl
from jax.experimental.pallas import tpu as pltpu
from jax.sharding import PartitionSpec as P

MESH = pl.DeviceIdType.MESH
HIGH = lax.Precision.HIGHEST
F32 = jnp.float32
BF16 = jnp.bfloat16
C = 1536
L = 256
FIRST_DILATE = 32
SECOND_DILATE = 64
EPS = 1e-05
CODES = 96
PAD = 128
ROWS = 256
WIDE = 2048
BLOCK = 256
BLOCKS = C // BLOCK
OWN = 48
GELU_A = 0.7978845608028654
GELU_B = 0.044715


def coords():
    pos = lax.axis_index("pos")
    strand = lax.axis_index("strand")
    rep = lax.axis_index("rep")
    high, core = lax.div(rep, 2), lax.rem(rep, 2)
    return lax.div(pos, 8), lax.rem(pos, 8), high * 2 + strand, core


PLANE = [(a, b) for a in range(4) for b in range(8) if a or b]
SQUARE = [(a, b) for a in range(4) for b in range(4) if a or b]


def wrapped(at, size):
    moved = [at] + [at + d for d in range(1, size)]
    return [at] + [jnp.where(m >= size, m - size, m) for m in moved[1:]]


class Net:
    def __init__(self, send, recv):
        self.send, self.recv, self.used = send, recv, 0

    def take(self, count):
        first = self.used
        self.used += count
        return first

    def copy(self, src, dst, to, sem):
        return pltpu.make_async_remote_copy(
            src_ref=src,
            dst_ref=dst,
            send_sem=self.send.at[sem],
            recv_sem=self.recv.at[sem],
            device_id=to,
            device_id_type=MESH,
        )

    def start(self, items, total):
        sem = self.take(1)
        for src, dst, to in items:
            self.copy(src, dst, to, sem).start()
        return self.copy(total, total, items[0][2], sem)


def share_out(onehot, value, parts):
    total = None
    for _ in range(parts):
        part = value.astype(BF16)
        value = value - part.astype(F32)
        term = dot(onehot.astype(BF16), part)
        total = term if total is None else total + term
    return total


def lanes(index, width):
    return pl.ds(pl.multiple_of(index * width, 128), width)


def rows(index, height):
    return pl.ds(pl.multiple_of(index * height, 8), height)


def dot(a, b, precision=None):
    return lax.dot_general(
        a, b, (((1,), (0,)), ((), ())), preferred_element_type=F32, precision=precision
    )


def dot_nt(a, b):
    return lax.dot_general(a, b, (((1,), (1,)), ((), ())), preferred_element_type=F32)


def split(value):
    high = value.astype(BF16)
    return high, (value - high.astype(F32)).astype(BF16)


def gelu_parts(pre):
    square = pre * pre
    th = jnp.tanh(pre * (GELU_A + (GELU_A * GELU_B) * square))
    half = 0.5 + 0.5 * th
    bend = pre * (GELU_A + (3.0 * GELU_A * GELU_B) * square)
    return pre * half, half * (1.0 + (1.0 - th) * bend)


def code_bases(code):
    inner, left = code < 64, code < 80
    one = jnp.where(inner, code // 16, jnp.where(left, -1, (code - 80) // 4))
    two = jnp.where(inner, (code // 4) % 4, jnp.where(left, (code - 64) // 4, code % 4))
    three = jnp.where(inner | left, code % 4, -1)
    return one, two, three


def code_onehot(code, column):
    one, two, three = code_bases(code)
    hit = (column == one) & (one >= 0)
    hit = hit | (column == 4 + two) | ((column == 8 + three) & (three >= 0))
    return jnp.where(hit & (code < CODES), 1.0, 0.0)


def iota(shape, axis):
    return lax.broadcasted_iota(jnp.int32, shape, axis)


def tap_rows(taps, table):
    return jnp.concatenate(
        [taps[0] * table[0:80], taps[1] * table[0:96], taps[2] * table[0:64], taps[2] * table[80:96]],
        axis=0,
    )


def code_of(left, middle, right):
    code = jnp.where(
        left == 4,
        64 + 4 * middle + right,
        jnp.where(right == 4, 80 + 4 * left + middle, 16 * left + 4 * middle + right),
    )
    return jnp.where(middle == 4, -1, code)


def tap_index(codes):
    first, second, third = codes
    second = jnp.where(second < 0, -1, 80 + second)
    third = jnp.where(third < 0, -1, jnp.where(third < 64, 176 + third, 160 + third))
    return first, second, third


def whole_kernel(
    tok_in,
    emb_in,
    k1_in,
    g1_in,
    w1_in,
    k2_in,
    g2_in,
    w2_in,
    cot_in,
    out_out,
    gw_ref,
    vec_ref,
    tok,
    emb16,
    k1_ref,
    g1_ref,
    k2_ref,
    g2_ref,
    wpad1,
    wpad2,
    cot,
    tsend,
    trecv,
    qsend,
    qrecv,
    qown,
    qparts,
    qfull,
    aown,
    ppart,
    py,
    psum,
    pz,
    pmid,
    pbuf,
    table,
    table_slope,
    table_v,
    hot,
    hot_t,
    wide_a,
    wide_b,
    mid_t,
    cots,
    mids,
    fins,
    preu,
    slope,
    acc,
    acc2,
    out_buf,
    xbuf,
    core_send,
    from_core,
    chip_low,
    xin,
    zin,
    full,
    pack,
    packs,
    fbuf,
    pack2,
    packs2,
    lsem,
    tsem,
    send,
    recv,
):
    y, z, x, c = coords()
    pos = lax.axis_index("pos")
    strand = lax.axis_index("strand")
    rep = lax.axis_index("rep")
    ys, zs, xs = wrapped(y, 4), wrapped(z, 8), wrapped(x, 4)
    zq = lax.rem(z, 4)
    zqs = wrapped(zq, 4)
    xsr = [(lax.rem(v, 2), lax.div(v, 2) * 2 + c) for v in xs]
    xsr[0] = (strand, rep)

    def peer_at(a, b, e):
        return {"pos": ys[a] * 8 + zs[b], "strand": xsr[e][0], "rep": xsr[e][1]}

    plane_ids = [peer_at(a, b, 0) for a, b in PLANE]
    square_ids = [peer_at(b, 0, a) for a, b in SQUARE]
    y_ids = [peer_at(d, 0, 0) for d in range(4)]
    z_ids = [peer_at(0, d, 0) for d in range(8)]
    hz_ids = [{"pos": pos - zq + zqs[d], "strand": strand, "rep": rep} for d in range(4)]
    core_id = {"pos": pos, "strand": strand, "rep": rep + 1 - 2 * c}
    frame = jnp.where(strand == 1, 31 - pos, pos)
    targets = [(frame + d + 32) % 32 for d in (-1, 0, 1)]
    net = Net(send, recv)

    wpad1[OWN:PAD] = jnp.zeros((PAD - OWN, C), BF16)
    wpad2[OWN:PAD] = jnp.zeros((PAD - OWN, C), BF16)
    loads = [
        pltpu.make_async_copy(src, dst, lsem.at[i])
        for i, (src, dst) in enumerate(
            (
                (emb_in, emb16),
                (k1_in, k1_ref),
                (g1_in, g1_ref),
                (w1_in, wpad1.at[0:OWN]),
                (k2_in, k2_ref),
                (g2_in, g2_ref),
                (tok_in, tok),
                (w2_in, wpad2.at[0:OWN]),
                (cot_in, cot),
            )
        )
    ]
    for load in loads:
        load.start()

    barrier = pltpu.get_barrier_semaphore()
    peers = plane_ids + [i for i, (a, b) in zip(square_ids, SQUARE) if a] + [core_id]
    for peer in peers:
        pl.semaphore_signal(barrier, inc=1, device_id=peer, device_id_type=MESH)

    for load in loads[:6]:
        load.wait()
    emb = emb16[...].astype(F32)
    k1, k2 = k1_ref[...], k2_ref[...]
    g1, g2 = g1_ref[...].reshape(1, C), g2_ref[...].reshape(1, C)
    packed = jnp.concatenate([emb, k1, g1, k2, g2, jnp.zeros((4, C), F32)], axis=0)
    vec = pltpu.roll(packed, lax.rem(C - pos * OWN, C), 1)[:, 0:PAD]
    vec = jnp.where(iota((16, PAD), 1) < OWN, vec, 0.0)
    e_own, g1_own, g2_own = vec[0:4], vec[7:8], vec[11:12]
    taps = [vec[8 + k : 9 + k] for k in range(3)]
    te_own = jnp.concatenate(
        [vec[4 + k : 5 + k] * e_own for k in range(3)] + [jnp.zeros((4, PAD), F32)], axis=0
    )
    high, low = split(g1_own * te_own)
    part = dot(jnp.concatenate([high, low], axis=0), wpad1[...])
    part = part[0:16] + part[16:32]
    qsend[...] = jnp.zeros_like(qsend)
    for i in range(32):
        qsend[i, :, 0:OWN] = part[0:8, OWN * i : OWN * i + OWN]
        qsend[i, :, 64 : 64 + OWN] = part[8:16, OWN * i : OWN * i + OWN]
    qrecv[pos] = qsend[pos]

    pl.semaphore_wait(barrier, len(peers))

    q_copies = net.start(
        [
            (qsend.at[to["pos"]], qrecv.at[pos], to)
            for to in plane_ids
        ],
        qrecv.at[0:31],
    )

    loads[6].wait()
    tokens = jnp.broadcast_to(tok[...], (8, L)).astype(F32)
    flip = jnp.where(iota((L, L), 0) + iota((L, L), 1) == L - 1, 1.0, 0.0)
    turned = 3.0 - dot(tokens, flip)
    tsend[...] = jnp.where(strand == 1, turned, tokens).astype(jnp.int32)

    def token_copy(j):
        return pltpu.make_async_remote_copy(
            src_ref=tsend,
            dst_ref=trecv.at[2 - j],
            send_sem=tsem.at[0, j],
            recv_sem=tsem.at[1, j],
            device_id={"pos": targets[j], "strand": strand, "rep": rep},
            device_id_type=MESH,
        )

    for j in range(3):
        @pl.when(targets[j] != pos)
        def _():
            token_copy(j).start()

        @pl.when(targets[j] == pos)
        def _():
            trecv[2 - j] = tsend[...]

    te = jnp.concatenate([k1[k : k + 1] * emb for k in range(3)] + [jnp.zeros((4, C), F32)], axis=0)
    hot_code = code_onehot(iota((PAD, 16), 0), iota((PAD, 16), 1))
    conv = share_out(hot_code, te, 3)
    inv_a = lax.rsqrt(jnp.mean(conv * conv, axis=-1, keepdims=True) + EPS)

    mirror = jnp.where(
        iota((BLOCK, BLOCK), 0) + iota((BLOCK, BLOCK), 1) == BLOCK - 1, 1.0, 0.0
    ).astype(BF16)
    loads[7].wait()
    loads[8].wait()

    def turn_cot(b, carry):
        here = lanes(b, BLOCK)
        there = lanes(BLOCKS - 1 - b, BLOCK)
        cots[0:L, here] = cot[:, here]
        cots[L : 2 * L, here] = dot(cot[:, there], mirror).astype(BF16)
        return carry

    lax.fori_loop(0, BLOCKS, turn_cot, 0)

    q_copies.wait()
    total = qrecv[0]
    for i in range(1, 32):
        total = total + qrecv[i]
    qown[...] = total
    qparts[pos] = total

    q_two = jnp.concatenate([total, pltpu.roll(total, 64, 1)], axis=0)
    q_two = jnp.where(iota((16, PAD), 1) < OWN, q_two, 0.0)
    pre_own = inv_a * share_out(hot_code, q_two, 3)
    act, slope_own = gelu_parts(pre_own)
    pads = jnp.zeros((4, PAD), F32)
    center = share_out(hot_code, jnp.concatenate([pads, e_own, pads, pads], axis=0), 1)
    m_own = jnp.where(iota((PAD, PAD), 0) < CODES, center + act, 0.0)
    m_own = m_own.astype(BF16).astype(F32)
    b_own = tap_rows(taps, m_own)
    a_own = g2_own * b_own
    aown[...] = a_own
    high, low = split(aown[rows(c, 128)])
    mine = lanes(x, 384)
    w2 = wpad2[:, mine]
    ppart[...] = dot(high, w2) + dot(low, w2)
    p_copies = net.start(
        [(ppart.at[rows(ys[d], 32)], py.at[d - 1], y_ids[d]) for d in range(1, 4)], py
    )
    q_copies = net.start(
        [(qown, qparts.at[pos], to) for to in plane_ids], qparts.at[0:31]
    )

    for j in range(3):
        @pl.when(targets[j] != pos)
        def _():
            token_copy(j).wait()
    joined = jnp.concatenate([trecv[0], trecv[1], trecv[2]], axis=1)
    place = (pos - 1) * L + iota((8, 3 * L), 1)
    ext = jnp.where((place >= 0) & (place < 32 * L), joined, 4)
    left = pltpu.roll(ext, FIRST_DILATE, 1)
    right = pltpu.roll(ext, 3 * L - FIRST_DILATE, 1)

    def other(base):
        return jnp.where(base == 4, 4, 3 - base)

    start = L - SECOND_DILATE
    code_a = pltpu.roll(code_of(left, ext, right), 3 * L - start, 1)[:, 0:384]
    code_b = pltpu.roll(code_of(other(right), other(ext), other(left)), 3 * L - start, 1)[:, 0:384]

    def shifts(code):
        return [code[:, 0:L]] + [
            pltpu.roll(code, 384 - s, 1)[:, 0:L] for s in (SECOND_DILATE, 2 * SECOND_DILATE)
        ]

    three_a = shifts(code_a)
    three_b = shifts(code_b)[::-1]
    index = [jnp.concatenate([a, b], axis=1) for a, b in zip(tap_index(three_a), tap_index(three_b))]
    line = iota((ROWS, 2 * L), 0)
    hit = (line == index[0][0:1]) | (line == index[1][0:1]) | (line == index[2][0:1])
    hot_t[...] = jnp.where(hit, 1.0, 0.0).astype(BF16)
    mid_t[...] = jnp.where(
        iota((PAD, 2 * L), 0) == jnp.concatenate([three_a[1], three_b[1]], axis=1)[0:1], 1.0, 0.0
    ).astype(BF16)

    def column(row):
        return jnp.transpose(row.astype(F32))[:, 0:1].astype(jnp.int32)

    p_copies.wait()
    psum[...] = ppart[rows(y, 32)] + py[0] + py[1] + py[2]
    p_copies = net.start(
        [(psum.at[rows(zqs[d % 4], 8)], pz.at[z], z_ids[d]) for d in range(1, 8)], pz.at[0:7]
    )
    pz[z] = psum[rows(zq, 8)]

    columns = [column(row) for row in index]
    line = iota((2 * L, ROWS), 1)
    hit = (line == columns[0]) | (line == columns[1]) | (line == columns[2])
    hot[...] = jnp.where(hit, 1.0, 0.0).astype(BF16)
    line = iota((384, PAD), 1)
    wide_a[...] = jnp.where(line == column(code_a), 1.0, 0.0).astype(BF16)
    wide_b[...] = jnp.where(line == column(code_b), 1.0, 0.0).astype(BF16)

    q_copies.wait()
    for i in range(32):
        tile = qparts[i]
        qfull[0:8, OWN * i : OWN * i + OWN] = tile[:, 0:OWN]
        qfull[8:16, OWN * i : OWN * i + OWN] = tile[:, 64 : 64 + OWN]

    table_v[...] = jnp.zeros_like(table_v)
    pads = jnp.zeros((4, BLOCK), F32)
    sums = jnp.zeros((PAD, 128), F32)
    for b in range(BLOCKS):
        if b == BLOCKS // 2:
            p_copies.wait()
            total = pz[0]
            for i in range(1, 8):
                total = total + pz[i]
            pmid[zq] = total
            p_copies = net.start(
                [(pmid.at[zq], pmid.at[zq], hz_ids[d]) for d in range(1, 4)],
                pmid.at[0:3],
            )
        here = slice(BLOCK * b, BLOCK * b + BLOCK)
        pre = inv_a * share_out(hot_code, qfull[:, here], 3)
        act, grad = gelu_parts(pre)
        center = share_out(
            hot_code, jnp.concatenate([pads, emb[:, here], pads, pads], axis=0), 1
        )
        live = iota((PAD, BLOCK), 0) < CODES
        table[:, here] = jnp.where(live, center + act, 0.0).astype(BF16)
        sv = jnp.where(live, grad * (0.5 * dot(mid_t[...], cots[:, here])), 0.0)
        table_v[:, here] = inv_a * sv
        prod = sv * pre
        sums = sums + prod[:, 0:128] + prod[:, 128:256]

    p_copies.wait()
    quarter = pl.ds(pl.multiple_of(c * 128 + y * 32, 32), 32)
    pbuf[quarter, mine] = jnp.concatenate([pmid[i] for i in range(4)], axis=0).astype(BF16)
    block = pbuf.at[quarter, mine]
    p_copies = net.start(
        [(block, block, to) for to in square_ids], pbuf.at[0:240, 0:768]
    )

    hot_ct = code_onehot(iota((16, PAD), 1), iota((16, PAD), 0))
    fv = share_out(hot_ct, table_v[...], 2)
    mean_v = jnp.sum(sums, axis=1, keepdims=True) * (1.0 / C)
    hot_gram = code_onehot(iota((PAD, PAD), 0), iota((PAD, PAD), 1) - 96)
    gram_v = share_out(hot_ct, (inv_a * inv_a * mean_v) * hot_gram, 2)
    xbuf[:, C + ROWS : WIDE] = jnp.zeros((ROWS, WIDE - C - ROWS), F32)
    xbuf[0:16, C + ROWS : C + ROWS + PAD] = gram_v
    for i in range(16):
        xbuf[16 * i : 16 * i + 16, C + ROWS : C + ROWS + 96] = fv[:, 96 * i : 96 * i + 96]

    acc[...] = jnp.zeros_like(acc)
    acc2[...] = jnp.zeros_like(acc2)

    def first_pass(b, carry):
        here = lanes(b, BLOCK)
        m = table[:, here]
        taps2 = k2_ref[:, here]
        for n, (wide, order) in enumerate(((wide_a, (0, 1, 2)), (wide_b, (2, 1, 0)))):
            mid = dot(wide[...], m)
            conv = (
                taps2[order[0] : order[0] + 1] * mid[0:L]
                + taps2[order[1] : order[1] + 1] * mid[64 : 64 + L]
                + taps2[order[2] : order[2] + 1] * mid[128 : 128 + L]
            )
            square = conv * conv
            acc[n * L : n * L + L] += square[:, 0:128] + square[:, 128:256]
            mids[n * L : n * L + L, here] = mid[64 : 64 + L].astype(BF16)
        return carry

    lax.fori_loop(0, BLOCKS, first_pass, 0)
    acc[...] = jnp.broadcast_to(
        lax.rsqrt(jnp.sum(acc[...], axis=1, keepdims=True) * (1.0 / C) + EPS), (2 * L, 128)
    )

    half = rows(c, 128)
    p_copies.wait()
    net.start([(pbuf.at[half], pbuf.at[half], core_id)], pbuf.at[half]).wait()

    base = net.take(2)
    away = rows(1 - c, 128)

    def core_copy(b):
        here = lanes(b, BLOCK)
        return net.copy(core_send.at[:, here], from_core.at[:, here], core_id, base + b // 4)

    def second_pass(b, carry):
        here = lanes(b, BLOCK)
        preu[...] = dot(hot[...], pbuf[:, here])

        def chunk(r, carry):
            some = rows(r, 64)
            inv = acc[some]
            kept = acc2[some]
            for part in (0, 128):
                cut = pl.ds(pl.multiple_of(b * BLOCK + part, 128), 128)
                pre = inv * preu[some, part : part + 128]
                act, grad = gelu_parts(pre)
                fins[some, cut] = (mids[some, cut].astype(F32) + act).astype(BF16)
                sl = cots[some, cut].astype(F32) * grad
                kept = kept + sl * pre
                slope[some, part : part + 128] = (inv * sl).astype(BF16)
            acc2[some] = kept
            return carry

        lax.fori_loop(0, 8, chunk, 0)
        xbuf[:, here] = 0.5 * dot(hot_t[...], slope[...])
        core_send[:, here] = xbuf[away, here].astype(BF16)
        core_copy(b).start()
        return carry

    third = pl.ds(pl.multiple_of(c * 128 + x * 32, 32), 32)

    def chip_sum(first, last):
        xbuf[half, first:last] = xbuf[half, first:last] + from_core[:, first:last].astype(F32)
        chip_low[:, first:last] = xbuf[half, first:last].astype(BF16)

    def strip(h, at):
        return pl.ds(pl.multiple_of(1024 * h + at * 256, 128), 256)

    def square_scatter(h):
        items = []
        for j, (a, b) in enumerate(SQUARE):
            block = chip_low.at[rows(xs[a], 32), strip(h, ys[b])]
            items.append((block, xin.at[h, j], square_ids[j]))
        return net.start(items, xin.at[h])

    def line_all(h, copies):
        copies.wait()
        total = xbuf[third, strip(h, y)]
        for j in range(15):
            total = total + xin[h, j].astype(F32)
        zin[h, z] = total.astype(BF16)
        block = zin.at[h, z]
        return net.start([(block, block, to) for to in z_ids[1:]], zin.at[h, 0:7])

    def square_gather(h, copies):
        copies.wait()
        total = zin[h, 0].astype(F32)
        for d in range(1, 8):
            total = total + zin[h, d].astype(F32)
        full[third, strip(h, y)] = total.astype(BF16)
        block = full.at[third, strip(h, y)]
        items = [(block, block, to) for to in square_ids]
        return net.start(items, full.at[0:240, 0:512])

    def share(h, copies):
        copies.wait()
        block = full.at[half, 1024 * h : 1024 * h + 1024]
        return net.start([(block, block, core_id)], block)

    lax.fori_loop(0, 4, second_pass, 0)
    net.copy(core_send.at[:, 0:1024], from_core.at[:, 0:1024], core_id, base).wait()
    chip_sum(0, 1024)
    scatter_0 = square_scatter(0)
    lax.fori_loop(4, BLOCKS, second_pass, 0)

    inv = acc[:, 0:1]
    weight = (0.5 / C) * inv * inv * jnp.sum(acc2[...], axis=1, keepdims=True)
    xbuf[:, C : C + ROWS] = dot(hot_t[...], (weight * hot[...].astype(F32)).astype(BF16))
    core_send[:, C:WIDE] = xbuf[away, C:WIDE].astype(BF16)
    net.copy(core_send.at[:, C:WIDE], from_core.at[:, C:WIDE], core_id, base + 1).start()
    net.copy(core_send.at[:, 1024:WIDE], from_core.at[:, 1024:WIDE], core_id, base + 1).wait()
    chip_sum(1024, WIDE)
    scatter_1 = square_scatter(1)
    line_0 = line_all(0, scatter_0)

    def third_pass(b, carry):
        here = lanes(b, BLOCK)
        there = lanes(BLOCKS - 1 - b, BLOCK)
        far = dot(fins[L : 2 * L, there], mirror)
        out_buf[:, here] = (0.5 * (fins[0:L, here].astype(F32) + far)).astype(BF16)
        return carry

    lax.fori_loop(0, BLOCKS, third_pass, 0)
    store = pltpu.make_async_copy(out_buf, out_out, lsem.at[9])
    store.start()

    line_1 = line_all(1, scatter_1)
    back_0 = square_gather(0, line_0)
    back_1 = square_gather(1, line_1)
    shares = share(0, back_0)
    turned_high, turned_low = split(jnp.transpose(a_own))
    both = jnp.concatenate([turned_high[0:OWN], turned_low[0:OWN]], axis=0)

    def grad_b(b):
        grad = dot(both, full[:, b : b + 512])
        gw_ref[OWN : 2 * OWN, b : b + 512] = grad[0:OWN] + grad[OWN : 2 * OWN]

    shares.wait()
    ew = dot_nt(full[:, 0:1024], wpad2[:, 0:1024])
    shares = share(1, back_1)
    grad_b(0)
    grad_b(512)
    fbuf[...] = jnp.zeros_like(fbuf)
    shares.wait()

    ew = ew + dot_nt(full[:, 1024:C], wpad2[:, 1024:C])
    high, low = split(b_own)
    gram = full[:, C : C + ROWS]
    d = g2_own * ew - (dot(gram, high) + dot(gram, low))

    def total_rows(value):
        return jnp.sum(value, axis=0, keepdims=True)

    taps_b = [
        total_rows(m_own[0:80] * d[0:80]),
        total_rows(m_own[0:96] * d[80:176]),
        total_rows(m_own[0:64] * d[176:240]) + total_rows(m_own[80:96] * d[240:256]),
    ]
    gain_b = total_rows(b_own * ew)
    up = taps[1] * d[80:176] + jnp.concatenate(
        [taps[0] * d[0:64] + taps[2] * d[176:240], taps[0] * d[64:80], taps[2] * d[240:256]],
        axis=0,
    )
    s = slope_own[0:CODES] * up
    inv = inv_a[0:CODES]
    mean_s = jnp.sum(s * pre_own[0:CODES], axis=1, keepdims=True) * (1.0 / C)
    narrow = hot_ct[:, 0:CODES]
    hot_far = code_onehot(iota((CODES, PAD), 0), iota((CODES, PAD), 1) - OWN)
    extra = C + ROWS
    fv = full[pl.ds(pl.multiple_of((pos // 2) * 16, 16), 16), extra : extra + PAD].astype(F32)
    fv = jnp.where(pos % 2 == 1, pltpu.roll(fv, PAD - OWN, 1), fv)
    fv = jnp.where(iota((16, PAD), 1) < OWN, fv, 0.0)
    own_rows = fv + share_out(narrow, inv * s, 2)
    f_rows = jnp.where(iota((16, PAD), 0) < 12, own_rows, 0.0)
    vec_rows = jnp.concatenate([jnp.zeros((12, PAD), F32)] + taps_b + [gain_b], axis=0)
    packet = f_rows + vec_rows + share_out(narrow, (inv * inv * mean_s) * hot_far, 2)
    pack[...] = packet[0:8] + pltpu.roll(packet[8:16], 64, 1)
    packs[pos] = pack[...]
    copies = net.start([(pack, packs.at[pos], to) for to in plane_ids], packs.at[0:31])

    grad_b(1024)
    copies.wait()
    total = jnp.zeros((8, PAD), F32)
    for i in range(32):
        tile = packs[i]
        fbuf[0:8, OWN * i : OWN * i + OWN] = tile[:, 0:OWN]
        fbuf[8:16, OWN * i : OWN * i + OWN] = tile[:, 64 : 64 + OWN]
        total = total + tile
    far = jnp.concatenate([total, pltpu.roll(total, 64, 1)], axis=0)
    far = far + pltpu.roll(full[0:16, extra : extra + PAD].astype(F32), PAD - OWN, 1)
    far = jnp.where((iota((16, PAD), 1) >= OWN) & (iota((16, PAD), 1) < OWN + 12), far, 0.0)
    high, low = split(fbuf[0:16])
    fw = dot_nt(jnp.concatenate([high, low], axis=0), wpad1[...])
    fw = fw[0:16] + fw[16:32]
    spread = jnp.concatenate(
        [jnp.zeros((OWN, PAD), F32), te_own, jnp.zeros((64, PAD), F32)], axis=0
    )
    da = g1_own * fw - dot(far, spread, HIGH)
    rows_a = [total_rows(e_own * da[4 * k : 4 * k + 4]) for k in range(3)]
    rows_a = rows_a + [total_rows(te_own * fw)]
    pack2[...] = jnp.concatenate(
        [
            rows_a[0] + pltpu.roll(rows_a[1], 64, 1),
            rows_a[2] + pltpu.roll(rows_a[3], 64, 1),
        ],
        axis=0,
    )
    packs2[pos] = pack2[...]
    copies = net.start(
        [(pack2, packs2.at[pos], to) for to in plane_ids], packs2.at[0:31]
    )

    wide = jnp.concatenate([g1_own * te_own, jnp.zeros((PAD - 16, PAD), F32)], axis=0)
    wide_high, wide_low = split(jnp.transpose(wide)[0:OWN])
    wide = jnp.concatenate([wide_high, wide_low], axis=0)
    for b in range(0, C, 512):
        f_high, f_low = split(fbuf[:, b : b + 512])
        grad = dot(wide, f_high)
        gw_ref[0:OWN, b : b + 512] = grad[0:OWN] + grad[OWN : 2 * OWN] + dot(wide_high, f_low)
    vec_ref[4:8, :] = fbuf[12:16, :]
    copies.wait()
    for i in range(32):
        tile = packs2[i]
        here = slice(OWN * i, OWN * i + OWN)
        vec_ref[0:1, here] = tile[0:1, 0:OWN]
        vec_ref[1:2, here] = tile[0:1, 64 : 64 + OWN]
        vec_ref[2:3, here] = tile[1:2, 0:OWN]
        vec_ref[3:4, here] = tile[1:2, 64 : 64 + OWN]
    store.wait()


def whole(*args):
    vmem = pl.BlockSpec(memory_space=pltpu.VMEM)
    hbm = pl.BlockSpec(memory_space=pltpu.HBM)
    anywhere = pl.BlockSpec(memory_space=pl.ANY)
    return pl.pallas_call(
        whole_kernel,
        out_shape=(
            jax.ShapeDtypeStruct((L, C), BF16),
            jax.ShapeDtypeStruct((2 * OWN, C), F32),
            jax.ShapeDtypeStruct((8, C), F32),
        ),
        in_specs=[hbm] * 9,
        out_specs=(anywhere, vmem, vmem),
        scratch_shapes=[
            pltpu.VMEM((1, L), jnp.int32),
            pltpu.VMEM((4, C), BF16),
            pltpu.VMEM((3, C), F32),
            pltpu.VMEM((C,), F32),
            pltpu.VMEM((3, C), F32),
            pltpu.VMEM((C,), F32),
            pltpu.VMEM((PAD, C), BF16),
            pltpu.VMEM((PAD, C), BF16),
            pltpu.VMEM((L, C), BF16),
            pltpu.VMEM((8, L), jnp.int32),
            pltpu.VMEM((3, 8, L), jnp.int32),
            pltpu.VMEM((32, 8, PAD), F32),
            pltpu.VMEM((32, 8, PAD), F32),
            pltpu.VMEM((8, PAD), F32),
            pltpu.VMEM((32, 8, PAD), F32),
            pltpu.VMEM((16, C), F32),
            pltpu.VMEM((ROWS, PAD), F32),
            pltpu.VMEM((128, 384), F32),
            pltpu.VMEM((3, 32, 384), F32),
            pltpu.VMEM((32, 384), F32),
            pltpu.VMEM((8, 8, 384), F32),
            pltpu.VMEM((4, 8, 384), F32),
            pltpu.VMEM((ROWS, C), BF16),
            pltpu.VMEM((PAD, C), BF16),
            pltpu.VMEM((8, PAD), F32),
            pltpu.VMEM((PAD, C), F32),
            pltpu.VMEM((2 * L, ROWS), BF16),
            pltpu.VMEM((ROWS, 2 * L), BF16),
            pltpu.VMEM((384, PAD), BF16),
            pltpu.VMEM((384, PAD), BF16),
            pltpu.VMEM((PAD, 2 * L), BF16),
            pltpu.VMEM((2 * L, C), BF16),
            pltpu.VMEM((2 * L, C), BF16),
            pltpu.VMEM((2 * L, C), BF16),
            pltpu.VMEM((2 * L, BLOCK), F32),
            pltpu.VMEM((2 * L, BLOCK), BF16),
            pltpu.VMEM((2 * L, 128), F32),
            pltpu.VMEM((2 * L, 128), F32),
            pltpu.VMEM((L, C), BF16),
            pltpu.VMEM((ROWS, WIDE), F32),
            pltpu.VMEM((128, WIDE), BF16),
            pltpu.VMEM((128, WIDE), BF16),
            pltpu.VMEM((128, WIDE), BF16),
            pltpu.VMEM((2, 15, 32, 256), BF16),
            pltpu.VMEM((2, 8, 32, 256), BF16),
            pltpu.VMEM((ROWS, WIDE), BF16),
            pltpu.VMEM((8, PAD), F32),
            pltpu.VMEM((32, 8, PAD), F32),
            pltpu.VMEM((PAD, C), F32),
            pltpu.VMEM((2, PAD), F32),
            pltpu.VMEM((32, 2, PAD), F32),
            pltpu.SemaphoreType.DMA((10,)),
            pltpu.SemaphoreType.DMA((2, 3)),
            pltpu.SemaphoreType.DMA((24,)),
            pltpu.SemaphoreType.DMA((24,)),
        ],
        compiler_params=pltpu.CompilerParams(
            collective_id=0, has_side_effects=True, vmem_limit_bytes=62 * 2**20
        ),
        name="whole",
    )(*args)


def place_kernel(out_in, gw_in, vec_ref, out_ref, gwa_ref, gwb_ref, ta_ref, tb_ref, ga_ref, gb_ref):
    out_ref[...] = out_in[...]
    gwa_ref[...] = gw_in[0:OWN]
    gwb_ref[...] = gw_in[OWN : 2 * OWN]
    ta_ref[...] = vec_ref[0:3]
    tb_ref[...] = vec_ref[4:7]
    ga_ref[...] = vec_ref[3]
    gb_ref[...] = vec_ref[7]


def placed_outputs(out, gw, vec):
    vmem = pl.BlockSpec(memory_space=pltpu.VMEM)
    return pl.pallas_call(
        place_kernel,
        out_shape=(
            jax.ShapeDtypeStruct((L, C), BF16),
            jax.ShapeDtypeStruct((OWN, C), F32),
            jax.ShapeDtypeStruct((OWN, C), F32),
            jax.ShapeDtypeStruct((3, C), F32),
            jax.ShapeDtypeStruct((3, C), F32),
            jax.ShapeDtypeStruct((C,), F32),
            jax.ShapeDtypeStruct((C,), F32),
        ),
        in_specs=[vmem] * 3,
        out_specs=(vmem,) * 7,
        compiler_params=pltpu.CompilerParams(vmem_limit_bytes=62 * 2**20),
        name="place",
    )(out, gw, vec)


def shards(tokens, embed, k1, g1, w1, k2, g2, w2, cotangent):
    out, gw, vec = whole(tokens, embed, k1, g1, w1, k2, g2, w2, cotangent.reshape(L, C))
    out, gwa, gwb, ta, tb, ga, gb = placed_outputs(out, gw, vec)
    return (out[None, None], gwa, gwb, ta, tb, ga, gb)


def solution(mesh):
    placed = (
        P("rep", "pos"),
        P(),
        P(),
        P(),
        P("pos", None),
        P(),
        P(),
        P("pos", None),
        P("rep", "strand", "pos", None),
    )
    return jax.shard_map(
        shards,
        mesh=mesh,
        in_specs=placed,
        out_specs=(
            P("rep", "strand", "pos", None),
            P("pos", None),
            P("pos", None),
            P(),
            P(),
            P(),
            P(),
        ),
        check_vma=False,
    )
```

```python
import functools

import jax
import jax.numpy as jnp
from jax import lax
from jax.experimental import pallas as pl
from jax.experimental.pallas import tpu as pltpu
from jax.sharding import PartitionSpec as P

MESH = pl.DeviceIdType.MESH
HIGH = lax.Precision.HIGHEST
F32 = jnp.float32
BF16 = jnp.bfloat16
C = 1536
L = 256
FIRST_DILATE = 32
SECOND_DILATE = 64
EPS = 1e-05
CODES = 96
PAD = 128
ROWS = 256
WIDE = 2048
BLOCK = 256
BLOCKS = C // BLOCK
OWN = 48
GELU_A = 0.7978845608028654
GELU_B = 0.044715


def coords():
    pos = lax.axis_index("pos")
    strand = lax.axis_index("strand")
    rep = lax.axis_index("rep")
    high, core = lax.div(rep, 2), lax.rem(rep, 2)
    return lax.div(pos, 8), lax.rem(pos, 8), high * 2 + strand, core


PLANE = [(a, b) for a in range(4) for b in range(8) if a or b]
SQUARE = [(a, b) for a in range(4) for b in range(4) if a or b]


def wrapped(at, size):
    moved = [at] + [at + d for d in range(1, size)]
    return [at] + [jnp.where(m >= size, m - size, m) for m in moved[1:]]


class Net:
    def __init__(self, send, recv):
        self.send, self.recv, self.used = send, recv, 0

    def take(self, count):
        first = self.used
        self.used += count
        return first

    def copy(self, src, dst, to, sem):
        return pltpu.make_async_remote_copy(
            src_ref=src,
            dst_ref=dst,
            send_sem=self.send.at[sem],
            recv_sem=self.recv.at[sem],
            device_id=to,
            device_id_type=MESH,
        )

    def start(self, items, total):
        sem = self.take(1)
        for src, dst, to in items:
            self.copy(src, dst, to, sem).start()
        return self.copy(total, total, items[0][2], sem)


def share_out(onehot, value, parts):
    total = None
    for _ in range(parts):
        part = value.astype(BF16)
        value = value - part.astype(F32)
        term = dot(onehot.astype(BF16), part)
        total = term if total is None else total + term
    return total


def lanes(index, width):
    return pl.ds(pl.multiple_of(index * width, 128), width)


def rows(index, height):
    return pl.ds(pl.multiple_of(index * height, 8), height)


def dot(a, b, precision=None):
    return lax.dot_general(
        a, b, (((1,), (0,)), ((), ())), preferred_element_type=F32, precision=precision
    )


def dot_nt(a, b):
    return lax.dot_general(a, b, (((1,), (1,)), ((), ())), preferred_element_type=F32)


def split(value):
    high = value.astype(BF16)
    return high, (value - high.astype(F32)).astype(BF16)


def gelu_parts(pre):
    square = pre * pre
    th = jnp.tanh(pre * (GELU_A + (GELU_A * GELU_B) * square))
    half = 0.5 + 0.5 * th
    bend = pre * (GELU_A + (3.0 * GELU_A * GELU_B) * square)
    return pre * half, half * (1.0 + (1.0 - th) * bend)


def code_bases(code):
    inner, left = code < 64, code < 80
    one = jnp.where(inner, code // 16, jnp.where(left, -1, (code - 80) // 4))
    two = jnp.where(inner, (code // 4) % 4, jnp.where(left, (code - 64) // 4, code % 4))
    three = jnp.where(inner | left, code % 4, -1)
    return one, two, three


def code_onehot(code, column):
    one, two, three = code_bases(code)
    hit = (column == one) & (one >= 0)
    hit = hit | (column == 4 + two) | ((column == 8 + three) & (three >= 0))
    return jnp.where(hit & (code < CODES), 1.0, 0.0)


def iota(shape, axis):
    return lax.broadcasted_iota(jnp.int32, shape, axis)


def tap_rows(taps, table):
    return jnp.concatenate(
        [taps[0] * table[0:80], taps[1] * table[0:96], taps[2] * table[0:64], taps[2] * table[80:96]],
        axis=0,
    )


def code_of(left, middle, right):
    code = jnp.where(
        left == 4,
        64 + 4 * middle + right,
        jnp.where(right == 4, 80 + 4 * left + middle, 16 * left + 4 * middle + right),
    )
    return jnp.where(middle == 4, -1, code)


def tap_index(codes):
    first, second, third = codes
    second = jnp.where(second < 0, -1, 80 + second)
    third = jnp.where(third < 0, -1, jnp.where(third < 64, 176 + third, 160 + third))
    return first, second, third


def whole_kernel(
    tok_in,
    emb_in,
    k1_in,
    g1_in,
    w1_in,
    k2_in,
    g2_in,
    w2_in,
    cot_in,
    out_out,
    gw_ref,
    vec_ref,
    tok,
    emb16,
    k1_ref,
    g1_ref,
    k2_ref,
    g2_ref,
    wpad1,
    wpad2,
    cot,
    tsend,
    trecv,
    qsend,
    qrecv,
    qown,
    qparts,
    qfull,
    aown,
    ppart,
    py,
    pz,
    pbuf,
    table,
    table_slope,
    table_v,
    hot,
    hot_t,
    wide_a,
    wide_b,
    mid_t,
    cots,
    mids,
    fins,
    preu,
    slope,
    acc,
    acc2,
    out_buf,
    xbuf,
    core_send,
    from_core,
    chip_low,
    xin,
    zin,
    full,
    pack,
    packs,
    fbuf,
    pack2,
    packs2,
    lsem,
    tsem,
    send,
    recv,
):
    y, z, x, c = coords()
    pos = lax.axis_index("pos")
    strand = lax.axis_index("strand")
    rep = lax.axis_index("rep")
    ys, zs, xs = wrapped(y, 4), wrapped(z, 8), wrapped(x, 4)
    xsr = [(lax.rem(v, 2), lax.div(v, 2) * 2 + c) for v in xs]
    xsr[0] = (strand, rep)

    def peer_at(a, b, e):
        return {"pos": ys[a] * 8 + zs[b], "strand": xsr[e][0], "rep": xsr[e][1]}

    plane_ids = [peer_at(a, b, 0) for a, b in PLANE]
    square_ids = [peer_at(b, 0, a) for a, b in SQUARE]
    y_ids = [peer_at(d, 0, 0) for d in range(4)]
    z_ids = [peer_at(0, d, 0) for d in range(8)]
    core_id = {"pos": pos, "strand": strand, "rep": rep + 1 - 2 * c}
    frame = jnp.where(strand == 1, 31 - pos, pos)
    targets = [(frame + d + 32) % 32 for d in (-1, 0, 1)]
    net = Net(send, recv)

    wpad1[OWN:PAD] = jnp.zeros((PAD - OWN, C), BF16)
    wpad2[OWN:PAD] = jnp.zeros((PAD - OWN, C), BF16)
    loads = [
        pltpu.make_async_copy(src, dst, lsem.at[i])
        for i, (src, dst) in enumerate(
            (
                (emb_in, emb16),
                (k1_in, k1_ref),
                (g1_in, g1_ref),
                (w1_in, wpad1.at[0:OWN]),
                (k2_in, k2_ref),
                (g2_in, g2_ref),
                (tok_in, tok),
                (w2_in, wpad2.at[0:OWN]),
                (cot_in, cot),
            )
        )
    ]
    for load in loads:
        load.start()

    barrier = pltpu.get_barrier_semaphore()
    peers = plane_ids + [i for i, (a, b) in zip(square_ids, SQUARE) if a] + [core_id]
    for peer in peers:
        pl.semaphore_signal(barrier, inc=1, device_id=peer, device_id_type=MESH)

    for load in loads[:6]:
        load.wait()
    emb = emb16[...].astype(F32)
    k1, k2 = k1_ref[...], k2_ref[...]
    g1, g2 = g1_ref[...].reshape(1, C), g2_ref[...].reshape(1, C)
    packed = jnp.concatenate([emb, k1, g1, k2, g2, jnp.zeros((4, C), F32)], axis=0)
    vec = pltpu.roll(packed, lax.rem(C - pos * OWN, C), 1)[:, 0:PAD]
    vec = jnp.where(iota((16, PAD), 1) < OWN, vec, 0.0)
    e_own, g1_own, g2_own = vec[0:4], vec[7:8], vec[11:12]
    taps = [vec[8 + k : 9 + k] for k in range(3)]
    te_own = jnp.concatenate(
        [vec[4 + k : 5 + k] * e_own for k in range(3)] + [jnp.zeros((4, PAD), F32)], axis=0
    )
    high, low = split(g1_own * te_own)
    part = dot(jnp.concatenate([high, low], axis=0), wpad1[...])
    part = part[0:16] + part[16:32]
    qsend[...] = jnp.zeros_like(qsend)
    for i in range(32):
        qsend[i, :, 0:OWN] = part[0:8, OWN * i : OWN * i + OWN]
        qsend[i, :, 64 : 64 + OWN] = part[8:16, OWN * i : OWN * i + OWN]
    qrecv[pos] = qsend[pos]

    pl.semaphore_wait(barrier, len(peers))

    q_copies = net.start(
        [
            (qsend.at[to["pos"]], qrecv.at[pos], to)
            for to in plane_ids
        ],
        qrecv.at[0:31],
    )

    loads[6].wait()
    tokens = jnp.broadcast_to(tok[...], (8, L)).astype(F32)
    flip = jnp.where(iota((L, L), 0) + iota((L, L), 1) == L - 1, 1.0, 0.0)
    turned = 3.0 - dot(tokens, flip)
    tsend[...] = jnp.where(strand == 1, turned, tokens).astype(jnp.int32)

    def token_copy(j):
        return pltpu.make_async_remote_copy(
            src_ref=tsend,
            dst_ref=trecv.at[2 - j],
            send_sem=tsem.at[0, j],
            recv_sem=tsem.at[1, j],
            device_id={"pos": targets[j], "strand": strand, "rep": rep},
            device_id_type=MESH,
        )

    for j in range(3):
        @pl.when(targets[j] != pos)
        def _():
            token_copy(j).start()

        @pl.when(targets[j] == pos)
        def _():
            trecv[2 - j] = tsend[...]

    te = jnp.concatenate([k1[k : k + 1] * emb for k in range(3)] + [jnp.zeros((4, C), F32)], axis=0)
    hot_code = code_onehot(iota((PAD, 16), 0), iota((PAD, 16), 1))
    conv = share_out(hot_code, te, 3)
    inv_a = lax.rsqrt(jnp.mean(conv * conv, axis=-1, keepdims=True) + EPS)

    mirror = jnp.where(
        iota((BLOCK, BLOCK), 0) + iota((BLOCK, BLOCK), 1) == BLOCK - 1, 1.0, 0.0
    ).astype(BF16)
    loads[7].wait()
    loads[8].wait()

    def turn_cot(b, carry):
        here = lanes(b, BLOCK)
        there = lanes(BLOCKS - 1 - b, BLOCK)
        cots[0:L, here] = cot[:, here]
        cots[L : 2 * L, here] = dot(cot[:, there], mirror).astype(BF16)
        return carry

    lax.fori_loop(0, BLOCKS, turn_cot, 0)

    q_copies.wait()
    total = qrecv[0]
    for i in range(1, 32):
        total = total + qrecv[i]
    qown[...] = total
    qparts[pos] = total

    q_two = jnp.concatenate([total, pltpu.roll(total, 64, 1)], axis=0)
    q_two = jnp.where(iota((16, PAD), 1) < OWN, q_two, 0.0)
    pre_own = inv_a * share_out(hot_code, q_two, 3)
    act, slope_own = gelu_parts(pre_own)
    pads = jnp.zeros((4, PAD), F32)
    center = share_out(hot_code, jnp.concatenate([pads, e_own, pads, pads], axis=0), 1)
    m_own = jnp.where(iota((PAD, PAD), 0) < CODES, center + act, 0.0)
    m_own = m_own.astype(BF16).astype(F32)
    b_own = tap_rows(taps, m_own)
    a_own = g2_own * b_own
    aown[...] = a_own
    high, low = split(aown[rows(c, 128)])
    mine = lanes(x, 384)
    w2 = wpad2[:, mine]
    ppart[...] = dot(high, w2) + dot(low, w2)
    p_copies = net.start(
        [(ppart.at[rows(ys[d], 32)], py.at[d - 1], y_ids[d]) for d in range(1, 4)], py
    )
    q_copies = net.start(
        [(qown, qparts.at[pos], to) for to in plane_ids], qparts.at[0:31]
    )

    for j in range(3):
        @pl.when(targets[j] != pos)
        def _():
            token_copy(j).wait()
    joined = jnp.concatenate([trecv[0], trecv[1], trecv[2]], axis=1)
    place = (pos - 1) * L + iota((8, 3 * L), 1)
    ext = jnp.where((place >= 0) & (place < 32 * L), joined, 4)
    left = pltpu.roll(ext, FIRST_DILATE, 1)
    right = pltpu.roll(ext, 3 * L - FIRST_DILATE, 1)

    def other(base):
        return jnp.where(base == 4, 4, 3 - base)

    start = L - SECOND_DILATE
    code_a = pltpu.roll(code_of(left, ext, right), 3 * L - start, 1)[:, 0:384]
    code_b = pltpu.roll(code_of(other(right), other(ext), other(left)), 3 * L - start, 1)[:, 0:384]

    def shifts(code):
        return [code[:, 0:L]] + [
            pltpu.roll(code, 384 - s, 1)[:, 0:L] for s in (SECOND_DILATE, 2 * SECOND_DILATE)
        ]

    three_a = shifts(code_a)
    three_b = shifts(code_b)[::-1]
    index = [jnp.concatenate([a, b], axis=1) for a, b in zip(tap_index(three_a), tap_index(three_b))]
    line = iota((ROWS, 2 * L), 0)
    hit = (line == index[0][0:1]) | (line == index[1][0:1]) | (line == index[2][0:1])
    hot_t[...] = jnp.where(hit, 1.0, 0.0).astype(BF16)
    mid_t[...] = jnp.where(
        iota((PAD, 2 * L), 0) == jnp.concatenate([three_a[1], three_b[1]], axis=1)[0:1], 1.0, 0.0
    ).astype(BF16)

    def column(row):
        return jnp.transpose(row.astype(F32))[:, 0:1].astype(jnp.int32)

    p_copies.wait()
    pz[z] = (ppart[rows(y, 32)] + py[0] + py[1] + py[2]).astype(BF16)
    p_copies = net.start([(pz.at[z], pz.at[z], to) for to in z_ids[1:]], pz.at[0:7])

    columns = [column(row) for row in index]
    line = iota((2 * L, ROWS), 1)
    hit = (line == columns[0]) | (line == columns[1]) | (line == columns[2])
    hot[...] = jnp.where(hit, 1.0, 0.0).astype(BF16)
    line = iota((384, PAD), 1)
    wide_a[...] = jnp.where(line == column(code_a), 1.0, 0.0).astype(BF16)
    wide_b[...] = jnp.where(line == column(code_b), 1.0, 0.0).astype(BF16)

    q_copies.wait()
    for i in range(32):
        tile = qparts[i]
        qfull[0:8, OWN * i : OWN * i + OWN] = tile[:, 0:OWN]
        qfull[8:16, OWN * i : OWN * i + OWN] = tile[:, 64 : 64 + OWN]

    table_v[...] = jnp.zeros_like(table_v)
    pads = jnp.zeros((4, BLOCK), F32)
    sums = jnp.zeros((PAD, 128), F32)
    for b in range(BLOCKS):
        here = slice(BLOCK * b, BLOCK * b + BLOCK)
        pre = inv_a * share_out(hot_code, qfull[:, here], 3)
        act, grad = gelu_parts(pre)
        center = share_out(
            hot_code, jnp.concatenate([pads, emb[:, here], pads, pads], axis=0), 1
        )
        live = iota((PAD, BLOCK), 0) < CODES
        table[:, here] = jnp.where(live, center + act, 0.0).astype(BF16)
        sv = jnp.where(live, grad * (0.5 * dot(mid_t[...], cots[:, here])), 0.0)
        table_v[:, here] = inv_a * sv
        prod = sv * pre
        sums = sums + prod[:, 0:128] + prod[:, 128:256]

    p_copies.wait()
    quarter = pl.ds(pl.multiple_of(c * 128 + y * 32, 32), 32)
    total = pz[0].astype(F32)
    for i in range(1, 8):
        total = total + pz[i].astype(F32)
    pbuf[quarter, mine] = total.astype(BF16)
    block = pbuf.at[quarter, mine]
    p_copies = net.start(
        [(block, block, to) for to in square_ids], pbuf.at[0:240, 0:768]
    )

    hot_ct = code_onehot(iota((16, PAD), 1), iota((16, PAD), 0))
    fv = share_out(hot_ct, table_v[...], 2)
    mean_v = jnp.sum(sums, axis=1, keepdims=True) * (1.0 / C)
    hot_gram = code_onehot(iota((PAD, PAD), 0), iota((PAD, PAD), 1) - 96)
    gram_v = share_out(hot_ct, (inv_a * inv_a * mean_v) * hot_gram, 2)
    xbuf[:, C + ROWS : WIDE] = jnp.zeros((ROWS, WIDE - C - ROWS), F32)
    xbuf[0:16, C + ROWS : C + ROWS + PAD] = gram_v
    for i in range(16):
        xbuf[16 * i : 16 * i + 16, C + ROWS : C + ROWS + 96] = fv[:, 96 * i : 96 * i + 96]

    acc[...] = jnp.zeros_like(acc)
    acc2[...] = jnp.zeros_like(acc2)

    def first_pass(b, carry):
        here = lanes(b, BLOCK)
        m = table[:, here]
        taps2 = k2_ref[:, here]
        for n, (wide, order) in enumerate(((wide_a, (0, 1, 2)), (wide_b, (2, 1, 0)))):
            mid = dot(wide[...], m)
            conv = (
                taps2[order[0] : order[0] + 1] * mid[0:L]
                + taps2[order[1] : order[1] + 1] * mid[64 : 64 + L]
                + taps2[order[2] : order[2] + 1] * mid[128 : 128 + L]
            )
            square = conv * conv
            acc[n * L : n * L + L] += square[:, 0:128] + square[:, 128:256]
            mids[n * L : n * L + L, here] = mid[64 : 64 + L].astype(BF16)
        return carry

    lax.fori_loop(0, BLOCKS, first_pass, 0)
    acc[...] = jnp.broadcast_to(
        lax.rsqrt(jnp.sum(acc[...], axis=1, keepdims=True) * (1.0 / C) + EPS), (2 * L, 128)
    )

    half = rows(c, 128)
    p_copies.wait()
    net.start([(pbuf.at[half], pbuf.at[half], core_id)], pbuf.at[half]).wait()

    base = net.take(2)
    away = rows(1 - c, 128)

    def core_copy(b):
        here = lanes(b, BLOCK)
        return net.copy(core_send.at[:, here], from_core.at[:, here], core_id, base + b // 4)

    def second_pass(b, carry):
        here = lanes(b, BLOCK)
        preu[...] = dot(hot[...], pbuf[:, here])

        def chunk(r, carry):
            some = rows(r, 64)
            inv = acc[some]
            kept = acc2[some]
            for part in (0, 128):
                cut = pl.ds(pl.multiple_of(b * BLOCK + part, 128), 128)
                pre = inv * preu[some, part : part + 128]
                act, grad = gelu_parts(pre)
                fins[some, cut] = (mids[some, cut].astype(F32) + act).astype(BF16)
                sl = cots[some, cut].astype(F32) * grad
                kept = kept + sl * pre
                slope[some, part : part + 128] = (inv * sl).astype(BF16)
            acc2[some] = kept
            return carry

        lax.fori_loop(0, 8, chunk, 0)
        xbuf[:, here] = 0.5 * dot(hot_t[...], slope[...])
        core_send[:, here] = xbuf[away, here].astype(BF16)
        core_copy(b).start()
        return carry

    third = pl.ds(pl.multiple_of(c * 128 + x * 32, 32), 32)

    def chip_sum(first, last):
        xbuf[half, first:last] = xbuf[half, first:last] + from_core[:, first:last].astype(F32)
        chip_low[:, first:last] = xbuf[half, first:last].astype(BF16)

    def strip(h, at):
        return pl.ds(pl.multiple_of(1024 * h + at * 256, 128), 256)

    def square_scatter(h):
        items = []
        for j, (a, b) in enumerate(SQUARE):
            block = chip_low.at[rows(xs[a], 32), strip(h, ys[b])]
            items.append((block, xin.at[h, j], square_ids[j]))
        return net.start(items, xin.at[h])

    def line_all(h, copies):
        copies.wait()
        total = xbuf[third, strip(h, y)]
        for j in range(15):
            total = total + xin[h, j].astype(F32)
        zin[h, z] = total.astype(BF16)
        block = zin.at[h, z]
        return net.start([(block, block, to) for to in z_ids[1:]], zin.at[h, 0:7])

    def square_gather(h, copies):
        copies.wait()
        total = zin[h, 0].astype(F32)
        for d in range(1, 8):
            total = total + zin[h, d].astype(F32)
        full[third, strip(h, y)] = total.astype(BF16)
        block = full.at[third, strip(h, y)]
        items = [(block, block, to) for to in square_ids]
        return net.start(items, full.at[0:240, 0:512])

    def share(h, copies):
        copies.wait()
        block = full.at[half, 1024 * h : 1024 * h + 1024]
        return net.start([(block, block, core_id)], block)

    lax.fori_loop(0, 5, second_pass, 0)
    net.copy(core_send.at[:, 0:1024], from_core.at[:, 0:1024], core_id, base).wait()
    chip_sum(0, 1024)
    scatter_0 = square_scatter(0)
    lax.fori_loop(5, BLOCKS, second_pass, 0)

    inv = acc[:, 0:1]
    weight = (0.5 / C) * inv * inv * jnp.sum(acc2[...], axis=1, keepdims=True)
    xbuf[:, C : C + ROWS] = dot(hot_t[...], (weight * hot[...].astype(F32)).astype(BF16))
    core_send[:, C:WIDE] = xbuf[away, C:WIDE].astype(BF16)
    net.copy(core_send.at[:, C:WIDE], from_core.at[:, C:WIDE], core_id, base + 1).start()
    net.copy(core_send.at[:, 1024:WIDE], from_core.at[:, 1024:WIDE], core_id, base + 1).wait()
    chip_sum(1024, WIDE)
    scatter_1 = square_scatter(1)
    line_0 = line_all(0, scatter_0)

    def third_pass(b, carry):
        here = lanes(b, BLOCK)
        there = lanes(BLOCKS - 1 - b, BLOCK)
        far = dot(fins[L : 2 * L, there], mirror)
        out_buf[:, here] = (0.5 * (fins[0:L, here].astype(F32) + far)).astype(BF16)
        return carry

    lax.fori_loop(0, BLOCKS, third_pass, 0)
    store = pltpu.make_async_copy(out_buf, out_out, lsem.at[9])
    store.start()

    line_1 = line_all(1, scatter_1)
    back_0 = square_gather(0, line_0)
    back_1 = square_gather(1, line_1)
    shares = share(0, back_0)
    turned_high, turned_low = split(jnp.transpose(a_own))
    both = jnp.concatenate([turned_high[0:OWN], turned_low[0:OWN]], axis=0)

    def grad_b(b):
        grad = dot(both, full[:, b : b + 512])
        gw_ref[OWN : 2 * OWN, b : b + 512] = grad[0:OWN] + grad[OWN : 2 * OWN]

    shares.wait()
    ew = dot_nt(full[:, 0:1024], wpad2[:, 0:1024])
    shares = share(1, back_1)
    grad_b(0)
    grad_b(512)
    fbuf[...] = jnp.zeros_like(fbuf)
    shares.wait()

    ew = ew + dot_nt(full[:, 1024:C], wpad2[:, 1024:C])
    high, low = split(b_own)
    gram = full[:, C : C + ROWS]
    d = g2_own * ew - (dot(gram, high) + dot(gram, low))

    def total_rows(value):
        return jnp.sum(value, axis=0, keepdims=True)

    taps_b = [
        total_rows(m_own[0:80] * d[0:80]),
        total_rows(m_own[0:96] * d[80:176]),
        total_rows(m_own[0:64] * d[176:240]) + total_rows(m_own[80:96] * d[240:256]),
    ]
    gain_b = total_rows(b_own * ew)
    up = taps[1] * d[80:176] + jnp.concatenate(
        [taps[0] * d[0:64] + taps[2] * d[176:240], taps[0] * d[64:80], taps[2] * d[240:256]],
        axis=0,
    )
    s = slope_own[0:CODES] * up
    inv = inv_a[0:CODES]
    mean_s = jnp.sum(s * pre_own[0:CODES], axis=1, keepdims=True) * (1.0 / C)
    narrow = hot_ct[:, 0:CODES]
    hot_far = code_onehot(iota((CODES, PAD), 0), iota((CODES, PAD), 1) - OWN)
    extra = C + ROWS
    fv = full[pl.ds(pl.multiple_of((pos // 2) * 16, 16), 16), extra : extra + PAD].astype(F32)
    fv = jnp.where(pos % 2 == 1, pltpu.roll(fv, PAD - OWN, 1), fv)
    fv = jnp.where(iota((16, PAD), 1) < OWN, fv, 0.0)
    own_rows = fv + share_out(narrow, inv * s, 2)
    f_rows = jnp.where(iota((16, PAD), 0) < 12, own_rows, 0.0)
    vec_rows = jnp.concatenate([jnp.zeros((12, PAD), F32)] + taps_b + [gain_b], axis=0)
    packet = f_rows + vec_rows + share_out(narrow, (inv * inv * mean_s) * hot_far, 2)
    pack[...] = packet[0:8] + pltpu.roll(packet[8:16], 64, 1)
    packs[pos] = pack[...]
    copies = net.start([(pack, packs.at[pos], to) for to in plane_ids], packs.at[0:31])

    grad_b(1024)
    copies.wait()
    total = jnp.zeros((8, PAD), F32)
    for i in range(32):
        tile = packs[i]
        fbuf[0:8, OWN * i : OWN * i + OWN] = tile[:, 0:OWN]
        fbuf[8:16, OWN * i : OWN * i + OWN] = tile[:, 64 : 64 + OWN]
        total = total + tile
    far = jnp.concatenate([total, pltpu.roll(total, 64, 1)], axis=0)
    far = far + pltpu.roll(full[0:16, extra : extra + PAD].astype(F32), PAD - OWN, 1)
    far = jnp.where((iota((16, PAD), 1) >= OWN) & (iota((16, PAD), 1) < OWN + 12), far, 0.0)
    high, low = split(fbuf[0:16])
    fw = dot_nt(jnp.concatenate([high, low], axis=0), wpad1[...])
    fw = fw[0:16] + fw[16:32]
    spread = jnp.concatenate(
        [jnp.zeros((OWN, PAD), F32), te_own, jnp.zeros((64, PAD), F32)], axis=0
    )
    da = g1_own * fw - dot(far, spread, HIGH)
    rows_a = [total_rows(e_own * da[4 * k : 4 * k + 4]) for k in range(3)]
    rows_a = rows_a + [total_rows(te_own * fw)]
    pack2[...] = jnp.concatenate(
        [
            rows_a[0] + pltpu.roll(rows_a[1], 64, 1),
            rows_a[2] + pltpu.roll(rows_a[3], 64, 1),
        ],
        axis=0,
    )
    packs2[pos] = pack2[...]
    copies = net.start(
        [(pack2, packs2.at[pos], to) for to in plane_ids], packs2.at[0:31]
    )

    wide = jnp.concatenate([g1_own * te_own, jnp.zeros((PAD - 16, PAD), F32)], axis=0)
    wide_high, wide_low = split(jnp.transpose(wide)[0:OWN])
    wide = jnp.concatenate([wide_high, wide_low], axis=0)
    for b in range(0, C, 512):
        f_high, f_low = split(fbuf[:, b : b + 512])
        grad = dot(wide, f_high)
        gw_ref[0:OWN, b : b + 512] = grad[0:OWN] + grad[OWN : 2 * OWN] + dot(wide_high, f_low)
    vec_ref[4:8, :] = fbuf[12:16, :]
    copies.wait()
    for i in range(32):
        tile = packs2[i]
        here = slice(OWN * i, OWN * i + OWN)
        vec_ref[0:1, here] = tile[0:1, 0:OWN]
        vec_ref[1:2, here] = tile[0:1, 64 : 64 + OWN]
        vec_ref[2:3, here] = tile[1:2, 0:OWN]
        vec_ref[3:4, here] = tile[1:2, 64 : 64 + OWN]
    store.wait()


def whole(*args):
    vmem = pl.BlockSpec(memory_space=pltpu.VMEM)
    hbm = pl.BlockSpec(memory_space=pltpu.HBM)
    anywhere = pl.BlockSpec(memory_space=pl.ANY)
    return pl.pallas_call(
        whole_kernel,
        out_shape=(
            jax.ShapeDtypeStruct((L, C), BF16),
            jax.ShapeDtypeStruct((2 * OWN, C), F32),
            jax.ShapeDtypeStruct((8, C), F32),
        ),
        in_specs=[hbm] * 9,
        out_specs=(anywhere, vmem, vmem),
        scratch_shapes=[
            pltpu.VMEM((1, L), jnp.int32),
            pltpu.VMEM((4, C), BF16),
            pltpu.VMEM((3, C), F32),
            pltpu.VMEM((C,), F32),
            pltpu.VMEM((3, C), F32),
            pltpu.VMEM((C,), F32),
            pltpu.VMEM((PAD, C), BF16),
            pltpu.VMEM((PAD, C), BF16),
            pltpu.VMEM((L, C), BF16),
            pltpu.VMEM((8, L), jnp.int32),
            pltpu.VMEM((3, 8, L), jnp.int32),
            pltpu.VMEM((32, 8, PAD), F32),
            pltpu.VMEM((32, 8, PAD), F32),
            pltpu.VMEM((8, PAD), F32),
            pltpu.VMEM((32, 8, PAD), F32),
            pltpu.VMEM((16, C), F32),
            pltpu.VMEM((ROWS, PAD), F32),
            pltpu.VMEM((128, 384), F32),
            pltpu.VMEM((3, 32, 384), F32),
            pltpu.VMEM((8, 32, 384), BF16),
            pltpu.VMEM((ROWS, C), BF16),
            pltpu.VMEM((PAD, C), BF16),
            pltpu.VMEM((8, PAD), F32),
            pltpu.VMEM((PAD, C), F32),
            pltpu.VMEM((2 * L, ROWS), BF16),
            pltpu.VMEM((ROWS, 2 * L), BF16),
            pltpu.VMEM((384, PAD), BF16),
            pltpu.VMEM((384, PAD), BF16),
            pltpu.VMEM((PAD, 2 * L), BF16),
            pltpu.VMEM((2 * L, C), BF16),
            pltpu.VMEM((2 * L, C), BF16),
            pltpu.VMEM((2 * L, C), BF16),
            pltpu.VMEM((2 * L, BLOCK), F32),
            pltpu.VMEM((2 * L, BLOCK), BF16),
            pltpu.VMEM((2 * L, 128), F32),
            pltpu.VMEM((2 * L, 128), F32),
            pltpu.VMEM((L, C), BF16),
            pltpu.VMEM((ROWS, WIDE), F32),
            pltpu.VMEM((128, WIDE), BF16),
            pltpu.VMEM((128, WIDE), BF16),
            pltpu.VMEM((128, WIDE), BF16),
            pltpu.VMEM((2, 15, 32, 256), BF16),
            pltpu.VMEM((2, 8, 32, 256), BF16),
            pltpu.VMEM((ROWS, WIDE), BF16),
            pltpu.VMEM((8, PAD), F32),
            pltpu.VMEM((32, 8, PAD), F32),
            pltpu.VMEM((PAD, C), F32),
            pltpu.VMEM((2, PAD), F32),
            pltpu.VMEM((32, 2, PAD), F32),
            pltpu.SemaphoreType.DMA((10,)),
            pltpu.SemaphoreType.DMA((2, 3)),
            pltpu.SemaphoreType.DMA((24,)),
            pltpu.SemaphoreType.DMA((24,)),
        ],
        compiler_params=pltpu.CompilerParams(
            collective_id=0, has_side_effects=True, vmem_limit_bytes=62 * 2**20
        ),
        name="whole",
    )(*args)


def place_kernel(out_in, gw_in, vec_ref, out_ref, gwa_ref, gwb_ref, ta_ref, tb_ref, ga_ref, gb_ref):
    out_ref[...] = out_in[...]
    gwa_ref[...] = gw_in[0:OWN]
    gwb_ref[...] = gw_in[OWN : 2 * OWN]
    ta_ref[...] = vec_ref[0:3]
    tb_ref[...] = vec_ref[4:7]
    ga_ref[...] = vec_ref[3]
    gb_ref[...] = vec_ref[7]


def placed_outputs(out, gw, vec):
    vmem = pl.BlockSpec(memory_space=pltpu.VMEM)
    return pl.pallas_call(
        place_kernel,
        out_shape=(
            jax.ShapeDtypeStruct((L, C), BF16),
            jax.ShapeDtypeStruct((OWN, C), F32),
            jax.ShapeDtypeStruct((OWN, C), F32),
            jax.ShapeDtypeStruct((3, C), F32),
            jax.ShapeDtypeStruct((3, C), F32),
            jax.ShapeDtypeStruct((C,), F32),
            jax.ShapeDtypeStruct((C,), F32),
        ),
        in_specs=[vmem] * 3,
        out_specs=(vmem,) * 7,
        compiler_params=pltpu.CompilerParams(vmem_limit_bytes=62 * 2**20),
        name="place",
    )(out, gw, vec)


def shards(tokens, embed, k1, g1, w1, k2, g2, w2, cotangent):
    out, gw, vec = whole(tokens, embed, k1, g1, w1, k2, g2, w2, cotangent.reshape(L, C))
    out, gwa, gwb, ta, tb, ga, gb = placed_outputs(out, gw, vec)
    return (out[None, None], gwa, gwb, ta, tb, ga, gb)


def solution(mesh):
    placed = (
        P("rep", "pos"),
        P(),
        P(),
        P(),
        P("pos", None),
        P(),
        P(),
        P("pos", None),
        P("rep", "strand", "pos", None),
    )
    return jax.shard_map(
        shards,
        mesh=mesh,
        in_specs=placed,
        out_specs=(
            P("rep", "strand", "pos", None),
            P("pos", None),
            P("pos", None),
            P(),
            P(),
            P(),
            P(),
        ),
        check_vma=False,
    )
```

```python
import functools

import jax
import jax.numpy as jnp
from jax import lax
from jax.experimental import pallas as pl
from jax.experimental.pallas import tpu as pltpu
from jax.sharding import PartitionSpec as P

MESH = pl.DeviceIdType.MESH
HIGH = lax.Precision.HIGHEST
F32 = jnp.float32
BF16 = jnp.bfloat16
C = 1536
L = 256
FIRST_DILATE = 32
SECOND_DILATE = 64
EPS = 1e-05
CODES = 96
PAD = 128
ROWS = 256
WIDE = 2048
BLOCK = 256
BLOCKS = C // BLOCK
OWN = 48
GELU_A = 0.7978845608028654
GELU_B = 0.044715


def coords():
    pos = lax.axis_index("pos")
    strand = lax.axis_index("strand")
    rep = lax.axis_index("rep")
    high, core = lax.div(rep, 2), lax.rem(rep, 2)
    return lax.div(pos, 8), lax.rem(pos, 8), high * 2 + strand, core


PLANE = [(a, b) for a in range(4) for b in range(8) if a or b]
SQUARE = [(a, b) for a in range(4) for b in range(4) if a or b]


def wrapped(at, size):
    moved = [at] + [at + d for d in range(1, size)]
    return [at] + [jnp.where(m >= size, m - size, m) for m in moved[1:]]


class Net:
    def __init__(self, send, recv):
        self.send, self.recv, self.used = send, recv, 0

    def take(self, count):
        first = self.used
        self.used += count
        return first

    def copy(self, src, dst, to, sem):
        return pltpu.make_async_remote_copy(
            src_ref=src,
            dst_ref=dst,
            send_sem=self.send.at[sem],
            recv_sem=self.recv.at[sem],
            device_id=to,
            device_id_type=MESH,
        )

    def start(self, items, total):
        sem = self.take(1)
        for src, dst, to in items:
            self.copy(src, dst, to, sem).start()
        return self.copy(total, total, items[0][2], sem)


def share_out(onehot, value, parts):
    total = None
    for _ in range(parts):
        part = value.astype(BF16)
        value = value - part.astype(F32)
        term = dot(onehot.astype(BF16), part)
        total = term if total is None else total + term
    return total


def lanes(index, width):
    return pl.ds(pl.multiple_of(index * width, 128), width)


def rows(index, height):
    return pl.ds(pl.multiple_of(index * height, 8), height)


def dot(a, b, precision=None):
    return lax.dot_general(
        a, b, (((1,), (0,)), ((), ())), preferred_element_type=F32, precision=precision
    )


def dot_nt(a, b):
    return lax.dot_general(a, b, (((1,), (1,)), ((), ())), preferred_element_type=F32)


def split(value):
    high = value.astype(BF16)
    return high, (value - high.astype(F32)).astype(BF16)


def gelu_parts(pre):
    square = pre * pre
    th = jnp.tanh(pre * (GELU_A + (GELU_A * GELU_B) * square))
    half = 0.5 + 0.5 * th
    bend = pre * (GELU_A + (3.0 * GELU_A * GELU_B) * square)
    return pre * half, half * (1.0 + (1.0 - th) * bend)


def code_bases(code):
    inner, left = code < 64, code < 80
    one = jnp.where(inner, code // 16, jnp.where(left, -1, (code - 80) // 4))
    two = jnp.where(inner, (code // 4) % 4, jnp.where(left, (code - 64) // 4, code % 4))
    three = jnp.where(inner | left, code % 4, -1)
    return one, two, three


def code_onehot(code, column):
    one, two, three = code_bases(code)
    hit = (column == one) & (one >= 0)
    hit = hit | (column == 4 + two) | ((column == 8 + three) & (three >= 0))
    return jnp.where(hit & (code < CODES), 1.0, 0.0)


def iota(shape, axis):
    return lax.broadcasted_iota(jnp.int32, shape, axis)


def tap_rows(taps, table):
    return jnp.concatenate(
        [taps[0] * table[0:80], taps[1] * table[0:96], taps[2] * table[0:64], taps[2] * table[80:96]],
        axis=0,
    )


def code_of(left, middle, right):
    code = jnp.where(
        left == 4,
        64 + 4 * middle + right,
        jnp.where(right == 4, 80 + 4 * left + middle, 16 * left + 4 * middle + right),
    )
    return jnp.where(middle == 4, -1, code)


def tap_index(codes):
    first, second, third = codes
    second = jnp.where(second < 0, -1, 80 + second)
    third = jnp.where(third < 0, -1, jnp.where(third < 64, 176 + third, 160 + third))
    return first, second, third


def whole_kernel(
    tok_in,
    emb_in,
    k1_in,
    g1_in,
    w1_in,
    k2_in,
    g2_in,
    w2_in,
    cot_in,
    out_out,
    gw_ref,
    vec_ref,
    tok,
    emb16,
    k1_ref,
    g1_ref,
    k2_ref,
    g2_ref,
    wpad1,
    wpad2,
    cot,
    tsend,
    trecv,
    qsend,
    qrecv,
    qown,
    qparts,
    qfull,
    aown,
    ppart,
    plow,
    py,
    pz,
    pbuf,
    table,
    table_slope,
    table_v,
    hot,
    hot_t,
    wide_a,
    wide_b,
    mid_t,
    cots,
    mids,
    fins,
    preu,
    slope,
    acc,
    acc2,
    out_buf,
    xbuf,
    core_send,
    from_core,
    chip_low,
    xin,
    zin,
    full,
    pack,
    packs,
    fbuf,
    pack2,
    packs2,
    lsem,
    tsem,
    send,
    recv,
):
    y, z, x, c = coords()
    pos = lax.axis_index("pos")
    strand = lax.axis_index("strand")
    rep = lax.axis_index("rep")
    ys, zs, xs = wrapped(y, 4), wrapped(z, 8), wrapped(x, 4)
    xsr = [(lax.rem(v, 2), lax.div(v, 2) * 2 + c) for v in xs]
    xsr[0] = (strand, rep)

    def peer_at(a, b, e):
        return {"pos": ys[a] * 8 + zs[b], "strand": xsr[e][0], "rep": xsr[e][1]}

    plane_ids = [peer_at(a, b, 0) for a, b in PLANE]
    square_ids = [peer_at(b, 0, a) for a, b in SQUARE]
    y_ids = [peer_at(d, 0, 0) for d in range(4)]
    z_ids = [peer_at(0, d, 0) for d in range(8)]
    core_id = {"pos": pos, "strand": strand, "rep": rep + 1 - 2 * c}
    frame = jnp.where(strand == 1, 31 - pos, pos)
    targets = [(frame + d + 32) % 32 for d in (-1, 0, 1)]
    net = Net(send, recv)

    wpad1[OWN:PAD] = jnp.zeros((PAD - OWN, C), BF16)
    wpad2[OWN:PAD] = jnp.zeros((PAD - OWN, C), BF16)
    loads = [
        pltpu.make_async_copy(src, dst, lsem.at[i])
        for i, (src, dst) in enumerate(
            (
                (emb_in, emb16),
                (k1_in, k1_ref),
                (g1_in, g1_ref),
                (w1_in, wpad1.at[0:OWN]),
                (k2_in, k2_ref),
                (g2_in, g2_ref),
                (tok_in, tok),
                (w2_in, wpad2.at[0:OWN]),
                (cot_in, cot),
            )
        )
    ]
    for load in loads:
        load.start()

    barrier = pltpu.get_barrier_semaphore()
    peers = plane_ids + [i for i, (a, b) in zip(square_ids, SQUARE) if a] + [core_id]
    for peer in peers:
        pl.semaphore_signal(barrier, inc=1, device_id=peer, device_id_type=MESH)

    for load in loads[:6]:
        load.wait()
    emb = emb16[...].astype(F32)
    k1, k2 = k1_ref[...], k2_ref[...]
    g1, g2 = g1_ref[...].reshape(1, C), g2_ref[...].reshape(1, C)
    packed = jnp.concatenate([emb, k1, g1, k2, g2, jnp.zeros((4, C), F32)], axis=0)
    vec = pltpu.roll(packed, lax.rem(C - pos * OWN, C), 1)[:, 0:PAD]
    vec = jnp.where(iota((16, PAD), 1) < OWN, vec, 0.0)
    e_own, g1_own, g2_own = vec[0:4], vec[7:8], vec[11:12]
    taps = [vec[8 + k : 9 + k] for k in range(3)]
    te_own = jnp.concatenate(
        [vec[4 + k : 5 + k] * e_own for k in range(3)] + [jnp.zeros((4, PAD), F32)], axis=0
    )
    high, low = split(g1_own * te_own)
    part = dot(jnp.concatenate([high, low], axis=0), wpad1[...])
    part = part[0:16] + part[16:32]
    qsend[...] = jnp.zeros_like(qsend)
    for i in range(32):
        qsend[i, :, 0:OWN] = part[0:8, OWN * i : OWN * i + OWN]
        qsend[i, :, 64 : 64 + OWN] = part[8:16, OWN * i : OWN * i + OWN]
    qrecv[pos] = qsend[pos]

    pl.semaphore_wait(barrier, len(peers))

    q_copies = net.start(
        [
            (qsend.at[to["pos"]], qrecv.at[pos], to)
            for to in plane_ids
        ],
        qrecv.at[0:31],
    )

    loads[6].wait()
    tokens = jnp.broadcast_to(tok[...], (8, L)).astype(F32)
    flip = jnp.where(iota((L, L), 0) + iota((L, L), 1) == L - 1, 1.0, 0.0)
    turned = 3.0 - dot(tokens, flip)
    tsend[...] = jnp.where(strand == 1, turned, tokens).astype(jnp.int32)

    def token_copy(j):
        return pltpu.make_async_remote_copy(
            src_ref=tsend,
            dst_ref=trecv.at[2 - j],
            send_sem=tsem.at[0, j],
            recv_sem=tsem.at[1, j],
            device_id={"pos": targets[j], "strand": strand, "rep": rep},
            device_id_type=MESH,
        )

    for j in range(3):
        @pl.when(targets[j] != pos)
        def _():
            token_copy(j).start()

        @pl.when(targets[j] == pos)
        def _():
            trecv[2 - j] = tsend[...]

    te = jnp.concatenate([k1[k : k + 1] * emb for k in range(3)] + [jnp.zeros((4, C), F32)], axis=0)
    hot_code = code_onehot(iota((PAD, 16), 0), iota((PAD, 16), 1))
    conv = share_out(hot_code, te, 3)
    inv_a = lax.rsqrt(jnp.mean(conv * conv, axis=-1, keepdims=True) + EPS)

    mirror = jnp.where(
        iota((BLOCK, BLOCK), 0) + iota((BLOCK, BLOCK), 1) == BLOCK - 1, 1.0, 0.0
    ).astype(BF16)
    loads[7].wait()
    loads[8].wait()

    def turn_cot(b, carry):
        here = lanes(b, BLOCK)
        there = lanes(BLOCKS - 1 - b, BLOCK)
        cots[0:L, here] = cot[:, here]
        cots[L : 2 * L, here] = dot(cot[:, there], mirror).astype(BF16)
        return carry

    lax.fori_loop(0, BLOCKS, turn_cot, 0)

    q_copies.wait()
    total = qrecv[0]
    for i in range(1, 32):
        total = total + qrecv[i]
    qown[...] = total
    qparts[pos] = total

    q_two = jnp.concatenate([total, pltpu.roll(total, 64, 1)], axis=0)
    q_two = jnp.where(iota((16, PAD), 1) < OWN, q_two, 0.0)
    pre_own = inv_a * share_out(hot_code, q_two, 3)
    act, slope_own = gelu_parts(pre_own)
    pads = jnp.zeros((4, PAD), F32)
    center = share_out(hot_code, jnp.concatenate([pads, e_own, pads, pads], axis=0), 1)
    m_own = jnp.where(iota((PAD, PAD), 0) < CODES, center + act, 0.0)
    m_own = m_own.astype(BF16).astype(F32)
    b_own = tap_rows(taps, m_own)
    a_own = g2_own * b_own
    aown[...] = a_own
    high, low = split(aown[rows(c, 128)])
    mine = lanes(x, 384)
    w2 = wpad2[:, mine]
    ppart[...] = dot(high, w2) + dot(low, w2)
    plow[...] = ppart[...].astype(BF16)
    p_copies = net.start(
        [(plow.at[rows(ys[d], 32)], py.at[d - 1], y_ids[d]) for d in range(1, 4)], py
    )
    q_copies = net.start(
        [(qown, qparts.at[pos], to) for to in plane_ids], qparts.at[0:31]
    )

    for j in range(3):
        @pl.when(targets[j] != pos)
        def _():
            token_copy(j).wait()
    joined = jnp.concatenate([trecv[0], trecv[1], trecv[2]], axis=1)
    place = (pos - 1) * L + iota((8, 3 * L), 1)
    ext = jnp.where((place >= 0) & (place < 32 * L), joined, 4)
    left = pltpu.roll(ext, FIRST_DILATE, 1)
    right = pltpu.roll(ext, 3 * L - FIRST_DILATE, 1)

    def other(base):
        return jnp.where(base == 4, 4, 3 - base)

    start = L - SECOND_DILATE
    code_a = pltpu.roll(code_of(left, ext, right), 3 * L - start, 1)[:, 0:384]
    code_b = pltpu.roll(code_of(other(right), other(ext), other(left)), 3 * L - start, 1)[:, 0:384]

    def shifts(code):
        return [code[:, 0:L]] + [
            pltpu.roll(code, 384 - s, 1)[:, 0:L] for s in (SECOND_DILATE, 2 * SECOND_DILATE)
        ]

    three_a = shifts(code_a)
    three_b = shifts(code_b)[::-1]
    index = [jnp.concatenate([a, b], axis=1) for a, b in zip(tap_index(three_a), tap_index(three_b))]
    line = iota((ROWS, 2 * L), 0)
    hit = (line == index[0][0:1]) | (line == index[1][0:1]) | (line == index[2][0:1])
    hot_t[...] = jnp.where(hit, 1.0, 0.0).astype(BF16)
    mid_t[...] = jnp.where(
        iota((PAD, 2 * L), 0) == jnp.concatenate([three_a[1], three_b[1]], axis=1)[0:1], 1.0, 0.0
    ).astype(BF16)

    def column(row):
        return jnp.transpose(row.astype(F32))[:, 0:1].astype(jnp.int32)

    p_copies.wait()
    total = ppart[rows(y, 32)]
    for i in range(3):
        total = total + py[i].astype(F32)
    pz[z] = total.astype(BF16)
    p_copies = net.start([(pz.at[z], pz.at[z], to) for to in z_ids[1:]], pz.at[0:7])

    columns = [column(row) for row in index]
    line = iota((2 * L, ROWS), 1)
    hit = (line == columns[0]) | (line == columns[1]) | (line == columns[2])
    hot[...] = jnp.where(hit, 1.0, 0.0).astype(BF16)
    line = iota((384, PAD), 1)
    wide_a[...] = jnp.where(line == column(code_a), 1.0, 0.0).astype(BF16)
    wide_b[...] = jnp.where(line == column(code_b), 1.0, 0.0).astype(BF16)

    q_copies.wait()
    for i in range(32):
        tile = qparts[i]
        qfull[0:8, OWN * i : OWN * i + OWN] = tile[:, 0:OWN]
        qfull[8:16, OWN * i : OWN * i + OWN] = tile[:, 64 : 64 + OWN]

    table_v[...] = jnp.zeros_like(table_v)
    pads = jnp.zeros((4, BLOCK), F32)
    sums = jnp.zeros((PAD, 128), F32)
    for b in range(BLOCKS):
        here = slice(BLOCK * b, BLOCK * b + BLOCK)
        pre = inv_a * share_out(hot_code, qfull[:, here], 3)
        act, grad = gelu_parts(pre)
        center = share_out(
            hot_code, jnp.concatenate([pads, emb[:, here], pads, pads], axis=0), 1
        )
        live = iota((PAD, BLOCK), 0) < CODES
        table[:, here] = jnp.where(live, center + act, 0.0).astype(BF16)
        sv = jnp.where(live, grad * (0.5 * dot(mid_t[...], cots[:, here])), 0.0)
        table_v[:, here] = inv_a * sv
        prod = sv * pre
        sums = sums + prod[:, 0:128] + prod[:, 128:256]

    p_copies.wait()
    quarter = pl.ds(pl.multiple_of(c * 128 + y * 32, 32), 32)
    total = pz[0].astype(F32)
    for i in range(1, 8):
        total = total + pz[i].astype(F32)
    pbuf[quarter, mine] = total.astype(BF16)
    block = pbuf.at[quarter, mine]
    p_copies = net.start(
        [(block, block, to) for to in square_ids], pbuf.at[0:240, 0:768]
    )

    hot_ct = code_onehot(iota((16, PAD), 1), iota((16, PAD), 0))
    fv = share_out(hot_ct, table_v[...], 2)
    mean_v = jnp.sum(sums, axis=1, keepdims=True) * (1.0 / C)
    hot_gram = code_onehot(iota((PAD, PAD), 0), iota((PAD, PAD), 1) - 96)
    gram_v = share_out(hot_ct, (inv_a * inv_a * mean_v) * hot_gram, 2)
    xbuf[:, C + ROWS : WIDE] = jnp.zeros((ROWS, WIDE - C - ROWS), F32)
    xbuf[0:16, C + ROWS : C + ROWS + PAD] = gram_v
    for i in range(16):
        xbuf[16 * i : 16 * i + 16, C + ROWS : C + ROWS + 96] = fv[:, 96 * i : 96 * i + 96]

    acc[...] = jnp.zeros_like(acc)
    acc2[...] = jnp.zeros_like(acc2)

    def first_pass(b, carry):
        here = lanes(b, BLOCK)
        m = table[:, here]
        taps2 = k2_ref[:, here]
        for n, (wide, order) in enumerate(((wide_a, (0, 1, 2)), (wide_b, (2, 1, 0)))):
            mid = dot(wide[...], m)
            conv = (
                taps2[order[0] : order[0] + 1] * mid[0:L]
                + taps2[order[1] : order[1] + 1] * mid[64 : 64 + L]
                + taps2[order[2] : order[2] + 1] * mid[128 : 128 + L]
            )
            square = conv * conv
            acc[n * L : n * L + L] += square[:, 0:128] + square[:, 128:256]
            mids[n * L : n * L + L, here] = mid[64 : 64 + L].astype(BF16)
        return carry

    lax.fori_loop(0, BLOCKS, first_pass, 0)
    acc[...] = jnp.broadcast_to(
        lax.rsqrt(jnp.sum(acc[...], axis=1, keepdims=True) * (1.0 / C) + EPS), (2 * L, 128)
    )

    half = rows(c, 128)
    p_copies.wait()
    net.start([(pbuf.at[half], pbuf.at[half], core_id)], pbuf.at[half]).wait()

    base = net.take(2)
    away = rows(1 - c, 128)

    def core_copy(b):
        here = lanes(b, BLOCK)
        return net.copy(core_send.at[:, here], from_core.at[:, here], core_id, base + b // 4)

    def second_pass(b, carry):
        here = lanes(b, BLOCK)
        preu[...] = dot(hot[...], pbuf[:, here])

        def chunk(r, carry):
            some = rows(r, 64)
            inv = acc[some]
            kept = acc2[some]
            for part in (0, 128):
                cut = pl.ds(pl.multiple_of(b * BLOCK + part, 128), 128)
                pre = inv * preu[some, part : part + 128]
                act, grad = gelu_parts(pre)
                fins[some, cut] = (mids[some, cut].astype(F32) + act).astype(BF16)
                sl = cots[some, cut].astype(F32) * grad
                kept = kept + sl * pre
                slope[some, part : part + 128] = (inv * sl).astype(BF16)
            acc2[some] = kept
            return carry

        lax.fori_loop(0, 8, chunk, 0, unroll=4)
        xbuf[:, here] = 0.5 * dot(hot_t[...], slope[...])
        core_send[:, here] = xbuf[away, here].astype(BF16)
        core_copy(b).start()
        return carry

    third = pl.ds(pl.multiple_of(c * 128 + x * 32, 32), 32)

    def chip_sum(first, last):
        xbuf[half, first:last] = xbuf[half, first:last] + from_core[:, first:last].astype(F32)
        chip_low[:, first:last] = xbuf[half, first:last].astype(BF16)

    def strip(h, at):
        return pl.ds(pl.multiple_of(1024 * h + at * 256, 128), 256)

    def square_scatter(h):
        items = []
        for j, (a, b) in enumerate(SQUARE):
            block = chip_low.at[rows(xs[a], 32), strip(h, ys[b])]
            items.append((block, xin.at[h, j], square_ids[j]))
        return net.start(items, xin.at[h])

    def line_all(h, copies):
        copies.wait()
        total = xbuf[third, strip(h, y)]
        for j in range(15):
            total = total + xin[h, j].astype(F32)
        zin[h, z] = total.astype(BF16)
        block = zin.at[h, z]
        return net.start([(block, block, to) for to in z_ids[1:]], zin.at[h, 0:7])

    def square_gather(h, copies):
        copies.wait()
        total = zin[h, 0].astype(F32)
        for d in range(1, 8):
            total = total + zin[h, d].astype(F32)
        full[third, strip(h, y)] = total.astype(BF16)
        block = full.at[third, strip(h, y)]
        items = [(block, block, to) for to in square_ids]
        return net.start(items, full.at[0:240, 0:512])

    def share(h, copies):
        copies.wait()
        block = full.at[half, 1024 * h : 1024 * h + 1024]
        return net.start([(block, block, core_id)], block)

    lax.fori_loop(0, 5, second_pass, 0)
    net.copy(core_send.at[:, 0:1024], from_core.at[:, 0:1024], core_id, base).wait()
    chip_sum(0, 1024)
    scatter_0 = square_scatter(0)
    lax.fori_loop(5, BLOCKS, second_pass, 0)

    inv = acc[:, 0:1]
    weight = (0.5 / C) * inv * inv * jnp.sum(acc2[...], axis=1, keepdims=True)
    xbuf[:, C : C + ROWS] = dot(hot_t[...], (weight * hot[...].astype(F32)).astype(BF16))
    core_send[:, C:WIDE] = xbuf[away, C:WIDE].astype(BF16)
    net.copy(core_send.at[:, C:WIDE], from_core.at[:, C:WIDE], core_id, base + 1).start()
    net.copy(core_send.at[:, 1024:WIDE], from_core.at[:, 1024:WIDE], core_id, base + 1).wait()
    chip_sum(1024, WIDE)
    scatter_1 = square_scatter(1)
    line_0 = line_all(0, scatter_0)

    def third_pass(b, carry):
        here = lanes(b, BLOCK)
        there = lanes(BLOCKS - 1 - b, BLOCK)
        far = dot(fins[L : 2 * L, there], mirror)
        out_buf[:, here] = (0.5 * (fins[0:L, here].astype(F32) + far)).astype(BF16)
        return carry

    lax.fori_loop(0, BLOCKS, third_pass, 0)
    store = pltpu.make_async_copy(out_buf, out_out, lsem.at[9])
    store.start()

    line_1 = line_all(1, scatter_1)
    back_0 = square_gather(0, line_0)
    back_1 = square_gather(1, line_1)
    shares = share(0, back_0)
    turned_high, turned_low = split(jnp.transpose(a_own))
    both = jnp.concatenate([turned_high[0:OWN], turned_low[0:OWN]], axis=0)

    def grad_b(b):
        grad = dot(both, full[:, b : b + 512])
        gw_ref[OWN : 2 * OWN, b : b + 512] = grad[0:OWN] + grad[OWN : 2 * OWN]

    shares.wait()
    ew = dot_nt(full[:, 0:1024], wpad2[:, 0:1024])
    shares = share(1, back_1)
    grad_b(0)
    grad_b(512)
    fbuf[...] = jnp.zeros_like(fbuf)
    shares.wait()

    ew = ew + dot_nt(full[:, 1024:C], wpad2[:, 1024:C])
    high, low = split(b_own)
    gram = full[:, C : C + ROWS]
    fix = dot(gram, jnp.concatenate([high, low], axis=1))
    d = g2_own * ew - (fix[:, 0:PAD] + fix[:, PAD : 2 * PAD])

    def total_rows(value):
        return jnp.sum(value, axis=0, keepdims=True)

    taps_b = [
        total_rows(m_own[0:80] * d[0:80]),
        total_rows(m_own[0:96] * d[80:176]),
        total_rows(m_own[0:64] * d[176:240]) + total_rows(m_own[80:96] * d[240:256]),
    ]
    gain_b = total_rows(b_own * ew)
    up = taps[1] * d[80:176] + jnp.concatenate(
        [taps[0] * d[0:64] + taps[2] * d[176:240], taps[0] * d[64:80], taps[2] * d[240:256]],
        axis=0,
    )
    s = slope_own[0:CODES] * up
    inv = inv_a[0:CODES]
    mean_s = jnp.sum(s * pre_own[0:CODES], axis=1, keepdims=True) * (1.0 / C)
    narrow = hot_ct[:, 0:CODES]
    hot_far = code_onehot(iota((CODES, PAD), 0), iota((CODES, PAD), 1) - OWN)
    extra = C + ROWS
    fv = full[pl.ds(pl.multiple_of((pos // 2) * 16, 16), 16), extra : extra + PAD].astype(F32)
    fv = jnp.where(pos % 2 == 1, pltpu.roll(fv, PAD - OWN, 1), fv)
    fv = jnp.where(iota((16, PAD), 1) < OWN, fv, 0.0)
    own_rows = fv + share_out(narrow, inv * s, 2)
    f_rows = jnp.where(iota((16, PAD), 0) < 12, own_rows, 0.0)
    vec_rows = jnp.concatenate([jnp.zeros((12, PAD), F32)] + taps_b + [gain_b], axis=0)
    packet = f_rows + vec_rows + share_out(narrow, (inv * inv * mean_s) * hot_far, 2)
    pack[...] = packet[0:8] + pltpu.roll(packet[8:16], 64, 1)
    packs[pos] = pack[...]
    copies = net.start([(pack, packs.at[pos], to) for to in plane_ids], packs.at[0:31])

    grad_b(1024)
    copies.wait()
    total = jnp.zeros((8, PAD), F32)
    for i in range(32):
        tile = packs[i]
        fbuf[0:8, OWN * i : OWN * i + OWN] = tile[:, 0:OWN]
        fbuf[8:16, OWN * i : OWN * i + OWN] = tile[:, 64 : 64 + OWN]
        total = total + tile
    far = jnp.concatenate([total, pltpu.roll(total, 64, 1)], axis=0)
    far = far + pltpu.roll(full[0:16, extra : extra + PAD].astype(F32), PAD - OWN, 1)
    far = jnp.where((iota((16, PAD), 1) >= OWN) & (iota((16, PAD), 1) < OWN + 12), far, 0.0)
    high, low = split(fbuf[0:16])
    fw = dot_nt(jnp.concatenate([high, low], axis=0), wpad1[...])
    fw = fw[0:16] + fw[16:32]
    spread = jnp.concatenate(
        [jnp.zeros((OWN, PAD), F32), te_own, jnp.zeros((64, PAD), F32)], axis=0
    )
    far_high, far_low = split(far)
    spread_high, spread_low = split(spread)
    fix = dot(jnp.concatenate([far_high, far_low], axis=0), spread_high)
    da = g1_own * fw - (fix[0:16] + fix[16:32] + dot(far_high, spread_low))
    rows_a = [total_rows(e_own * da[4 * k : 4 * k + 4]) for k in range(3)]
    rows_a = rows_a + [total_rows(te_own * fw)]
    pack2[...] = jnp.concatenate(
        [
            rows_a[0] + pltpu.roll(rows_a[1], 64, 1),
            rows_a[2] + pltpu.roll(rows_a[3], 64, 1),
        ],
        axis=0,
    )
    packs2[pos] = pack2[...]
    copies = net.start(
        [(pack2, packs2.at[pos], to) for to in plane_ids], packs2.at[0:31]
    )

    wide = jnp.concatenate([g1_own * te_own, jnp.zeros((PAD - 16, PAD), F32)], axis=0)
    wide_high, wide_low = split(jnp.transpose(wide)[0:OWN])
    wide = jnp.concatenate([wide_high, wide_low], axis=0)
    for b in range(0, C, 512):
        f_high, f_low = split(fbuf[:, b : b + 512])
        grad = dot(wide, f_high)
        gw_ref[0:OWN, b : b + 512] = grad[0:OWN] + grad[OWN : 2 * OWN] + dot(wide_high, f_low)
    vec_ref[4:8, :] = fbuf[12:16, :]
    copies.wait()
    for i in range(32):
        tile = packs2[i]
        here = slice(OWN * i, OWN * i + OWN)
        vec_ref[0:1, here] = tile[0:1, 0:OWN]
        vec_ref[1:2, here] = tile[0:1, 64 : 64 + OWN]
        vec_ref[2:3, here] = tile[1:2, 0:OWN]
        vec_ref[3:4, here] = tile[1:2, 64 : 64 + OWN]
    store.wait()


def whole(*args):
    vmem = pl.BlockSpec(memory_space=pltpu.VMEM)
    hbm = pl.BlockSpec(memory_space=pltpu.HBM)
    anywhere = pl.BlockSpec(memory_space=pl.ANY)
    return pl.pallas_call(
        whole_kernel,
        out_shape=(
            jax.ShapeDtypeStruct((L, C), BF16),
            jax.ShapeDtypeStruct((2 * OWN, C), F32),
            jax.ShapeDtypeStruct((8, C), F32),
        ),
        in_specs=[hbm] * 9,
        out_specs=(anywhere, vmem, vmem),
        scratch_shapes=[
            pltpu.VMEM((1, L), jnp.int32),
            pltpu.VMEM((4, C), BF16),
            pltpu.VMEM((3, C), F32),
            pltpu.VMEM((C,), F32),
            pltpu.VMEM((3, C), F32),
            pltpu.VMEM((C,), F32),
            pltpu.VMEM((PAD, C), BF16),
            pltpu.VMEM((PAD, C), BF16),
            pltpu.VMEM((L, C), BF16),
            pltpu.VMEM((8, L), jnp.int32),
            pltpu.VMEM((3, 8, L), jnp.int32),
            pltpu.VMEM((32, 8, PAD), F32),
            pltpu.VMEM((32, 8, PAD), F32),
            pltpu.VMEM((8, PAD), F32),
            pltpu.VMEM((32, 8, PAD), F32),
            pltpu.VMEM((16, C), F32),
            pltpu.VMEM((ROWS, PAD), F32),
            pltpu.VMEM((128, 384), F32),
            pltpu.VMEM((128, 384), BF16),
            pltpu.VMEM((3, 32, 384), BF16),
            pltpu.VMEM((8, 32, 384), BF16),
            pltpu.VMEM((ROWS, C), BF16),
            pltpu.VMEM((PAD, C), BF16),
            pltpu.VMEM((8, PAD), F32),
            pltpu.VMEM((PAD, C), F32),
            pltpu.VMEM((2 * L, ROWS), BF16),
            pltpu.VMEM((ROWS, 2 * L), BF16),
            pltpu.VMEM((384, PAD), BF16),
            pltpu.VMEM((384, PAD), BF16),
            pltpu.VMEM((PAD, 2 * L), BF16),
            pltpu.VMEM((2 * L, C), BF16),
            pltpu.VMEM((2 * L, C), BF16),
            pltpu.VMEM((2 * L, C), BF16),
            pltpu.VMEM((2 * L, BLOCK), F32),
            pltpu.VMEM((2 * L, BLOCK), BF16),
            pltpu.VMEM((2 * L, 128), F32),
            pltpu.VMEM((2 * L, 128), F32),
            pltpu.VMEM((L, C), BF16),
            pltpu.VMEM((ROWS, WIDE), F32),
            pltpu.VMEM((128, WIDE), BF16),
            pltpu.VMEM((128, WIDE), BF16),
            pltpu.VMEM((128, WIDE), BF16),
            pltpu.VMEM((2, 15, 32, 256), BF16),
            pltpu.VMEM((2, 8, 32, 256), BF16),
            pltpu.VMEM((ROWS, WIDE), BF16),
            pltpu.VMEM((8, PAD), F32),
            pltpu.VMEM((32, 8, PAD), F32),
            pltpu.VMEM((PAD, C), F32),
            pltpu.VMEM((2, PAD), F32),
            pltpu.VMEM((32, 2, PAD), F32),
            pltpu.SemaphoreType.DMA((10,)),
            pltpu.SemaphoreType.DMA((2, 3)),
            pltpu.SemaphoreType.DMA((24,)),
            pltpu.SemaphoreType.DMA((24,)),
        ],
        compiler_params=pltpu.CompilerParams(
            collective_id=0, has_side_effects=True, vmem_limit_bytes=62 * 2**20
        ),
        name="whole",
    )(*args)


def place_kernel(out_in, gw_in, vec_ref, out_ref, gwa_ref, gwb_ref, ta_ref, tb_ref, ga_ref, gb_ref):
    out_ref[...] = out_in[...]
    gwa_ref[...] = gw_in[0:OWN]
    gwb_ref[...] = gw_in[OWN : 2 * OWN]
    ta_ref[...] = vec_ref[0:3]
    tb_ref[...] = vec_ref[4:7]
    ga_ref[...] = vec_ref[3]
    gb_ref[...] = vec_ref[7]


def placed_outputs(out, gw, vec):
    vmem = pl.BlockSpec(memory_space=pltpu.VMEM)
    return pl.pallas_call(
        place_kernel,
        out_shape=(
            jax.ShapeDtypeStruct((L, C), BF16),
            jax.ShapeDtypeStruct((OWN, C), F32),
            jax.ShapeDtypeStruct((OWN, C), F32),
            jax.ShapeDtypeStruct((3, C), F32),
            jax.ShapeDtypeStruct((3, C), F32),
            jax.ShapeDtypeStruct((C,), F32),
            jax.ShapeDtypeStruct((C,), F32),
        ),
        in_specs=[vmem] * 3,
        out_specs=(vmem,) * 7,
        compiler_params=pltpu.CompilerParams(vmem_limit_bytes=62 * 2**20),
        name="place",
    )(out, gw, vec)


def shards(tokens, embed, k1, g1, w1, k2, g2, w2, cotangent):
    out, gw, vec = whole(tokens, embed, k1, g1, w1, k2, g2, w2, cotangent.reshape(L, C))
    out, gwa, gwb, ta, tb, ga, gb = placed_outputs(out, gw, vec)
    return (out[None, None], gwa, gwb, ta, tb, ga, gb)


def solution(mesh):
    placed = (
        P("rep", "pos"),
        P(),
        P(),
        P(),
        P("pos", None),
        P(),
        P(),
        P("pos", None),
        P("rep", "strand", "pos", None),
    )
    return jax.shard_map(
        shards,
        mesh=mesh,
        in_specs=placed,
        out_specs=(
            P("rep", "strand", "pos", None),
            P("pos", None),
            P("pos", None),
            P(),
            P(),
            P(),
            P(),
        ),
        check_vma=False,
    )
```
